128 devices in a mesh: frame: 8 (over x, z_hi), head: 8 (over y, z_lo), rep: 2 (over core).
Axes of the slice: x: 4, y: 4, z: 4 (z_hi: 2, z_lo: 2; z = z_hi * 2 + z_lo), core: 2. Of those that a mesh axis runs over, the one named last changes fastest.
Arguments:
- tokens: bfloat16 [24576, 3072], P(('rep', 'frame', 'head')), parts along dimension 0, may hold values from -6 to 6
- shift: float32 [3072], replicated, may hold values from -3 to 3
- mod_scale: float32 [3072], replicated, may hold values from -3 to 3
- gate: float32 [3072], replicated, may hold values from -4 to 4
- w_qkv: bfloat16 [3072, 24, 384], P(None, 'head'), may hold values from -0.109375 to 0.109375
- q_gain: float32 [128], replicated, may hold values from 0.1 to 1.9
- k_gain: float32 [128], replicated, may hold values from 0.1 to 1.9
- w_out: bfloat16 [3072, 3072], P('head'), may hold values from -0.109375 to 0.109375
- pattern: int32 [3, 4, 4], replicated, may hold values from 0 to 1, as said below
- counts: int32 [8], replicated, may hold values from 64 to 384, as said below
Outputs:
- mixed: bfloat16 [24576, 3072], P(('rep', 'frame', 'head')), parts along dimension 0
The draws below stay inside these ranges and needn't reach their ends.
There are 2 independent parts, one for each index of `rep`. The reference program is written for one: setup_inputs(seed, part) draws one part's arguments, and reference() takes and returns one part's arrays. A program takes and returns all parts, laid end to end along the dimension named above; an argument that names none is the same for every part. Nothing has to cross between parts.
Inputs may be any that keep to these rules, and one draw needn't show every extreme that they name: Every entry of pattern is 0 or 1; pattern[1, i, i] = 1 for every spatial tile i. counts[t] = 8 * 8 * min(max(V - t * 6, 1), 6) for a number V of valid frames with (6) * 6 + 2 <= V <= 42; tiles past the valid frames keep one frame; non-increasing, the first tile full, the last one holding exactly one frame.
All inputs are finite; a program needn't handle non-finite values.
Results may differ from the reference program's by a relative error of at most 0.011.
Values may be sent and summed in bfloat16 or wider, within the bound.
A program may use at most 192 MiB of HBM per device.

```python
import jax
import jax.numpy as jnp
from jax import lax

D = 3072
HEADS = 24
HD = 128
TF = 6
TH = 8
TW = 8
TILE = 384
GS = 4
NT = 8
TOKENS = 12288


def draw_pattern(key, part):
    key = jax.random.fold_in(key, 11)
    random_bits = jax.random.randint(key, (3, GS, GS), 0, 2)
    identity = (jnp.arange(GS)[:, None] == jnp.arange(GS)[None, :]).astype(jnp.int32)
    middle = jnp.maximum(random_bits[1], identity)
    return jnp.stack([random_bits[0], middle, random_bits[2]]).astype(jnp.int32)


def draw_counts(key, part):
    key = jax.random.fold_in(key, 23)
    offset = jax.random.randint(key, (), 1, TF)
    valid = (NT - 1) * TF + 1 - offset
    filled = jnp.clip(valid - jnp.arange(NT) * TF, 1, TF)
    return (filled * (TH * TW)).astype(jnp.int32)


def levels(key, shape, split, low, top_value):
    level, own = 1.0, jax.random.fold_in(key, 6)
    for axis_at, shards_of in split:
        steps = jnp.exp(jax.random.uniform(jax.random.fold_in(own, axis_at), (shards_of,), jnp.float32, low / len(split), top_value / len(split)))
        level = level * jnp.repeat(steps, shape[axis_at] // shards_of).reshape([-1 if axis == axis_at else 1 for axis in range(len(shape))])
    return level


def bell_draw(stream_key, extent, scale, reach, cuts=(), kind=jnp.bfloat16):
    level = levels(stream_key, extent, cuts, -0.22, 0.18) if cuts else 1.0
    values = jax.random.normal(stream_key, extent, jnp.float32) * scale * level
    return jnp.minimum(jnp.maximum(values, -reach), reach).astype(kind)


def setup_inputs(seed: int = 0, part: int = 0) -> dict:
    key_of = jax.random.split(jax.random.key(seed), 11)
    part_splits = jax.random.split(jax.random.fold_in(key_of[10], part), 11)
    tokens = bell_draw(part_splits[0], (TOKENS, D), 1.0, 6.0, ((0, 64),))
    shift = bell_draw(key_of[1], (D,), 0.5, 3.0, (), jnp.float32)
    mod_scale = bell_draw(key_of[2], (D,), 0.5, 3.0, (), jnp.float32)
    gate = bell_draw(key_of[3], (D,), 1.0, 4.0, (), jnp.float32)
    w_qkv = bell_draw(key_of[4], (D, HEADS, 3 * HD), D ** -0.5, 0.109375, ((1, 8),))
    q_gain = jnp.clip(1.0 + 0.18 * jax.random.normal(key_of[5], (HD,), jnp.float32), 0.1, 1.9)
    k_gain = jnp.clip(1.0 + 0.18 * jax.random.normal(key_of[6], (HD,), jnp.float32), 0.1, 1.9)
    w_out = bell_draw(key_of[7], (HEADS * HD, D), (HEADS * HD) ** -0.5, 0.109375, ((0, 8),))
    pattern = draw_pattern(jax.random.fold_in(key_of[10], 71), part)
    counts = draw_counts(jax.random.fold_in(key_of[10], 71), part)
    return dict(tokens=tokens, shift=shift, mod_scale=mod_scale, gate=gate, w_qkv=w_qkv, q_gain=q_gain, k_gain=k_gain, w_out=w_out, pattern=pattern, counts=counts)


def modulate(rows, shift, mod_scale):
    values = rows.astype(jnp.float32)
    center = lax.optimization_barrier(jnp.mean(values, axis=-1, keepdims=True))
    centred = values - center
    spread = lax.optimization_barrier(jnp.mean(centred * centred, axis=-1, keepdims=True))
    return (centred * lax.rsqrt(spread + 1e-06) * (1.0 + mod_scale) + shift).astype(jnp.bfloat16)

def head_norm(values, gain):
    square = lax.optimization_barrier(jnp.mean(values * values, axis=-1, keepdims=True))
    return (values * lax.rsqrt(square + 1e-06) * gain).astype(jnp.bfloat16)

def project(normed, w_qkv, q_gain, k_gain):
    heads = w_qkv.shape[1]
    width = w_qkv.shape[2] // 3
    flat_weight = w_qkv.reshape(w_qkv.shape[0], heads * 3 * width)
    mixing = jnp.dot(normed, flat_weight, preferred_element_type=jnp.float32)
    mixing = mixing.reshape(normed.shape[0], heads, 3, width)
    queries = head_norm(mixing[:, :, 0], q_gain)
    keyset = head_norm(mixing[:, :, 1], k_gain)
    valueset = mixing[:, :, 2].astype(jnp.bfloat16)
    return jnp.stack([queries, keyset, valueset], axis=1)

def tile_attention(query, keyset, valueset, pattern, counts, position):
    spatial = pattern.shape[1]
    rows = query.shape[0]
    tile = rows // spatial
    width = query.shape[1]
    flat_keys = keyset.reshape(3 * rows, width)
    scores = lax.dot_general(query, flat_keys, (((1,), (1,)), ((), ())), preferred_element_type=jnp.float32)
    scores = (scores * width ** (-0.5)).reshape(spatial, tile, 3, spatial, tile)
    targets = position + jnp.arange(3, dtype=jnp.int32) - 1
    inside = (targets >= 0) & (targets < counts.shape[0])
    matches = targets[:, None] == jnp.arange(counts.shape[0], dtype=jnp.int32)[None, :]
    target_counts = lax.optimization_barrier(jnp.sum(jnp.where(matches, counts[None, :], 0), axis=1))
    live = inside[:, None] & (jnp.arange(tile, dtype=jnp.int32)[None, :] < target_counts[:, None])
    allowed = jnp.transpose(pattern, (1, 0, 2)) > 0
    maskset = allowed[:, None, :, :, None] & live[None, None, :, None, :]
    scores = jnp.where(maskset, scores, -jnp.inf)
    highest = lax.optimization_barrier(jnp.max(scores, axis=(2, 3, 4), keepdims=True))
    expo = jnp.exp(scores - highest)
    totals = lax.optimization_barrier(jnp.sum(expo, axis=(2, 3, 4), keepdims=True))
    weights = (expo / totals).astype(jnp.bfloat16).reshape(rows, 3 * rows)
    flat_values = valueset.reshape(3 * rows, width)
    return jnp.dot(weights, flat_values, preferred_element_type=jnp.float32).astype(jnp.bfloat16)

def reference(tokens, shift, mod_scale, gate, w_qkv, q_gain, k_gain, w_out, pattern, counts):
    rows = GS * TILE
    normed = modulate(tokens, shift, mod_scale).reshape(NT, rows, D)

    def project_block(block):
        return project(block, w_qkv, q_gain, k_gain)
    stacked = lax.map(project_block, normed)
    queries = jnp.transpose(stacked[:, :, 0], (2, 0, 1, 3))
    keyvals = jnp.transpose(stacked[:, :, 1:], (3, 0, 2, 1, 4))
    zeroes = jnp.zeros((HEADS, 1, 2, rows, HD), jnp.bfloat16)
    padded = jnp.concatenate([zeroes, keyvals, zeroes], axis=1)

    def one_pair(flat):
        head_index = flat // NT
        position = flat % NT
        query = queries[head_index, position]
        window = lax.dynamic_slice_in_dim(padded[head_index], position, 3, 0)
        return tile_attention(query, window[:, 0], window[:, 1], pattern, counts, position)
    outputs = lax.map(one_pair, jnp.arange(HEADS * NT, dtype=jnp.int32))
    attn = outputs.reshape(HEADS, NT, rows, HD).transpose(1, 2, 0, 3).reshape(NT * rows, HEADS * HD)
    result = jnp.dot(attn, w_out, preferred_element_type=jnp.float32)
    return (tokens.astype(jnp.float32) + gate * result).astype(jnp.bfloat16)
```

```python
import functools

import jax
import jax.numpy as jnp
from jax import lax
from jax.experimental import pallas as pl
from jax.experimental.pallas import tpu as pltpu
from jax.sharding import PartitionSpec as P

TILE = 384
GS = 4
HD = 128
NT = 8
ROWS = GS * TILE
VMEM_LIMIT = 56 * 1024 * 1024
QSCALE = HD**-0.5 * 1.4426950408889634


def modulate(rows, shift, mod_scale):
    values = rows.astype(jnp.float32)
    center = jnp.mean(values, axis=-1, keepdims=True)
    centred = values - center
    spread = jnp.mean(centred * centred, axis=-1, keepdims=True)
    return (centred * lax.rsqrt(spread + 1e-06) * (1.0 + mod_scale) + shift).astype(jnp.bfloat16)


def head_norm(values, gain):
    square = jnp.mean(values * values, axis=-1, keepdims=True)
    return (values * lax.rsqrt(square + 1e-06) * gain).astype(jnp.bfloat16)


def project_kernel(x_ref, w_ref, qg_ref, kg_ref, q_ref, kv_ref):
    x = x_ref[...]
    heads = w_ref.shape[0]
    for h in range(heads):
        mixed = jnp.dot(x, w_ref[h], preferred_element_type=jnp.float32)
        q_ref[:, h * HD : (h + 1) * HD] = head_norm(mixed[:, :HD], qg_ref[...])
        kv_ref[:, h * HD : (h + 1) * HD] = head_norm(mixed[:, HD : 2 * HD], kg_ref[...])
        kv_ref[:, (heads + h) * HD : (heads + h + 1) * HD] = mixed[:, 2 * HD :].astype(jnp.bfloat16)


def project(normed, w, q_gain, k_gain):
    heads, depth, width = w.shape
    rows = normed.shape[0]
    step = 192
    return pl.pallas_call(
        project_kernel,
        name="project",
        grid=(rows // step,),
        out_shape=(
            jax.ShapeDtypeStruct((rows, heads * HD), jnp.bfloat16),
            jax.ShapeDtypeStruct((rows, 2 * heads * HD), jnp.bfloat16),
        ),
        in_specs=[
            pl.BlockSpec((step, depth), lambda i: (i, 0)),
            pl.BlockSpec((heads, depth, width), lambda i: (0, 0, 0), pipeline_mode=pl.Buffered(1)),
            pl.BlockSpec((1, HD), lambda i: (0, 0)),
            pl.BlockSpec((1, HD), lambda i: (0, 0)),
        ],
        out_specs=(
            pl.BlockSpec((step, heads * HD), lambda i: (i, 0)),
            pl.BlockSpec((step, 2 * heads * HD), lambda i: (i, 0)),
        ),
        compiler_params=pltpu.CompilerParams(vmem_limit_bytes=VMEM_LIMIT),
    )(normed, w, (q_gain * QSCALE)[None], k_gain[None])


def attention_kernel(heads, pat_ref, cnt_ref, t_ref, q_ref, a_ref, b_ref, c_ref, out_ref, kwin, vwin, vext, acc, todo, sem):
    t = t_ref[0]
    width = heads * HD
    windows = (a_ref, b_ref, c_ref)
    copies = []
    for o in range(3):
        for part, into in ((0, kwin), (1, vwin)):
            copy = pltpu.make_async_copy(
                windows[o].at[:, part * width : (part + 1) * width], into.at[o], sem.at[2 * o + part]
            )
            copy.start()
            copies.append(copy)

    def list_tile(i, carry):
        count = jnp.int32(0)
        for o in range(3):
            inside = (t + o - 1 >= 0) & (t + o - 1 < NT)
            for j in range(GS):
                todo[i * 13 + 1 + count] = o * GS + j
                live = inside & (pat_ref[(o * GS + i) * GS + j] > 0)
                count = count + live.astype(jnp.int32)
        todo[i * 13] = count
        return carry

    lax.fori_loop(0, GS, list_tile, 0)
    for copy in copies:
        copy.wait()

    place = lax.broadcasted_iota(jnp.int32, (TILE, HD), 0)
    for o in range(3):
        valid = cnt_ref[jnp.clip(t + o - 1, 0, NT - 1)]
        keep = place < valid
        ones = jnp.where(keep, 1.0, 0.0).astype(jnp.bfloat16)

        def fill(j, carry):
            rows = pl.ds(pl.multiple_of(j * TILE, TILE), TILE)
            for h in range(heads):
                vext[o, rows, 2 * h * HD : (2 * h + 1) * HD] = (
                    vwin[o, rows, h * HD : (h + 1) * HD] * ones
                )
                vext[o, rows, (2 * h + 1) * HD : (2 * h + 2) * HD] = ones
            return carry

        lax.fori_loop(0, GS, fill, 0)

    def tile(i, carry):
        mine = pl.ds(pl.multiple_of(i * TILE, TILE), TILE)
        acc[...] = jnp.zeros_like(acc)

        def pair(n, carry):
            which = todo[i * 13 + 1 + n]
            o = which // GS
            keys = pl.ds(pl.multiple_of((which % GS) * TILE, TILE), TILE)
            for h in range(heads):
                score = lax.dot_general(
                    q_ref[mine, h * HD : (h + 1) * HD],
                    kwin[o, keys, h * HD : (h + 1) * HD],
                    (((1,), (1,)), ((), ())),
                    preferred_element_type=jnp.float32,
                )
                prob = jnp.exp2(score).astype(jnp.bfloat16)
                acc[h] += jnp.dot(
                    prob, vext[o, keys, 2 * h * HD : (2 * h + 2) * HD], preferred_element_type=jnp.float32
                )
            return carry

        lax.fori_loop(0, todo[i * 13], pair, 0)
        for h in range(heads):
            out_ref[mine, h * HD : (h + 1) * HD] = (acc[h, :, :HD] / acc[h, :, HD:]).astype(jnp.bfloat16)
        return carry

    lax.fori_loop(0, GS, tile, 0)


def attention(q, before, own, after, pattern, counts, t):
    rows, width = q.shape
    heads = width // HD
    smem = pl.BlockSpec(memory_space=pltpu.SMEM)
    hbm = pl.BlockSpec(memory_space=pl.ANY)
    vmem = pl.BlockSpec(memory_space=pltpu.VMEM)
    return pl.pallas_call(
        functools.partial(attention_kernel, heads),
        name="attention",
        out_shape=jax.ShapeDtypeStruct((rows, width), jnp.bfloat16),
        in_specs=[smem, smem, smem, vmem, hbm, hbm, hbm],
        out_specs=vmem,
        scratch_shapes=[
            pltpu.VMEM((3, rows, width), jnp.bfloat16),
            pltpu.VMEM((3, rows, width), jnp.bfloat16),
            pltpu.VMEM((3, rows, 2 * width), jnp.bfloat16),
            pltpu.VMEM((heads, TILE, 2 * HD), jnp.float32),
            pltpu.SMEM((GS * 13 + 4,), jnp.int32),
            pltpu.SemaphoreType.DMA((6,)),
        ],
        compiler_params=pltpu.CompilerParams(vmem_limit_bytes=VMEM_LIMIT),
    )(pattern.reshape(-1), counts, t.reshape(1), q, before, own, after)


def per_device(tokens, shift, mod_scale, gate, w_qkv, q_gain, k_gain, w_out, pattern, counts):
    normed = modulate(tokens, shift, mod_scale)
    gathered = lax.all_gather(normed, "head", axis=0, tiled=True)
    q, kv = project(gathered, jnp.transpose(w_qkv, (1, 0, 2)), q_gain, k_gain)
    size = lax.axis_size("frame")
    up = [(i, (i + 1) % size) for i in range(size - 1)]
    down = [(j, i) for i, j in up]
    before = lax.ppermute(kv, "frame", up)
    after = lax.ppermute(kv, "frame", down)
    attn = attention(q, before, kv, after, pattern, counts, lax.axis_index("frame"))
    result = lax.psum_scatter(
        jnp.dot(attn, w_out, preferred_element_type=jnp.float32).astype(jnp.bfloat16),
        "head",
        scatter_dimension=0,
        tiled=True,
    ).astype(jnp.float32)
    return (tokens.astype(jnp.float32) + gate * result).astype(jnp.bfloat16)


def solution(mesh):
    placed = (
        P(("rep", "frame", "head"), None),
        P(),
        P(),
        P(),
        P(None, "head", None),
        P(),
        P(),
        P("head", None),
        P(),
        P(),
    )
    return jax.shard_map(
        per_device,
        mesh=mesh,
        in_specs=placed,
        out_specs=P(("rep", "frame", "head"), None),
        check_vma=False,
    )
```

```python
import functools

import jax
import jax.numpy as jnp
from jax import lax
from jax.experimental import pallas as pl
from jax.experimental.pallas import tpu as pltpu
from jax.sharding import PartitionSpec as P

TILE = 384
GS = 4
HD = 128
NT = 8
ROWS = GS * TILE
VMEM_LIMIT = 56 * 1024 * 1024
QSCALE = HD**-0.5 * 1.4426950408889634


def head_norm(values, gain):
    square = jnp.mean(values * values, axis=-1, keepdims=True)
    return (values * lax.rsqrt(square + 1e-06) * gain).astype(jnp.bfloat16)


MESH = pl.DeviceIdType.MESH
CHUNKS = 4
SWAP, YP_OWN, YM_OWN, Z_OWN, YP_FWD, YM_FWD, YP_PEER, YM_PEER, Z_OPP = range(0, 4 * 9, 4)
MESSAGES = 36
SLICES = 8


def place():
    f, h, c = lax.axis_index("frame"), lax.axis_index("head"), lax.axis_index("rep")
    return f // 2, f % 2, h // 2, h % 2, c


def gather_kernel(heads, tok_ref, scale_ref, shift_ref, w_hbm, qg_ref, kg_ref, q_out, kv_out,
                  xbuf, mine, w, qbuf, kvbuf, send, recv, halo_send, halo_recv, out_sem, w_sem):
    x, zh, y, zl, c = place()
    nx = lax.axis_size("frame") // 2
    rows = mine.shape[0]
    part = rows // CHUNKS
    pos = y * 2 + zl
    flip = (zh + c) % 2
    yp, ym = {"head": (y + 1) % 4 * 2 + zl}, {"head": (y + 3) % 4 * 2 + zl}
    zp = {"head": y * 2 + 1 - zl}
    partner = {"frame": x * 2 + 1 - zh, "head": y * 2 + 1 - zl, "rep": 1 - c}
    sibling = {"rep": 1 - c}
    xn = {"frame": (x + nx + 2 * c - 1) % nx * 2 + zh, "rep": 1 - c}

    barrier = pltpu.get_barrier_semaphore()
    neighbours = (yp, ym, zp, partner, sibling, xn)
    for device in neighbours:
        pl.semaphore_signal(barrier, inc=1, device_id=device, device_id_type=MESH)

    w_copy = pltpu.make_async_copy(w_hbm, w, w_sem)
    w_copy.start()

    def chunk(k):
        return pl.ds(k * part, part)

    for k in range(CHUNKS):
        values = tok_ref[chunk(k), :].astype(jnp.float32)
        center = jnp.mean(values, axis=-1, keepdims=True)
        centred = values - center
        spread = jnp.mean(centred * centred, axis=-1, keepdims=True)
        normed = (centred * lax.rsqrt(spread + 1e-06) * scale_ref[...] + shift_ref[...]).astype(jnp.bfloat16)
        mine[chunk(k), :] = normed

        @pl.when(flip == 0)
        def _():
            xbuf[pos, chunk(k), :] = normed

    pl.semaphore_wait(barrier, len(neighbours))

    def slot_of(dy, dz):
        return (y + dy) % 4 * 2 + (zl + dz) % 2

    def message(number, k, slot, device):
        there = xbuf.at[slot, chunk(k)]
        return pltpu.make_async_remote_copy(
            src_ref=there, dst_ref=there, send_sem=send.at[number + k], recv_sem=recv.at[number + k],
            device_id=device, device_id_type=MESH,
        )

    def swap(k, slot):
        return pltpu.make_async_remote_copy(
            src_ref=mine.at[chunk(k)], dst_ref=xbuf.at[slot, chunk(k)], send_sem=send.at[SWAP + k],
            recv_sem=recv.at[SWAP + k], device_id=partner, device_id_type=MESH,
        )

    @pl.when(flip == 1)
    def _():
        for k in (0, 3, 1, 2):
            swap(k, y * 2 + 1 - zl).start()

    def arrive(number, k, slot):
        message(number, k, slot, zp).wait_recv()

    def own(number, ks, device):
        for k in ks:
            message(number, k, pos, device).start()

    for k, to_yp, to_ym in ((0, (0,), ()), (3, (), (3,)), (1, (1,), ()), (2, (), (2,))):
        @pl.when(flip == 1)
        def _():
            swap(k, pos).wait_recv()

        own(Z_OWN, (k,), zp)
        own(YP_OWN, to_yp, yp)
        own(YM_OWN, to_ym, ym)
    own(YP_OWN, (2, 3), yp)
    own(YM_OWN, (1, 0), ym)

    below, above, across, facing = slot_of(3, 0), slot_of(1, 0), slot_of(0, 1), slot_of(2, 0)

    def peer(k):
        arrive(Z_OWN, k, across)
        message(YP_PEER, k, across, yp).start()
        message(YM_PEER, k, across, ym).start()

    def forward_up(k):
        arrive(YP_OWN, k, below)
        message(YP_FWD, k, below, yp).start()

    def forward_down(k):
        arrive(YM_OWN, k, above)
        message(YM_FWD, k, above, ym).start()

    def opposite(number, k):
        arrive(number, k, facing)
        message(Z_OPP, k, facing, zp).start()

    def second():
        forward_up(0)
        forward_down(3)
        peer(0)
        peer(3)
        forward_up(1)
        forward_down(2)
        peer(1)
        peer(2)
        arrive(YP_OWN, 2, below)
        arrive(YP_OWN, 3, below)

    def third():
        arrive(YM_OWN, 1, above)
        arrive(YM_OWN, 0, above)

    def fifth():
        opposite(YP_FWD, 0)
        opposite(YM_FWD, 3)
        opposite(YP_FWD, 1)
        opposite(YM_FWD, 2)

    def sixth():
        for k in range(CHUNKS):
            arrive(YP_PEER, k, slot_of(3, 1))

    def seventh():
        for k in range(CHUNKS):
            arrive(YM_PEER, k, slot_of(1, 1))

    def eighth():
        for k in range(CHUNKS):
            arrive(Z_OPP, k, slot_of(2, 1))

    order = (
        (0, 0, None), (3, 0, second), (1, 0, third), (0, 1, None),
        (2, 0, fifth), (3, 1, sixth), (1, 1, seventh), (2, 1, eighth),
    )

    def slice_rows(s):
        return pl.ds(pl.multiple_of(s * rows, rows), rows)

    def halo(s, slot, number, device):
        return pltpu.make_async_remote_copy(
            src_ref=kvbuf.at[slice_rows(s)], dst_ref=kv_out.at[slot, slice_rows(s)],
            send_sem=halo_send.at[number + s], recv_sem=halo_recv.at[number + s],
            device_id=device, device_id_type=MESH,
        )

    def out_copies(s):
        return (
            pltpu.make_async_copy(qbuf.at[slice_rows(s)], q_out.at[slice_rows(s)], out_sem.at[s]),
            pltpu.make_async_copy(kvbuf.at[slice_rows(s)], kv_out.at[0, slice_rows(s)], out_sem.at[SLICES + s]),
        )

    def step(n, carry):
        dy, dz = jnp.int32(0), jnp.int32(0)
        for k, (one, two, handler) in enumerate(order):
            dy = jnp.where(n == k, one, dy)
            dz = jnp.where(n == k, two, dz)
            if handler is not None:
                pl.when(n == k)(handler)
        slot = slot_of(dy, dz)
        s = (y + dy) % 4 * 2 + (zl + dz + flip) % 2
        here = slice_rows(s)

        def head(h, carry):
            mixed = jnp.dot(xbuf[slot], w[h], preferred_element_type=jnp.float32)
            cols = pl.ds(pl.multiple_of(h * HD, HD), HD)
            values = pl.ds(pl.multiple_of((heads + h) * HD, HD), HD)
            qbuf[here, cols] = head_norm(mixed[:, :HD], qg_ref[...])
            kvbuf[here, cols] = head_norm(mixed[:, HD : 2 * HD], kg_ref[...])
            kvbuf[here, values] = mixed[:, 2 * HD :].astype(jnp.bfloat16)
            return carry

        lax.fori_loop(0, heads, head, 0)
        halo(s, 2, SLICES, xn).start()
        halo(s, 1, 0, sibling).start()
        for copy in out_copies(s):
            copy.start()
        return carry

    w_copy.wait()
    lax.fori_loop(0, SLICES, step, 0)

    @pl.when(flip == 1)
    def _():
        for k in range(CHUNKS):
            swap(k, y * 2 + 1 - zl).wait_send()

    for number, ks in ((YP_OWN, range(4)), (YM_OWN, range(4)), (Z_OWN, range(4)), (YP_FWD, (0, 1)), (YM_FWD, (2, 3)),
                       (YP_PEER, range(4)), (YM_PEER, range(4)), (Z_OPP, range(4))):
        for k in ks:
            message(number, k, pos, zp).wait_send()

    def finish(s, carry):
        for copy in out_copies(s):
            copy.wait()
        halo(s, 1, 0, sibling).wait()
        halo(s, 2, SLICES, xn).wait()
        return carry

    lax.fori_loop(0, SLICES, finish, 0)


def gather_project(tokens, shift, mod_scale, w, q_gain, k_gain):
    rows, depth = tokens.shape
    heads = w.shape[0]
    width = heads * HD
    vmem = pl.BlockSpec(memory_space=pltpu.VMEM)
    hbm = pl.BlockSpec(memory_space=pl.ANY)
    dma = pltpu.SemaphoreType.DMA
    return pl.pallas_call(
        functools.partial(gather_kernel, heads),
        name="gather_project",
        out_shape=(
            jax.ShapeDtypeStruct((SLICES * rows, width), jnp.bfloat16),
            jax.ShapeDtypeStruct((3, SLICES * rows, 2 * width), jnp.bfloat16),
        ),
        in_specs=[vmem, vmem, vmem, hbm, vmem, vmem],
        out_specs=(hbm, hbm),
        scratch_shapes=[
            pltpu.VMEM((SLICES, rows, depth), jnp.bfloat16),
            pltpu.VMEM((rows, depth), jnp.bfloat16),
            pltpu.VMEM(w.shape, jnp.bfloat16),
            pltpu.VMEM((SLICES * rows, width), jnp.bfloat16),
            pltpu.VMEM((SLICES * rows, 2 * width), jnp.bfloat16),
            dma((MESSAGES,)), dma((MESSAGES,)), dma((2 * SLICES,)), dma((2 * SLICES,)), dma((2 * SLICES,)), dma(()),
        ],
        compiler_params=pltpu.CompilerParams(
            vmem_limit_bytes=VMEM_LIMIT, collective_id=0, has_side_effects=True
        ),
    )(tokens, (1.0 + mod_scale)[None], shift[None], w, (q_gain * QSCALE)[None], k_gain[None])


def attention_kernel(heads, pat_ref, cnt_ref, t_ref, q_ref, kv_ref, out_ref, kwin, vwin, vext, acc, todo, sem):
    t = t_ref[0]
    width = heads * HD
    slots = (2 - t % 2, 0, 1 + t % 2)
    copies = []
    for o in range(3):
        for part, into in ((0, kwin), (1, vwin)):
            copy = pltpu.make_async_copy(
                kv_ref.at[slots[o], :, part * width : (part + 1) * width], into.at[o], sem.at[2 * o + part]
            )
            copy.start()
            copies.append(copy)

    def list_tile(i, carry):
        count = jnp.int32(0)
        for o in range(3):
            inside = (t + o - 1 >= 0) & (t + o - 1 < NT)
            for j in range(GS):
                todo[i * 13 + 1 + count] = o * GS + j
                live = inside & (pat_ref[(o * GS + i) * GS + j] > 0)
                count = count + live.astype(jnp.int32)
        todo[i * 13] = count
        return carry

    lax.fori_loop(0, GS, list_tile, 0)
    for copy in copies:
        copy.wait()

    place = lax.broadcasted_iota(jnp.int32, (TILE, HD), 0)
    for o in range(3):
        valid = cnt_ref[jnp.clip(t + o - 1, 0, NT - 1)]
        keep = place < valid
        ones = jnp.where(keep, 1.0, 0.0).astype(jnp.bfloat16)

        def fill(j, carry):
            rows = pl.ds(pl.multiple_of(j * TILE, TILE), TILE)
            for h in range(heads):
                vext[o, rows, 2 * h * HD : (2 * h + 1) * HD] = (
                    vwin[o, rows, h * HD : (h + 1) * HD] * ones
                )
                vext[o, rows, (2 * h + 1) * HD : (2 * h + 2) * HD] = ones
            return carry

        lax.fori_loop(0, GS, fill, 0)

    def tile(i, carry):
        mine = pl.ds(pl.multiple_of(i * TILE, TILE), TILE)
        acc[...] = jnp.zeros_like(acc)

        def pair(n, carry):
            which = todo[i * 13 + 1 + n]
            o = which // GS
            keys = pl.ds(pl.multiple_of((which % GS) * TILE, TILE), TILE)
            for h in range(heads):
                score = lax.dot_general(
                    q_ref[mine, h * HD : (h + 1) * HD],
                    kwin[o, keys, h * HD : (h + 1) * HD],
                    (((1,), (1,)), ((), ())),
                    preferred_element_type=jnp.float32,
                )
                prob = jnp.exp2(score).astype(jnp.bfloat16)
                acc[h] += jnp.dot(
                    prob, vext[o, keys, 2 * h * HD : (2 * h + 2) * HD], preferred_element_type=jnp.float32
                )
            return carry

        lax.fori_loop(0, todo[i * 13], pair, 0)
        for h in range(heads):
            out_ref[mine, h * HD : (h + 1) * HD] = (acc[h, :, :HD] / acc[h, :, HD:]).astype(jnp.bfloat16)
        return carry

    lax.fori_loop(0, GS, tile, 0)


def attention(q, kv, pattern, counts, t):
    rows, width = q.shape
    heads = width // HD
    smem = pl.BlockSpec(memory_space=pltpu.SMEM)
    hbm = pl.BlockSpec(memory_space=pl.ANY)
    vmem = pl.BlockSpec(memory_space=pltpu.VMEM)
    return pl.pallas_call(
        functools.partial(attention_kernel, heads),
        name="attention",
        out_shape=jax.ShapeDtypeStruct((rows, width), jnp.bfloat16),
        in_specs=[smem, smem, smem, vmem, hbm],
        out_specs=vmem,
        scratch_shapes=[
            pltpu.VMEM((3, rows, width), jnp.bfloat16),
            pltpu.VMEM((3, rows, width), jnp.bfloat16),
            pltpu.VMEM((3, rows, 2 * width), jnp.bfloat16),
            pltpu.VMEM((heads, TILE, 2 * HD), jnp.float32),
            pltpu.SMEM((GS * 13 + 4,), jnp.int32),
            pltpu.SemaphoreType.DMA((6,)),
        ],
        compiler_params=pltpu.CompilerParams(vmem_limit_bytes=VMEM_LIMIT),
    )(pattern.reshape(-1), counts, t.reshape(1), q, kv)


def per_device(tokens, shift, mod_scale, gate, w_qkv, q_gain, k_gain, w_out, pattern, counts):
    q, kv = gather_project(tokens, shift, mod_scale, jnp.transpose(w_qkv, (1, 0, 2)), q_gain, k_gain)
    block = lax.axis_index("frame") // 2 * 2 + lax.axis_index("rep")
    attn = attention(q, kv, pattern, counts, block)
    result = lax.psum_scatter(
        jnp.dot(attn, w_out, preferred_element_type=jnp.float32).astype(jnp.bfloat16),
        "head",
        scatter_dimension=0,
        tiled=True,
    )
    size = lax.axis_size("frame")
    swap = [(f * 2 + c, (f // 2 * 2 + c) * 2 + f % 2) for f in range(size) for c in range(2)]
    result = lax.ppermute(result, ("frame", "rep"), swap).astype(jnp.float32)
    return (tokens.astype(jnp.float32) + gate * result).astype(jnp.bfloat16)


def solution(mesh):
    placed = (
        P(("rep", "frame", "head"), None),
        P(),
        P(),
        P(),
        P(None, "head", None),
        P(),
        P(),
        P("head", None),
        P(),
        P(),
    )
    return jax.shard_map(
        per_device,
        mesh=mesh,
        in_specs=placed,
        out_specs=P(("rep", "frame", "head"), None),
        check_vma=False,
    )
```

```python
import functools

import jax
import jax.numpy as jnp
from jax import lax
from jax.experimental import pallas as pl
from jax.experimental.pallas import tpu as pltpu
from jax.sharding import PartitionSpec as P

TILE = 384
GS = 4
HD = 128
NT = 8
ROWS = GS * TILE
VMEM_LIMIT = 56 * 1024 * 1024
QSCALE = HD**-0.5 * 1.4426950408889634


def head_norm(values, gain):
    square = jnp.mean(values * values, axis=-1, keepdims=True)
    return (values * lax.rsqrt(square + 1e-06) * gain).astype(jnp.bfloat16)


MESH = pl.DeviceIdType.MESH
CHUNKS = 4
SWAP, YP_OWN, YM_OWN, Z_OWN, YP_FWD, YM_FWD, YP_PEER, YM_PEER, Z_OPP = range(0, 4 * 9, 4)
MESSAGES = 36
W_YP, W_YM, W_YP_FWD, W_YM_FWD, W_ZF, W_ZF_ALL, W_XP, W_XM, W_SIB, W_SIB_ALL = 0, 1, 2, 3, 4, 7, 8, 14, 20, 38
W_MESSAGES = 39
SLICES = 8


def place():
    f, h, c = lax.axis_index("frame"), lax.axis_index("head"), lax.axis_index("rep")
    return f // 2, f % 2, h // 2, h % 2, c


def gather_kernel(heads, tok_ref, scale_ref, shift_ref, w_hbm, qg_ref, kg_ref, wo_ref, q_out, kv_out, wall,
                  xbuf, mine, w, qbuf, kvbuf, send, recv, halo_send, halo_recv, out_sem, w_sem, wo_send, wo_recv):
    x, zh, y, zl, c = place()
    nx = lax.axis_size("frame") // 2
    rows = mine.shape[0]
    part = rows // CHUNKS
    pos = y * 2 + zl
    flip = (zh + c) % 2
    yp, ym = {"head": (y + 1) % 4 * 2 + zl}, {"head": (y + 3) % 4 * 2 + zl}
    zp = {"head": y * 2 + 1 - zl}
    partner = {"frame": x * 2 + 1 - zh, "head": y * 2 + 1 - zl, "rep": 1 - c}
    sibling = {"rep": 1 - c}
    xn = {"frame": (x + nx + 2 * c - 1) % nx * 2 + zh, "rep": 1 - c}

    zf = {"frame": x * 2 + 1 - zh, "head": y * 2 + 1 - zl}
    xp, xm = {"frame": (x + 1) % nx * 2 + zh}, {"frame": (x + nx - 1) % nx * 2 + zh}

    barrier = pltpu.get_barrier_semaphore()
    neighbours = (yp, ym, zp, partner, sibling, xn, zf, xp, xm)
    for device in neighbours:
        pl.semaphore_signal(barrier, inc=1, device_id=device, device_id_type=MESH)

    w_copy = pltpu.make_async_copy(w_hbm, w, w_sem)
    w_copy.start()

    def chunk(k):
        return pl.ds(k * part, part)

    for k in range(CHUNKS):
        values = tok_ref[chunk(k), :].astype(jnp.float32)
        center = jnp.mean(values, axis=-1, keepdims=True)
        centred = values - center
        spread = jnp.mean(centred * centred, axis=-1, keepdims=True)
        normed = (centred * lax.rsqrt(spread + 1e-06) * scale_ref[...] + shift_ref[...]).astype(jnp.bfloat16)
        mine[chunk(k), :] = normed

        @pl.when(flip == 0)
        def _():
            xbuf[pos, chunk(k), :] = normed

    pl.semaphore_wait(barrier, len(neighbours))

    def slot_of(dy, dz):
        return (y + dy) % 4 * 2 + (zl + dz) % 2

    def message(number, k, slot, device):
        there = xbuf.at[slot, chunk(k)]
        return pltpu.make_async_remote_copy(
            src_ref=there, dst_ref=there, send_sem=send.at[number + k], recv_sem=recv.at[number + k],
            device_id=device, device_id_type=MESH,
        )

    def swap(k, slot):
        return pltpu.make_async_remote_copy(
            src_ref=mine.at[chunk(k)], dst_ref=xbuf.at[slot, chunk(k)], send_sem=send.at[SWAP + k],
            recv_sem=recv.at[SWAP + k], device_id=partner, device_id_type=MESH,
        )

    @pl.when(flip == 1)
    def _():
        for k in (0, 3, 1, 2):
            swap(k, y * 2 + 1 - zl).start()

    half = wo_ref.shape[-1] // 2

    def piece(number, src, dst, device):
        return pltpu.make_async_remote_copy(
            src_ref=src, dst_ref=dst, send_sem=wo_send.at[number], recv_sem=wo_recv.at[number],
            device_id=device, device_id_type=MESH,
        )

    def held(dy, zl_, k):
        return wall.at[dy, zl_, c, k]

    def w_first(number, dy, device):
        return piece(number, wo_ref.at[c, x], held(dy, zl, x), device)

    def w_forward(number, dy, cols, device):
        return piece(number, held(dy, zl, x).at[:, cols], held(2, zl, x).at[:, cols], device)

    def w_diagonal(dy, zl_):
        return piece(W_ZF + dy - 1, held(dy, zl_, x), held(dy, zl_, x), zf)

    def w_diagonal_all(zl_):
        return piece(W_ZF_ALL, wo_ref.at[c], wall.at[0, zl_, c], zf)

    def w_along(number, dy, z, k, device):
        return piece(number + 2 * (dy - 1) + z, held(dy, (zl + z) % 2, k), held(dy, (zl + z) % 2, k), device)

    def w_sibling(which, dy, z, core):
        there = wall.at[dy, (zl + z) % 2, core, (x + which) % 4]
        return piece(W_SIB + 6 * {0: 0, 1: 1, 3: 2}[which] + 2 * (dy - 1) + z, there, there, sibling)

    def w_sibling_all(core):
        there = wall.at[0, 1 - zl, core]
        return piece(W_SIB_ALL, there, there, sibling)

    def w_spread(dy, z):
        w_along(W_XP, dy, z, x, xp).start()
        w_along(W_XM, dy, z, x, xm).start()
        w_sibling(0, dy, z, c).start()

    low, high = pl.ds(0, half), pl.ds(half, half)
    w_first(W_YP, 3, yp).start()
    w_first(W_YM, 1, ym).start()

    def w_one():
        w_first(W_YP, 3, yp).wait_recv()
        w_forward(W_YP_FWD, 3, low, yp).start()
        w_diagonal(3, zl).start()
        w_spread(3, 0)
        w_first(W_YM, 1, ym).wait_recv()
        w_forward(W_YM_FWD, 1, high, ym).start()
        w_diagonal(1, zl).start()
        w_spread(1, 0)

    def w_two():
        w_forward(W_YP_FWD, 2, low, yp).wait_recv()
        w_forward(W_YM_FWD, 2, high, ym).wait_recv()
        w_diagonal(2, zl).start()
        w_spread(2, 0)
        w_diagonal_all(zl).start()
        for dy in (3, 1):
            w_diagonal(dy, 1 - zl).wait_recv()
            w_spread(dy, 1)

    def w_three():
        w_diagonal(2, 1 - zl).wait_recv()
        w_spread(2, 1)

    def w_four(z):
        for dy in (3, 1, 2):
            w_along(W_XP, dy, z, (x + 3) % 4, xp).wait_recv()
            w_sibling(3, dy, z, c).start()
            w_along(W_XM, dy, z, (x + 1) % 4, xm).wait_recv()
            w_sibling(1, dy, z, c).start()

    def arrive(number, k, slot):
        message(number, k, slot, zp).wait_recv()

    def own(number, ks, device):
        for k in ks:
            message(number, k, pos, device).start()

    for k, to_yp, to_ym in ((0, (0,), ()), (3, (), (3,)), (1, (1,), ()), (2, (), (2,))):
        @pl.when(flip == 1)
        def _():
            swap(k, pos).wait_recv()

        own(Z_OWN, (k,), zp)
        own(YP_OWN, to_yp, yp)
        own(YM_OWN, to_ym, ym)
    own(YP_OWN, (2, 3), yp)
    own(YM_OWN, (1, 0), ym)

    below, above, across, facing = slot_of(3, 0), slot_of(1, 0), slot_of(0, 1), slot_of(2, 0)

    def peer(k):
        arrive(Z_OWN, k, across)
        message(YP_PEER, k, across, yp).start()
        message(YM_PEER, k, across, ym).start()

    def forward_up(k):
        arrive(YP_OWN, k, below)
        message(YP_FWD, k, below, yp).start()

    def forward_down(k):
        arrive(YM_OWN, k, above)
        message(YM_FWD, k, above, ym).start()

    def opposite(number, k):
        arrive(number, k, facing)
        message(Z_OPP, k, facing, zp).start()

    def second():
        w_one()
        forward_up(0)
        forward_down(3)
        peer(0)
        peer(3)
        forward_up(1)
        forward_down(2)
        peer(1)
        peer(2)
        arrive(YP_OWN, 2, below)
        arrive(YP_OWN, 3, below)

    def third():
        w_two()
        arrive(YM_OWN, 1, above)
        arrive(YM_OWN, 0, above)

    def fifth():
        opposite(YP_FWD, 0)
        opposite(YM_FWD, 3)
        opposite(YP_FWD, 1)
        opposite(YM_FWD, 2)
        w_three()

    def sixth():
        for k in range(CHUNKS):
            arrive(YP_PEER, k, slot_of(3, 1))

    def seventh():
        for k in range(CHUNKS):
            arrive(YM_PEER, k, slot_of(1, 1))

    def eighth():
        for k in range(CHUNKS):
            arrive(Z_OPP, k, slot_of(2, 1))

    order = (
        (0, 0, None), (3, 0, second), (1, 0, third), (0, 1, None),
        (2, 0, fifth), (3, 1, sixth), (1, 1, seventh), (2, 1, eighth),
    )

    def slice_rows(s):
        return pl.ds(pl.multiple_of(s * rows, rows), rows)

    def halo(s, slot, number, device):
        return pltpu.make_async_remote_copy(
            src_ref=kvbuf.at[slice_rows(s)], dst_ref=kv_out.at[slot, slice_rows(s)],
            send_sem=halo_send.at[number + s], recv_sem=halo_recv.at[number + s],
            device_id=device, device_id_type=MESH,
        )

    def out_copies(s):
        return (
            pltpu.make_async_copy(qbuf.at[slice_rows(s)], q_out.at[slice_rows(s)], out_sem.at[s]),
            pltpu.make_async_copy(kvbuf.at[slice_rows(s)], kv_out.at[0, slice_rows(s)], out_sem.at[SLICES + s]),
        )

    def step(n, carry):
        dy, dz = jnp.int32(0), jnp.int32(0)
        for k, (one, two, handler) in enumerate(order):
            dy = jnp.where(n == k, one, dy)
            dz = jnp.where(n == k, two, dz)
            if handler is not None:
                pl.when(n == k)(handler)
        slot = slot_of(dy, dz)
        s = (y + dy) % 4 * 2 + (zl + dz + flip) % 2
        here = slice_rows(s)

        def head(h, carry):
            mixed = jnp.dot(xbuf[slot], w[h], preferred_element_type=jnp.float32)
            cols = pl.ds(pl.multiple_of(h * HD, HD), HD)
            values = pl.ds(pl.multiple_of((heads + h) * HD, HD), HD)
            qbuf[here, cols] = head_norm(mixed[:, :HD], qg_ref[...])
            kvbuf[here, cols] = head_norm(mixed[:, HD : 2 * HD], kg_ref[...])
            kvbuf[here, values] = mixed[:, 2 * HD :].astype(jnp.bfloat16)
            return carry

        lax.fori_loop(0, heads, head, 0)
        halo(s, 2, SLICES, xn).start()
        halo(s, 1, 0, sibling).start()
        for copy in out_copies(s):
            copy.start()
        return carry

    w_copy.wait()
    lax.fori_loop(0, SLICES, step, 0)
    w_diagonal_all(1 - zl).wait_recv()
    w_sibling_all(c).start()
    w_four(0)
    w_four(1)

    @pl.when(flip == 1)
    def _():
        for k in range(CHUNKS):
            swap(k, y * 2 + 1 - zl).wait_send()

    for number, ks in ((YP_OWN, range(4)), (YM_OWN, range(4)), (Z_OWN, range(4)), (YP_FWD, (0, 1)), (YM_FWD, (2, 3)),
                       (YP_PEER, range(4)), (YM_PEER, range(4)), (Z_OPP, range(4))):
        for k in ks:
            message(number, k, pos, zp).wait_send()

    def finish(s, carry):
        for copy in out_copies(s):
            copy.wait()
        halo(s, 1, 0, sibling).wait()
        halo(s, 2, SLICES, xn).wait()
        return carry

    lax.fori_loop(0, SLICES, finish, 0)
    w_first(W_YP, 3, yp).wait_send()
    w_first(W_YM, 1, ym).wait_send()
    w_forward(W_YP_FWD, 2, low, yp).wait_send()
    w_forward(W_YM_FWD, 2, high, ym).wait_send()
    w_diagonal_all(zl).wait_send()
    w_sibling_all(1 - c).wait()
    for dy in (1, 2, 3):
        w_diagonal(dy, zl).wait_send()
        for z in (0, 1):
            w_along(W_XP, dy, z, x, xp).wait_send()
            w_along(W_XM, dy, z, x, xm).wait_send()
            for which in (0, 1, 3):
                w_sibling(which, dy, z, 1 - c).wait()


def gather_project(tokens, shift, mod_scale, w, q_gain, k_gain, w_out):
    rows, depth = tokens.shape
    heads = w.shape[0]
    width = heads * HD
    vmem = pl.BlockSpec(memory_space=pltpu.VMEM)
    hbm = pl.BlockSpec(memory_space=pl.ANY)
    dma = pltpu.SemaphoreType.DMA
    return pl.pallas_call(
        functools.partial(gather_kernel, heads),
        name="gather_project",
        out_shape=(
            jax.ShapeDtypeStruct((SLICES * rows, width), jnp.bfloat16),
            jax.ShapeDtypeStruct((3, SLICES * rows, 2 * width), jnp.bfloat16),
            jax.ShapeDtypeStruct((4, 2) + w_out.shape, jnp.bfloat16),
        ),
        in_specs=[vmem, vmem, vmem, hbm, vmem, vmem, hbm],
        out_specs=(hbm, hbm, hbm),
        scratch_shapes=[
            pltpu.VMEM((SLICES, rows, depth), jnp.bfloat16),
            pltpu.VMEM((rows, depth), jnp.bfloat16),
            pltpu.VMEM(w.shape, jnp.bfloat16),
            pltpu.VMEM((SLICES * rows, width), jnp.bfloat16),
            pltpu.VMEM((SLICES * rows, 2 * width), jnp.bfloat16),
            dma((MESSAGES,)), dma((MESSAGES,)), dma((2 * SLICES,)), dma((2 * SLICES,)), dma((2 * SLICES,)), dma(()),
            dma((W_MESSAGES,)), dma((W_MESSAGES,)),
        ],
        compiler_params=pltpu.CompilerParams(
            vmem_limit_bytes=VMEM_LIMIT, collective_id=0, has_side_effects=True
        ),
    )(tokens, (1.0 + mod_scale)[None], shift[None], w, (q_gain * QSCALE)[None], k_gain[None], w_out)


def attention_kernel(heads, pat_ref, cnt_ref, t_ref, q_ref, kv_ref, out_ref, kwin, vwin, vext, acc, todo, sem):
    t = t_ref[0]
    width = heads * HD
    slots = (2 - t % 2, 0, 1 + t % 2)
    copies = []
    for o in range(3):
        for part, into in ((0, kwin), (1, vwin)):
            copy = pltpu.make_async_copy(
                kv_ref.at[slots[o], :, part * width : (part + 1) * width], into.at[o], sem.at[2 * o + part]
            )
            copy.start()
            copies.append(copy)

    def list_tile(i, carry):
        count = jnp.int32(0)
        for o in range(3):
            inside = (t + o - 1 >= 0) & (t + o - 1 < NT)
            for j in range(GS):
                todo[i * 13 + 1 + count] = o * GS + j
                live = inside & (pat_ref[(o * GS + i) * GS + j] > 0)
                count = count + live.astype(jnp.int32)
        todo[i * 13] = count
        return carry

    lax.fori_loop(0, GS, list_tile, 0)
    for copy in copies:
        copy.wait()

    place = lax.broadcasted_iota(jnp.int32, (TILE, HD), 0)
    for o in range(3):
        valid = cnt_ref[jnp.clip(t + o - 1, 0, NT - 1)]
        keep = place < valid
        ones = jnp.where(keep, 1.0, 0.0).astype(jnp.bfloat16)

        def fill(j, carry):
            rows = pl.ds(pl.multiple_of(j * TILE, TILE), TILE)
            for h in range(heads):
                vext[o, rows, 2 * h * HD : (2 * h + 1) * HD] = (
                    vwin[o, rows, h * HD : (h + 1) * HD] * ones
                )
                vext[o, rows, (2 * h + 1) * HD : (2 * h + 2) * HD] = ones
            return carry

        lax.fori_loop(0, GS, fill, 0)

    def tile(i, carry):
        mine = pl.ds(pl.multiple_of(i * TILE, TILE), TILE)
        acc[...] = jnp.zeros_like(acc)

        def pair(n, carry):
            which = todo[i * 13 + 1 + n]
            o = which // GS
            keys = pl.ds(pl.multiple_of((which % GS) * TILE, TILE), TILE)
            for h in range(heads):
                score = lax.dot_general(
                    q_ref[mine, h * HD : (h + 1) * HD],
                    kwin[o, keys, h * HD : (h + 1) * HD],
                    (((1,), (1,)), ((), ())),
                    preferred_element_type=jnp.float32,
                )
                prob = jnp.exp2(score).astype(jnp.bfloat16)
                acc[h] += jnp.dot(
                    prob, vext[o, keys, 2 * h * HD : (2 * h + 2) * HD], preferred_element_type=jnp.float32
                )
            return carry

        lax.fori_loop(0, todo[i * 13], pair, 0)
        for h in range(heads):
            out_ref[mine, h * HD : (h + 1) * HD] = (acc[h, :, :HD] / acc[h, :, HD:]).astype(jnp.bfloat16)
        return carry

    lax.fori_loop(0, GS, tile, 0)


def attention(q, kv, pattern, counts, t):
    rows, width = q.shape
    heads = width // HD
    smem = pl.BlockSpec(memory_space=pltpu.SMEM)
    hbm = pl.BlockSpec(memory_space=pl.ANY)
    vmem = pl.BlockSpec(memory_space=pltpu.VMEM)
    return pl.pallas_call(
        functools.partial(attention_kernel, heads),
        name="attention",
        out_shape=jax.ShapeDtypeStruct((rows, width), jnp.bfloat16),
        in_specs=[smem, smem, smem, vmem, hbm],
        out_specs=vmem,
        scratch_shapes=[
            pltpu.VMEM((3, rows, width), jnp.bfloat16),
            pltpu.VMEM((3, rows, width), jnp.bfloat16),
            pltpu.VMEM((3, rows, 2 * width), jnp.bfloat16),
            pltpu.VMEM((heads, TILE, 2 * HD), jnp.float32),
            pltpu.SMEM((GS * 13 + 4,), jnp.int32),
            pltpu.SemaphoreType.DMA((6,)),
        ],
        compiler_params=pltpu.CompilerParams(vmem_limit_bytes=VMEM_LIMIT),
    )(pattern.reshape(-1), counts, t.reshape(1), q, kv)


def finish_kernel(attn, tok_ref, gate_ref, wo_ref, wall, out_ref, rows_in, wv, acc, a_send, a_recv, x_send, x_recv, s_send, s_recv, w_sem, own_sem):
    x, zh, y, zl, c = place()
    nx = lax.axis_size("frame") // 2
    rows = tok_ref.shape[0]
    depth = tok_ref.shape[1]
    pos = y * 2 + zl
    straight = zh == c
    sibling = {"rep": 1 - c}
    xp, xm = {"frame": (x + 1) % nx * 2 + zh}, {"frame": (x + nx - 1) % nx * 2 + zh}

    def owner(s):
        return {"frame": x * 2 + c, "head": s, "rep": zh}

    def others(s):
        return jnp.logical_or(s != pos, jnp.logical_not(straight))

    barrier = pltpu.get_barrier_semaphore()
    for device in (sibling, xp, xm):
        pl.semaphore_signal(barrier, inc=1, device_id=device, device_id_type=MESH)

    def greet(s, carry):
        @pl.when(others(s))
        def _():
            pl.semaphore_signal(barrier, inc=1, device_id=owner(s), device_id_type=MESH)

        return carry

    lax.fori_loop(0, SLICES, greet, 0)

    def load(dy, k):
        return pltpu.make_async_copy(wall.at[dy, :, :, k], wv.at[dy, :, :, k], w_sem.at[4 * dy + k])

    def loads(act):
        act(pltpu.make_async_copy(wo_ref, wv.at[0, zl], w_sem.at[0]))
        act(pltpu.make_async_copy(wall.at[0, 1 - zl], wv.at[0, 1 - zl], w_sem.at[1]))

    loads(lambda copy: copy.start())
    for dy in (1, 3, 2):
        for which in (0, 1, 3):
            load(dy, (x + which) % 4).start()
    pl.semaphore_wait(barrier, jnp.where(straight, SLICES + 2, SLICES + 3))

    def hand_out(s, source):
        return pltpu.make_async_remote_copy(
            src_ref=attn.at[pl.ds(pl.multiple_of(s * rows, rows), rows)], dst_ref=rows_in.at[source],
            send_sem=a_send.at[s], recv_sem=a_recv.at[source], device_id=owner(s), device_id_type=MESH,
        )

    def keep():
        return pltpu.make_async_copy(
            attn.at[pl.ds(pl.multiple_of(pos * rows, rows), rows)], rows_in.at[pos], own_sem
        )

    def scatter(n, carry):
        s = (pos + n) % SLICES

        @pl.when(others(s))
        def _():
            hand_out(s, pos).start()

        return carry

    lax.fori_loop(0, SLICES, scatter, 0)

    @pl.when(straight)
    def _():
        keep().start()

    def far(number, dy, z, k, device):
        return pltpu.make_async_remote_copy(
            src_ref=wall.at[dy, z, c, k], dst_ref=wv.at[dy, z, c, k], send_sem=x_send.at[number + dy],
            recv_sem=x_recv.at[number + dy], device_id=device, device_id_type=MESH,
        )

    def share(number, dy, z, core):
        there = wv.at[dy, z, core, (x + 2) % 4]
        return pltpu.make_async_remote_copy(
            src_ref=there, dst_ref=there, send_sem=s_send.at[number + dy], recv_sem=s_recv.at[number + dy],
            device_id=sibling, device_id_type=MESH,
        )

    for dy in (1, 3, 2):
        far(0, dy, 0, (x + 3) % 4, xp).start()
        far(4, dy, 1, (x + 1) % 4, xm).start()

    acc[...] = tok_ref[...].astype(jnp.float32)
    cols = min(512, depth)

    def add(dy, z):
        source = (y + dy) % 4 * 2 + (zl + z) % 2
        kept = jnp.logical_and(straight, source == pos)

        @pl.when(kept)
        def _():
            keep().wait()

        @pl.when(jnp.logical_not(kept))
        def _():
            hand_out(0, source).wait_recv()

        def column(n, carry):
            here = pl.ds(pl.multiple_of(n * cols, cols), cols)
            weight = wv[dy, (zl + z) % 2, :, :, :, here].reshape(rows_in.shape[2], cols)
            acc[:, here] += gate_ref[:, here] * jnp.dot(rows_in[source], weight, preferred_element_type=jnp.float32)
            return carry

        lax.fori_loop(0, depth // cols, column, 0)

    loads(lambda copy: copy.wait())
    add(0, 0)
    add(0, 1)
    for dy in (1, 3, 2):
        far(0, dy, 0, (x + 2) % 4, xp).wait_recv()
        share(0, dy, 0, c).start()
        far(4, dy, 1, (x + 2) % 4, xm).wait_recv()
        share(4, dy, 1, c).start()
        for which in (0, 1, 3):
            load(dy, (x + which) % 4).wait()
        share(0, dy, 0, 1 - c).wait_recv()
        share(4, dy, 1, 1 - c).wait_recv()
        add(dy, 0)
        add(dy, 1)
    out_ref[...] = acc[...].astype(jnp.bfloat16)

    def sent(s, carry):
        @pl.when(others(s))
        def _():
            hand_out(s, pos).wait_send()

        return carry

    lax.fori_loop(0, SLICES, sent, 0)
    for dy in (1, 3, 2):
        far(0, dy, 0, (x + 3) % 4, xp).wait_send()
        far(4, dy, 1, (x + 1) % 4, xm).wait_send()
        share(0, dy, 0, c).wait_send()
        share(4, dy, 1, c).wait_send()


def finish(attn, tokens, gate, w_out, wall):
    rows, depth = tokens.shape
    vmem = pl.BlockSpec(memory_space=pltpu.VMEM)
    hbm = pl.BlockSpec(memory_space=pl.ANY)
    dma = pltpu.SemaphoreType.DMA
    return pl.pallas_call(
        finish_kernel,
        name="finish",
        out_shape=jax.ShapeDtypeStruct((rows, depth), jnp.bfloat16),
        in_specs=[hbm, vmem, vmem, hbm, hbm],
        out_specs=vmem,
        scratch_shapes=[
            pltpu.VMEM((SLICES, rows, attn.shape[1]), jnp.bfloat16),
            pltpu.VMEM(wall.shape, jnp.bfloat16),
            pltpu.VMEM((rows, depth), jnp.float32),
            dma((SLICES,)), dma((SLICES,)), dma((8,)), dma((8,)), dma((8,)), dma((8,)), dma((16,)), dma(()),
        ],
        compiler_params=pltpu.CompilerParams(
            vmem_limit_bytes=VMEM_LIMIT, collective_id=1, has_side_effects=True
        ),
    )(attn, tokens, gate[None], w_out, wall)


def per_device(tokens, shift, mod_scale, gate, w_qkv, q_gain, k_gain, w_out, pattern, counts):
    w_parts = w_out.reshape(2, 4, w_out.shape[0] // 8, w_out.shape[1])
    q, kv, wall = gather_project(tokens, shift, mod_scale, jnp.transpose(w_qkv, (1, 0, 2)), q_gain, k_gain, w_parts)
    block = lax.axis_index("frame") // 2 * 2 + lax.axis_index("rep")
    attn = attention(q, kv, pattern, counts, block)
    return finish(attn, tokens, gate, w_parts, wall)


def solution(mesh):
    placed = (
        P(("rep", "frame", "head"), None),
        P(),
        P(),
        P(),
        P(None, "head", None),
        P(),
        P(),
        P("head", None),
        P(),
        P(),
    )
    return jax.shard_map(
        per_device,
        mesh=mesh,
        in_specs=placed,
        out_specs=P(("rep", "frame", "head"), None),
        check_vma=False,
    )
```

```python
import functools

import jax
import jax.numpy as jnp
from jax import lax
from jax.experimental import pallas as pl
from jax.experimental.pallas import tpu as pltpu
from jax.sharding import PartitionSpec as P

TILE = 384
GS = 4
HD = 128
NT = 8
ROWS = GS * TILE
NONE = 3 * GS
VMEM_LIMIT = 56 * 1024 * 1024
QSCALE = HD**-0.5 * 1.4426950408889634


def head_norm(values, gain):
    square = jnp.mean(values * values, axis=-1, keepdims=True)
    return (values * lax.rsqrt(square + 1e-06) * gain).astype(jnp.bfloat16)


MESH = pl.DeviceIdType.MESH
CHUNKS = 4
SWAP, YP_OWN, YM_OWN, Z_OWN, YP_FWD, YM_FWD, YP_PEER, YM_PEER, Z_OPP = range(0, 4 * 9, 4)
Z_BELOW, Z_ABOVE = YP_PEER, YM_PEER
MESSAGES = 36
W_YP, W_YM, W_YP_FWD, W_YM_FWD, W_ZF, W_ZF_ALL, W_XP, W_XM, W_SIB, W_SIB_ALL = 0, 1, 2, 3, 4, 7, 8, 14, 20, 38
W_MESSAGES = 40
SLICES = 8


def place():
    f, h, c = lax.axis_index("frame"), lax.axis_index("head"), lax.axis_index("rep")
    return f // 2, f % 2, h // 2, h % 2, c


def gather_kernel(heads, tok_ref, scale_ref, shift_ref, w_hbm, qg_ref, kg_ref, wo_ref, q_out, kv_out, wall,
                  xbuf, mine, w, qbuf, kvbuf, send, recv, halo_send, halo_recv, out_sem, w_sem, wo_send, wo_recv):
    x, zh, y, zl, c = place()
    nx = lax.axis_size("frame") // 2
    rows = mine.shape[0]
    part = rows // CHUNKS
    pos = y * 2 + zl
    flip = (zh + c) % 2
    yp, ym = {"head": (y + 1) % 4 * 2 + zl}, {"head": (y + 3) % 4 * 2 + zl}
    zp = {"head": y * 2 + 1 - zl}
    partner = {"frame": x * 2 + 1 - zh, "head": y * 2 + 1 - zl, "rep": 1 - c}
    sibling = {"rep": 1 - c}
    xn = {"frame": (x + nx + 2 * c - 1) % nx * 2 + zh, "rep": 1 - c}

    zf = {"frame": x * 2 + 1 - zh, "head": y * 2 + 1 - zl}
    xp, xm = {"frame": (x + 1) % nx * 2 + zh}, {"frame": (x + nx - 1) % nx * 2 + zh}

    barrier = pltpu.get_barrier_semaphore()
    neighbours = (yp, ym, zp, partner, sibling, xn, zf, xp, xm)
    for device in neighbours:
        pl.semaphore_signal(barrier, inc=1, device_id=device, device_id_type=MESH)

    w_copies = [
        pltpu.make_async_copy(w_hbm.at[h], w.at[:, h * 3 * HD : (h + 1) * 3 * HD], w_sem.at[h]) for h in range(heads)
    ]
    for copy in w_copies:
        copy.start()

    def chunk(k):
        return pl.ds(k * part, part)

    scale = 1.0 + scale_ref[...]
    for k in range(CHUNKS):
        values = tok_ref[chunk(k), :].astype(jnp.float32)
        center = jnp.mean(values, axis=-1, keepdims=True)
        centred = values - center
        spread = jnp.mean(centred * centred, axis=-1, keepdims=True)
        normed = (centred * lax.rsqrt(spread + 1e-06) * scale + shift_ref[...]).astype(jnp.bfloat16)
        mine[chunk(k), :] = normed

        @pl.when(flip == 0)
        def _():
            xbuf[pos, chunk(k), :] = normed

    pl.semaphore_wait(barrier, len(neighbours))

    def slot_of(dy, dz):
        return (y + dy) % 4 * 2 + (zl + dz) % 2

    def message(number, k, slot, device):
        there = xbuf.at[slot, chunk(k)]
        return pltpu.make_async_remote_copy(
            src_ref=there, dst_ref=there, send_sem=send.at[number + k], recv_sem=recv.at[number + k],
            device_id=device, device_id_type=MESH,
        )

    def swap(k, slot):
        return pltpu.make_async_remote_copy(
            src_ref=mine.at[chunk(k)], dst_ref=xbuf.at[slot, chunk(k)], send_sem=send.at[SWAP + k],
            recv_sem=recv.at[SWAP + k], device_id=partner, device_id_type=MESH,
        )

    @pl.when(flip == 1)
    def _():
        for k in (0, 3, 1, 2):
            swap(k, y * 2 + 1 - zl).start()

    half = wo_ref.shape[-1] // 2

    def piece(number, src, dst, device):
        return pltpu.make_async_remote_copy(
            src_ref=src, dst_ref=dst, send_sem=wo_send.at[number], recv_sem=wo_recv.at[number],
            device_id=device, device_id_type=MESH,
        )

    def held(dy, zl_, k):
        return wall.at[dy, zl_, c, k]

    def w_first(number, dy, device):
        return piece(number, wo_ref.at[c, x], held(dy, zl, x), device)

    def w_forward(number, dy, cols, device):
        return piece(number, held(dy, zl, x).at[:, cols], held(2, zl, x).at[:, cols], device)

    def w_diagonal(dy, zl_):
        return piece(W_ZF + dy - 1, held(dy, zl_, x), held(dy, zl_, x), zf)

    def w_diagonal_all(zl_, k):
        both = pl.ds(k, 2)
        return piece(W_ZF_ALL + k // 2 * (W_MESSAGES - 1 - W_ZF_ALL), wo_ref.at[c, both], wall.at[0, zl_, c, both], zf)

    def w_along(number, dy, z, k, device):
        return piece(number + 2 * (dy - 1) + z, held(dy, (zl + z) % 2, k), held(dy, (zl + z) % 2, k), device)

    def w_sibling(which, dy, z, core):
        there = wall.at[dy, (zl + z) % 2, core, (x + which) % 4]
        return piece(W_SIB + 6 * {0: 0, 1: 1, 3: 2}[which] + 2 * (dy - 1) + z, there, there, sibling)

    def w_sibling_all(core):
        there = wall.at[0, 1 - zl, core]
        return piece(W_SIB_ALL, there, there, sibling)

    def w_spread(dy, z):
        w_along(W_XP, dy, z, x, xp).start()
        w_along(W_XM, dy, z, x, xm).start()
        w_sibling(0, dy, z, c).start()

    low, high = pl.ds(0, half), pl.ds(half, half)
    w_first(W_YP, 3, yp).start()
    w_first(W_YM, 1, ym).start()

    def w_one():
        w_first(W_YP, 3, yp).wait_recv()
        w_forward(W_YP_FWD, 3, low, yp).start()
        w_diagonal(3, zl).start()
        w_spread(3, 0)
        w_first(W_YM, 1, ym).wait_recv()
        w_forward(W_YM_FWD, 1, high, ym).start()
        w_diagonal(1, zl).start()
        w_spread(1, 0)

    def w_two():
        for dy in (3, 1):
            w_diagonal(dy, 1 - zl).wait_recv()
            w_spread(dy, 1)
        w_diagonal_all(zl, 0).start()

    def w_three():
        w_forward(W_YP_FWD, 2, low, yp).wait_recv()
        w_forward(W_YM_FWD, 2, high, ym).wait_recv()
        w_diagonal(2, zl).start()
        w_spread(2, 0)
        w_diagonal_all(zl, 2).start()

    def w_four():
        w_diagonal(2, 1 - zl).wait_recv()
        w_spread(2, 1)

    def w_five(z):
        for dy in (3, 1, 2):
            w_along(W_XP, dy, z, (x + 3) % 4, xp).wait_recv()
            w_sibling(3, dy, z, c).start()
            w_along(W_XM, dy, z, (x + 1) % 4, xm).wait_recv()
            w_sibling(1, dy, z, c).start()

    def arrive(number, k, slot):
        message(number, k, slot, zp).wait_recv()

    def own(number, ks, device):
        for k in ks:
            message(number, k, pos, device).start()

    for k, to_yp, to_ym in ((0, (0,), ()), (3, (), (3,)), (1, (1,), ()), (2, (), (2,))):
        @pl.when(flip == 1)
        def _():
            swap(k, pos).wait_recv()

        own(Z_OWN, (k,), zp)
        own(YP_OWN, to_yp, yp)
        own(YM_OWN, to_ym, ym)
    own(YP_OWN, (2, 3), yp)
    own(YM_OWN, (1, 0), ym)

    below, above, across, facing = slot_of(3, 0), slot_of(1, 0), slot_of(0, 1), slot_of(2, 0)

    def peer(k):
        arrive(Z_OWN, k, across)
        message(YP_PEER, k, across, yp).start()
        message(YM_PEER, k, across, ym).start()

    def forward_up(k):
        arrive(YP_OWN, k, below)
        message(YP_FWD, k, below, yp).start()

    def forward_down(k):
        arrive(YM_OWN, k, above)
        message(YM_FWD, k, above, ym).start()

    def opposite(number, k):
        arrive(number, k, facing)
        message(Z_OPP, k, facing, zp).start()

    def second():
        w_one()
        forward_up(0)
        forward_down(3)
        message(Z_ABOVE, 3, above, zp).start()
        peer(0)
        w_two()
        arrive(Z_OWN, 3, across)
        forward_up(1)
        forward_down(2)
        peer(1)
        peer(2)
        arrive(YP_OWN, 2, below)
        arrive(YP_OWN, 3, below)
        message(Z_BELOW, 3, below, zp).start()

    def third():
        arrive(YM_OWN, 1, above)
        arrive(YM_OWN, 0, above)

    def fourth():
        w_three()

    def fifth():
        opposite(YP_FWD, 0)
        opposite(YM_FWD, 3)
        opposite(YP_FWD, 1)
        opposite(YM_FWD, 2)

    last = ((3, YP_PEER), (1, YM_PEER), (2, Z_OPP))

    def last_early():
        w_four()
        for dy, number in last:
            arrive(number, 0, slot_of(dy, 1))
            arrive(number, 3, slot_of(dy, 1))

    def last_late():
        for dy, number in last:
            arrive(number, 1, slot_of(dy, 1))
            arrive(number, 2, slot_of(dy, 1))

    order = ((0, 0, None), (3, 0, second), (1, 0, third), (0, 1, fourth), (2, 0, fifth))

    def slice_rows(s):
        return pl.ds(pl.multiple_of(s * rows, rows), rows)

    def halo(s, k, slot, number, device):
        rows_ = slice_rows(s) if k is None else pl.ds(pl.multiple_of(s * rows + k * part, part), part)
        sem = number + CHUNKS * s + (0 if k is None else k)
        return pltpu.make_async_remote_copy(
            src_ref=kvbuf.at[rows_], dst_ref=kv_out.at[slot, rows_], send_sem=halo_send.at[sem],
            recv_sem=halo_recv.at[sem], device_id=device, device_id_type=MESH,
        )

    def halos(s, k):
        return halo(s, k, 2, CHUNKS * SLICES, xn), halo(s, k, 1, 0, sibling)

    def out_copies(s):
        return (
            pltpu.make_async_copy(qbuf.at[slice_rows(s)], q_out.at[slice_rows(s)], out_sem.at[s]),
            pltpu.make_async_copy(kvbuf.at[slice_rows(s)], kv_out.at[0, slice_rows(s)], out_sem.at[SLICES + s]),
        )

    def slice_of(dy, dz, flip_):
        return (y + dy) % 4 * 2 + (zl + dz + flip_) % 2

    q_gain = qg_ref[...] * QSCALE

    def put(mixed, spans):
        for h in range(heads):
            at = h * 3 * HD
            query = head_norm(mixed[:, at : at + HD], q_gain)
            key = head_norm(mixed[:, at + HD : at + 2 * HD], kg_ref[...])
            value = mixed[:, at + 2 * HD : at + 3 * HD].astype(jnp.bfloat16)
            for first, count, here in spans:
                taken = slice(first, first + count)
                qbuf[here, h * HD : (h + 1) * HD] = query[taken]
                kvbuf[here, h * HD : (h + 1) * HD] = key[taken]
                kvbuf[here, (heads + h) * HD : (heads + h + 1) * HD] = value[taken]

    def step(n, carry):
        dy, dz = jnp.int32(0), jnp.int32(0)
        for k, (one, two, handler) in enumerate(order):
            dy = jnp.where(n == k, one, dy)
            dz = jnp.where(n == k, two, dz)
            if handler is not None:
                pl.when(n == k)(handler)
        s = slice_of(dy, dz, flip)
        put(jnp.dot(xbuf[slot_of(dy, dz)], w[...], preferred_element_type=jnp.float32), ((0, rows, slice_rows(s)),))
        for copy in halos(s, None) + out_copies(s):
            copy.start()
        return carry

    for copy in w_copies:
        copy.wait()
    lax.fori_loop(0, len(order), step, 0)

    def last_step(n, carry):
        pl.when(n == 0)(last_early)
        pl.when(n == 1)(last_late)
        chunks = (n, 3 - n)
        taken, spans = [], []
        for dy, _ in last:
            s = slice_of(dy, 1, flip)
            for k in chunks:
                spans.append((len(taken) * part, part, pl.ds(pl.multiple_of(s * rows + k * part, part), part)))
                taken.append(xbuf[slot_of(dy, 1), pl.ds(pl.multiple_of(k * part, part), part), :])
        put(jnp.dot(jnp.concatenate(taken, axis=0), w[...], preferred_element_type=jnp.float32), spans)
        for dy, _ in last:
            s = slice_of(dy, 1, flip)
            for k in chunks:
                for copy in halos(s, k):
                    copy.start()
        return carry

    lax.fori_loop(0, 2, last_step, 0)
    for dy, _ in last:
        for copy in out_copies(slice_of(dy, 1, flip)):
            copy.start()
    w_diagonal_all(1 - zl, 0).wait_recv()
    w_diagonal_all(1 - zl, 2).wait_recv()
    w_sibling_all(c).start()
    w_five(0)
    w_five(1)

    @pl.when(flip == 1)
    def _():
        for k in range(CHUNKS):
            swap(k, y * 2 + 1 - zl).wait_send()

    for number, ks in ((YP_OWN, range(4)), (YM_OWN, range(4)), (Z_OWN, range(4)), (YP_FWD, (0, 1)), (YM_FWD, (2, 3)),
                       (YP_PEER, range(4)), (YM_PEER, range(4)), (Z_OPP, range(4))):
        for k in ks:
            message(number, k, pos, zp).wait_send()

    for dy, dz in [one[:2] for one in order]:
        for copy in out_copies(slice_of(dy, dz, flip)):
            copy.wait()
        for copy in halos(slice_of(dy, dz, flip), None):
            copy.wait_send()
        for copy in halos(slice_of(dy, dz, 1 - flip), None):
            copy.wait_recv()
    for dy, _ in last:
        for copy in out_copies(slice_of(dy, 1, flip)):
            copy.wait()
        for k in range(CHUNKS):
            for copy in halos(slice_of(dy, 1, flip), k):
                copy.wait_send()
            for copy in halos(slice_of(dy, 1, 1 - flip), k):
                copy.wait_recv()
    w_first(W_YP, 3, yp).wait_send()
    w_first(W_YM, 1, ym).wait_send()
    w_forward(W_YP_FWD, 2, low, yp).wait_send()
    w_forward(W_YM_FWD, 2, high, ym).wait_send()
    w_diagonal_all(zl, 0).wait_send()
    w_diagonal_all(zl, 2).wait_send()
    w_sibling_all(1 - c).wait()
    for dy in (1, 2, 3):
        w_diagonal(dy, zl).wait_send()
        for z in (0, 1):
            w_along(W_XP, dy, z, x, xp).wait_send()
            w_along(W_XM, dy, z, x, xm).wait_send()
            for which in (0, 1, 3):
                w_sibling(which, dy, z, 1 - c).wait()


def gather_project(tokens, shift, mod_scale, w, q_gain, k_gain, w_out):
    rows, depth = tokens.shape
    heads = w.shape[0]
    width = heads * HD
    vmem = pl.BlockSpec(memory_space=pltpu.VMEM)
    hbm = pl.BlockSpec(memory_space=pl.ANY)
    dma = pltpu.SemaphoreType.DMA
    return pl.pallas_call(
        functools.partial(gather_kernel, heads),
        name="gather_project",
        out_shape=(
            jax.ShapeDtypeStruct((SLICES * rows, width), jnp.bfloat16),
            jax.ShapeDtypeStruct((3, SLICES * rows, 2 * width), jnp.bfloat16),
            jax.ShapeDtypeStruct((4, 2) + w_out.shape, jnp.bfloat16),
        ),
        in_specs=[vmem, vmem, vmem, hbm, vmem, vmem, hbm],
        out_specs=(hbm, hbm, hbm),
        scratch_shapes=[
            pltpu.VMEM((SLICES, rows, depth), jnp.bfloat16),
            pltpu.VMEM((rows, depth), jnp.bfloat16),
            pltpu.VMEM((depth, 3 * width), jnp.bfloat16),
            pltpu.VMEM((SLICES * rows, width), jnp.bfloat16),
            pltpu.VMEM((SLICES * rows, 2 * width), jnp.bfloat16),
            dma((MESSAGES,)), dma((MESSAGES,)), dma((2 * CHUNKS * SLICES,)), dma((2 * CHUNKS * SLICES,)), dma((2 * SLICES,)), dma((heads,)),
            dma((W_MESSAGES,)), dma((W_MESSAGES,)),
        ],
        compiler_params=pltpu.CompilerParams(
            vmem_limit_bytes=VMEM_LIMIT, collective_id=0, has_side_effects=True
        ),
    )(tokens, mod_scale[None], shift[None], w, q_gain[None], k_gain[None], w_out)


def attention_kernel(heads, pat_ref, cnt_ref, t_ref, q_ref, kv_ref, out_ref, kwin, vwin, vext, acc, todo, sem):
    t = t_ref[0]
    width = heads * HD
    slots = (2 - t % 2, 0, 1 + t % 2)
    copies = []
    for o in range(3):
        for part, into in ((0, kwin), (1, vwin)):
            copy = pltpu.make_async_copy(
                kv_ref.at[slots[o], :, :, part * width : (part + 1) * width],
                into.at[o * GS : (o + 1) * GS],
                sem.at[2 * o + part],
            )
            copy.start()
            copies.append(copy)

    def list_tile(i, carry):
        count = jnp.int32(0)
        for o in range(3):
            inside = (t + o - 1 >= 0) & (t + o - 1 < NT)
            for j in range(GS):
                todo[i * 14 + 1 + count] = o * GS + j
                live = inside & (pat_ref[o, i, j] > 0)
                count = count + live.astype(jnp.int32)
        todo[i * 14 + 1 + count] = NONE
        todo[i * 14] = (count + 1) // 2
        return carry

    lax.fori_loop(0, GS, list_tile, 0)
    for copy in copies:
        copy.wait()

    kwin[NONE] = jnp.zeros_like(kwin[NONE])
    vext[NONE] = jnp.zeros_like(vext[NONE])
    place = lax.broadcasted_iota(jnp.int32, (TILE, HD), 0)
    for o in range(3):
        valid = cnt_ref[jnp.clip(t + o - 1, 0, NT - 1)]
        keep = place < valid
        ones = jnp.where(keep, 1.0, 0.0).astype(jnp.bfloat16)

        def fill(j, carry):
            for h in range(heads):
                vext[o * GS + j, :, 2 * h * HD : (2 * h + 1) * HD] = (
                    vwin[o * GS + j, :, h * HD : (h + 1) * HD] * ones
                )
                vext[o * GS + j, :, (2 * h + 1) * HD : (2 * h + 2) * HD] = ones
            return carry

        lax.fori_loop(0, GS, fill, 0)

    def tile(i, carry):
        mine = pl.ds(pl.multiple_of(i * TILE, TILE), TILE)
        acc[...] = jnp.zeros_like(acc)

        def pair(n, carry):
            both = (todo[i * 14 + 1 + 2 * n], todo[i * 14 + 2 + 2 * n])
            probs = []
            for h in range(heads):
                cols = slice(h * HD, (h + 1) * HD)
                score = lax.dot_general(
                    q_ref[mine, cols],
                    jnp.concatenate([kwin[one, :, cols] for one in both], axis=0),
                    (((1,), (1,)), ((), ())),
                    preferred_element_type=jnp.float32,
                )
                probs.append(jnp.exp2(score).astype(jnp.bfloat16))
            for h in range(heads):
                cols = slice(2 * h * HD, (2 * h + 2) * HD)
                values = jnp.concatenate([vext[one, :, cols] for one in both], axis=0)
                acc[h] += jnp.dot(probs[h], values, preferred_element_type=jnp.float32)
            return carry

        lax.fori_loop(0, todo[i * 14], pair, 0)
        for h in range(heads):
            out_ref[mine, h * HD : (h + 1) * HD] = (acc[h, :, :HD] / acc[h, :, HD:]).astype(jnp.bfloat16)
        return carry

    lax.fori_loop(0, GS, tile, 0)


def attention(q, kv, pattern, counts, t):
    rows, width = q.shape
    heads = width // HD
    smem = pl.BlockSpec(memory_space=pltpu.SMEM)
    hbm = pl.BlockSpec(memory_space=pl.ANY)
    vmem = pl.BlockSpec(memory_space=pltpu.VMEM)
    return pl.pallas_call(
        functools.partial(attention_kernel, heads),
        name="attention",
        out_shape=jax.ShapeDtypeStruct((rows, width), jnp.bfloat16),
        in_specs=[smem, smem, smem, vmem, hbm],
        out_specs=vmem,
        scratch_shapes=[
            pltpu.VMEM((NONE + 1, TILE, width), jnp.bfloat16),
            pltpu.VMEM((NONE, TILE, width), jnp.bfloat16),
            pltpu.VMEM((NONE + 1, TILE, 2 * width), jnp.bfloat16),
            pltpu.VMEM((heads, TILE, 2 * HD), jnp.float32),
            pltpu.SMEM((GS * 14,), jnp.int32),
            pltpu.SemaphoreType.DMA((6,)),
        ],
        compiler_params=pltpu.CompilerParams(vmem_limit_bytes=VMEM_LIMIT),
    )(pattern, counts, t.reshape(1), q, kv.reshape(3, GS, TILE, 2 * width))


def finish_kernel(attn, wo_ref, wall, out_ref, rows_in, wv, a_send, a_recv, x_send, x_recv, s_send, s_recv, w_sem, own_sem):
    x, zh, y, zl, c = place()
    nx = lax.axis_size("frame") // 2
    rows, depth = out_ref.shape
    width = attn.shape[1]
    pos = y * 2 + zl
    straight = zh == c
    sibling = {"rep": 1 - c}
    xp, xm = {"frame": (x + 1) % nx * 2 + zh}, {"frame": (x + nx - 1) % nx * 2 + zh}

    def owner(s):
        return {"frame": x * 2 + c, "head": s, "rep": zh}

    def others(s):
        return jnp.logical_or(s != pos, jnp.logical_not(straight))

    barrier = pltpu.get_barrier_semaphore()
    for device in (sibling, xp, xm):
        pl.semaphore_signal(barrier, inc=1, device_id=device, device_id_type=MESH)

    def greet(s, carry):
        @pl.when(others(s))
        def _():
            pl.semaphore_signal(barrier, inc=1, device_id=owner(s), device_id_type=MESH)

        return carry

    lax.fori_loop(0, SLICES, greet, 0)

    def load(dy, k):
        return pltpu.make_async_copy(wall.at[dy, :, :, k], wv.at[dy, :, :, k], w_sem.at[4 * dy + k])

    def loads(act):
        act(pltpu.make_async_copy(wo_ref, wv.at[0, zl], w_sem.at[0]))
        act(pltpu.make_async_copy(wall.at[0, 1 - zl], wv.at[0, 1 - zl], w_sem.at[1]))

    loads(lambda copy: copy.start())
    for dy in (1, 3, 2):
        for which in (0, 1, 3):
            load(dy, (x + which) % 4).start()
    pl.semaphore_wait(barrier, jnp.where(straight, SLICES + 2, SLICES + 3))

    def landing(source):
        cols = pl.ds(pl.multiple_of(source % 2 * width, width), width)
        return rows_in.at[source // 2, :, cols]

    def hand_out(s, source):
        return pltpu.make_async_remote_copy(
            src_ref=attn.at[pl.ds(pl.multiple_of(s * rows, rows), rows)], dst_ref=landing(source),
            send_sem=a_send.at[s], recv_sem=a_recv.at[source], device_id=owner(s), device_id_type=MESH,
        )

    def keep():
        return pltpu.make_async_copy(
            attn.at[pl.ds(pl.multiple_of(pos * rows, rows), rows)], landing(pos), own_sem
        )

    def scatter(n, carry):
        s = (pos + n) % SLICES

        @pl.when(others(s))
        def _():
            hand_out(s, pos).start()

        return carry

    lax.fori_loop(0, SLICES, scatter, 0)

    @pl.when(straight)
    def _():
        keep().start()

    def far(number, dy, z, k, device):
        return pltpu.make_async_remote_copy(
            src_ref=wall.at[dy, z, c, k], dst_ref=wv.at[dy, z, c, k], send_sem=x_send.at[number + dy],
            recv_sem=x_recv.at[number + dy], device_id=device, device_id_type=MESH,
        )

    def share(number, dy, z, core):
        there = wv.at[dy, z, core, (x + 2) % 4]
        return pltpu.make_async_remote_copy(
            src_ref=there, dst_ref=there, send_sem=s_send.at[number + dy], recv_sem=s_recv.at[number + dy],
            device_id=sibling, device_id_type=MESH,
        )

    for dy in (1, 3, 2):
        far(0, dy, 0, (x + 3) % 4, xp).start()
        far(4, dy, 1, (x + 1) % 4, xm).start()

    cols = min(512, depth)

    def arrived(dy, z):
        source = (y + dy) % 4 * 2 + (zl + z) % 2
        kept = jnp.logical_and(straight, source == pos)

        @pl.when(kept)
        def _():
            keep().wait()

        @pl.when(jnp.logical_not(kept))
        def _():
            hand_out(0, source).wait_recv()

    def add(dy, first):
        arrived(dy, 0)
        arrived(dy, 1)

        def column(n, carry):
            here = pl.ds(pl.multiple_of(n * cols, cols), cols)
            weight = wv[dy, :, :, :, :, here].reshape(2 * width, cols)
            term = jnp.dot(rows_in[(y + dy) % 4], weight, preferred_element_type=jnp.float32)
            out_ref[:, here] = term if first else out_ref[:, here] + term
            return carry

        lax.fori_loop(0, depth // cols, column, 0)

    loads(lambda copy: copy.wait())
    add(0, True)
    for dy in (1, 3, 2):
        far(0, dy, 0, (x + 2) % 4, xp).wait_recv()
        share(0, dy, 0, c).start()
        far(4, dy, 1, (x + 2) % 4, xm).wait_recv()
        share(4, dy, 1, c).start()
        for which in (0, 1, 3):
            load(dy, (x + which) % 4).wait()
        share(0, dy, 0, 1 - c).wait_recv()
        share(4, dy, 1, 1 - c).wait_recv()
        add(dy, False)

    def sent(s, carry):
        @pl.when(others(s))
        def _():
            hand_out(s, pos).wait_send()

        return carry

    lax.fori_loop(0, SLICES, sent, 0)
    for dy in (1, 3, 2):
        far(0, dy, 0, (x + 3) % 4, xp).wait_send()
        far(4, dy, 1, (x + 1) % 4, xm).wait_send()
        share(0, dy, 0, c).wait_send()
        share(4, dy, 1, c).wait_send()


def finish(attn, rows, w_out, wall):
    width = attn.shape[1]
    depth = wall.shape[-1]
    vmem = pl.BlockSpec(memory_space=pltpu.VMEM)
    hbm = pl.BlockSpec(memory_space=pl.ANY)
    dma = pltpu.SemaphoreType.DMA
    return pl.pallas_call(
        finish_kernel,
        name="finish",
        out_shape=jax.ShapeDtypeStruct((rows, depth), jnp.float32),
        in_specs=[hbm, hbm, hbm],
        out_specs=vmem,
        scratch_shapes=[
            pltpu.VMEM((SLICES // 2, rows, 2 * width), jnp.bfloat16),
            pltpu.VMEM(wall.shape, jnp.bfloat16),
            dma((SLICES,)), dma((SLICES,)), dma((8,)), dma((8,)), dma((8,)), dma((8,)), dma((16,)), dma(()),
        ],
        compiler_params=pltpu.CompilerParams(
            vmem_limit_bytes=VMEM_LIMIT, collective_id=1, has_side_effects=True
        ),
    )(attn, w_out, wall)


def per_device(tokens, shift, mod_scale, gate, w_qkv, q_gain, k_gain, w_out, pattern, counts):
    w_parts = w_out.reshape(2, 4, w_out.shape[0] // 8, w_out.shape[1])
    q, kv, wall = gather_project(tokens, shift, mod_scale, jnp.transpose(w_qkv, (1, 0, 2)), q_gain, k_gain, w_parts)
    block = lax.axis_index("frame") // 2 * 2 + lax.axis_index("rep")
    attn = attention(q, kv, pattern, counts, block)
    result = finish(attn, tokens.shape[0], w_parts, wall)
    return (tokens.astype(jnp.float32) + gate * result).astype(jnp.bfloat16)


def solution(mesh):
    placed = (
        P(("rep", "frame", "head"), None),
        P(),
        P(),
        P(),
        P(None, "head", None),
        P(),
        P(),
        P("head", None),
        P(),
        P(),
    )
    return jax.shard_map(
        per_device,
        mesh=mesh,
        in_specs=placed,
        out_specs=P(("rep", "frame", "head"), None),
        check_vma=False,
    )
```

```python
import functools

import jax
import jax.numpy as jnp
from jax import lax
from jax.experimental import pallas as pl
from jax.experimental.pallas import tpu as pltpu
from jax.sharding import PartitionSpec as P

TILE = 384
GS = 4
HD = 128
NT = 8
ROWS = GS * TILE
NONE = 3 * GS
VMEM_LIMIT = 56 * 1024 * 1024
QSCALE = HD**-0.5 * 1.4426950408889634


def head_norm(values, gain):
    square = jnp.mean(values * values, axis=-1, keepdims=True)
    return (values * lax.rsqrt(square + 1e-06) * gain).astype(jnp.bfloat16)


MESH = pl.DeviceIdType.MESH
CHUNKS = 4
SWAP, YP_OWN, YM_OWN, Z_OWN, YP_FWD, YM_FWD, YP_PEER, YM_PEER, Z_OPP = range(0, 4 * 9, 4)
Z_BELOW, Z_ABOVE = YP_PEER, YM_PEER
MESSAGES = 36
W_YP, W_YM, W_YP_FWD, W_YM_FWD, W_ZF, W_ZF_ALL, W_XP, W_XM, W_SIB, W_SIB_ALL = 0, 1, 2, 3, 4, 7, 8, 14, 20, 38
W_MESSAGES = 42
SLICES = 8


def place():
    f, h, c = lax.axis_index("frame"), lax.axis_index("head"), lax.axis_index("rep")
    return f // 2, f % 2, h // 2, h % 2, c


def gather_kernel(heads, tok_ref, scale_ref, shift_ref, w_hbm, qg_ref, kg_ref, wo_ref, q_out, kv_out, wall,
                  xbuf, mine, w, qbuf, kvbuf, send, recv, halo_send, halo_recv, out_sem, w_sem, wo_send, wo_recv):
    x, zh, y, zl, c = place()
    nx = lax.axis_size("frame") // 2
    rows = mine.shape[0]
    part = rows // CHUNKS
    pos = y * 2 + zl
    flip = (zh + c) % 2
    yp, ym = {"head": (y + 1) % 4 * 2 + zl}, {"head": (y + 3) % 4 * 2 + zl}
    zp = {"head": y * 2 + 1 - zl}
    partner = {"frame": x * 2 + 1 - zh, "head": y * 2 + 1 - zl, "rep": 1 - c}
    sibling = {"rep": 1 - c}
    xn = {"frame": (x + nx + 2 * c - 1) % nx * 2 + zh, "rep": 1 - c}

    zf = {"frame": x * 2 + 1 - zh, "head": y * 2 + 1 - zl}
    xp, xm = {"frame": (x + 1) % nx * 2 + zh}, {"frame": (x + nx - 1) % nx * 2 + zh}

    barrier = pltpu.get_barrier_semaphore()
    neighbours = (yp, ym, zp, partner, sibling, xn, zf, xp, xm)
    for device in neighbours:
        pl.semaphore_signal(barrier, inc=1, device_id=device, device_id_type=MESH)

    w_copies = [
        pltpu.make_async_copy(w_hbm.at[h], w.at[:, h * 3 * HD : (h + 1) * 3 * HD], w_sem.at[h]) for h in range(heads)
    ]
    for copy in w_copies:
        copy.start()

    def chunk(k):
        return pl.ds(k * part, part)

    scale = 1.0 + scale_ref[...]

    def normalise(k):
        values = tok_ref[chunk(k), :].astype(jnp.float32)
        center = jnp.mean(values, axis=-1, keepdims=True)
        centred = values - center
        spread = jnp.mean(centred * centred, axis=-1, keepdims=True)
        normed = (centred * lax.rsqrt(spread + 1e-06) * scale + shift_ref[...]).astype(jnp.bfloat16)
        mine[chunk(k), :] = normed

        @pl.when(flip == 0)
        def _():
            xbuf[pos, chunk(k), :] = normed

    def slot_of(dy, dz):
        return (y + dy) % 4 * 2 + (zl + dz) % 2

    def message(number, k, slot, device):
        there = xbuf.at[slot, chunk(k)]
        return pltpu.make_async_remote_copy(
            src_ref=there, dst_ref=there, send_sem=send.at[number + k], recv_sem=recv.at[number + k],
            device_id=device, device_id_type=MESH,
        )

    def swap(k, slot):
        return pltpu.make_async_remote_copy(
            src_ref=mine.at[chunk(k)], dst_ref=xbuf.at[slot, chunk(k)], send_sem=send.at[SWAP + k],
            recv_sem=recv.at[SWAP + k], device_id=partner, device_id_type=MESH,
        )

    half = wo_ref.shape[-1] // 2

    def piece(number, src, dst, device):
        return pltpu.make_async_remote_copy(
            src_ref=src, dst_ref=dst, send_sem=wo_send.at[number], recv_sem=wo_recv.at[number],
            device_id=device, device_id_type=MESH,
        )

    def held(dy, zl_, k):
        return wall.at[dy, zl_, c, k]

    def w_first(number, dy, device):
        return piece(number, wo_ref.at[c, x], held(dy, zl, x), device)

    def w_forward(number, dy, cols, device):
        return piece(number, held(dy, zl, x).at[:, cols], held(2, zl, x).at[:, cols], device)

    def w_diagonal(dy, zl_):
        return piece(W_ZF + dy - 1, held(dy, zl_, x), held(dy, zl_, x), zf)

    def w_diagonal_all(zl_, k):
        both = pl.ds(k, 2)
        return piece(W_ZF_ALL + k // 2 * (W_MESSAGES - 1 - W_ZF_ALL), wo_ref.at[c, both], wall.at[0, zl_, c, both], zf)

    def w_along(number, dy, z, k, device):
        return piece(number + 2 * (dy - 1) + z, held(dy, (zl + z) % 2, k), held(dy, (zl + z) % 2, k), device)

    def w_sibling(which, dy, z, core):
        there = wall.at[dy, (zl + z) % 2, core, (x + which) % 4]
        return piece(W_SIB + 6 * {0: 0, 1: 1, 3: 2}[which] + 2 * (dy - 1) + z, there, there, sibling)

    def w_sibling_all(core, k):
        there = wall.at[0, 1 - zl, core, pl.ds(k, 2)]
        return piece(W_SIB_ALL + k, there, there, sibling)

    def w_half(k):
        w_diagonal_all(1 - zl, k).wait_recv()
        w_sibling_all(c, k).start()

    def w_spread(dy, z):
        w_along(W_XP, dy, z, x, xp).start()
        w_along(W_XM, dy, z, x, xm).start()
        w_sibling(0, dy, z, c).start()

    low, high = pl.ds(0, half), pl.ds(half, half)

    def w_one():
        w_first(W_YP, 3, yp).wait_recv()
        w_forward(W_YP_FWD, 3, low, yp).start()
        w_diagonal(3, zl).start()
        w_spread(3, 0)
        w_first(W_YM, 1, ym).wait_recv()
        w_forward(W_YM_FWD, 1, high, ym).start()
        w_diagonal(1, zl).start()
        w_spread(1, 0)

    def w_two():
        for dy in (3, 1):
            w_diagonal(dy, 1 - zl).wait_recv()
            w_spread(dy, 1)
        w_diagonal_all(zl, 0).start()

    def w_three():
        w_forward(W_YP_FWD, 2, low, yp).wait_recv()
        w_forward(W_YM_FWD, 2, high, ym).wait_recv()
        w_diagonal(2, zl).start()
        w_spread(2, 0)
        w_diagonal_all(zl, 2).start()

    def w_four():
        w_diagonal(2, 1 - zl).wait_recv()
        w_spread(2, 1)

    def w_five(z):
        for dy in (3, 1, 2):
            w_along(W_XP, dy, z, (x + 3) % 4, xp).wait_recv()
            w_sibling(3, dy, z, c).start()
            w_along(W_XM, dy, z, (x + 1) % 4, xm).wait_recv()
            w_sibling(1, dy, z, c).start()

    def arrive(number, k, slot):
        message(number, k, slot, zp).wait_recv()

    def own(number, ks, device):
        for k in ks:
            message(number, k, pos, device).start()

    def own_out(k, to_yp, to_ym):
        own(Z_OWN, (k,), zp)
        own(YP_OWN, to_yp, yp)
        own(YM_OWN, to_ym, ym)

    first_out = ((0, (0,), ()), (3, (), (3,)), (1, (1,), ()), (2, (), (2,)))
    for k, to_yp, to_ym in first_out:
        normalise(k)
        if k == 0:
            pl.semaphore_wait(barrier, len(neighbours))
            w_first(W_YP, 3, yp).start()
            w_first(W_YM, 1, ym).start()

        @pl.when(flip == 1)
        def _():
            swap(k, y * 2 + 1 - zl).start()

        @pl.when(flip == 0)
        def _():
            own_out(k, to_yp, to_ym)

    @pl.when(flip == 1)
    def _():
        for k, to_yp, to_ym in first_out:
            swap(k, pos).wait_recv()
            own_out(k, to_yp, to_ym)

    below, above, across, facing = slot_of(3, 0), slot_of(1, 0), slot_of(0, 1), slot_of(2, 0)

    def peer(k):
        arrive(Z_OWN, k, across)
        if k != 0:
            message(YP_PEER, k, across, yp).start()
        if k != 3:
            message(YM_PEER, k, across, ym).start()

    def forward_up(k):
        arrive(YP_OWN, k, below)
        message(YP_FWD, k, below, yp).start()

    def forward_down(k):
        arrive(YM_OWN, k, above)
        message(YM_FWD, k, above, ym).start()

    def opposite(number, k):
        arrive(number, k, facing)
        message(Z_OPP, k, facing, zp).start()

    def second():
        w_one()
        forward_up(0)
        message(Z_BELOW, 0, below, zp).start()
        forward_down(3)
        message(Z_ABOVE, 3, above, zp).start()
        forward_up(1)
        forward_down(2)
        own(YP_OWN, (2, 3), yp)
        own(YM_OWN, (1, 0), ym)
        peer(0)
        peer(3)
        w_two()
        peer(1)
        opposite(YP_FWD, 0)
        opposite(YM_FWD, 3)
        peer(2)
        w_three()
        opposite(YP_FWD, 1)
        opposite(YM_FWD, 2)
        w_four()

    def fourth():
        arrive(YP_OWN, 2, below)
        arrive(YP_OWN, 3, below)

    def fifth():
        arrive(YM_OWN, 1, above)
        arrive(YM_OWN, 0, above)

    last = ((3, YP_PEER), (1, YM_PEER), (2, Z_OPP))

    def last_chunk(k):
        def handler():
            if k == 0:
                w_half(0)
            for dy, number in last:
                arrive(number, k, slot_of(dy, 1))

        return handler

    order = ((0, 0, None), (0, 1, second), (2, 0, None), (3, 0, fourth), (1, 0, fifth))

    def slice_rows(s):
        return pl.ds(pl.multiple_of(s * rows, rows), rows)

    def halo(s, k, slot, number, device):
        rows_ = slice_rows(s) if k is None else pl.ds(pl.multiple_of(s * rows + k * part, part), part)
        sem = number + CHUNKS * s + (0 if k is None else k)
        return pltpu.make_async_remote_copy(
            src_ref=kvbuf.at[rows_], dst_ref=kv_out.at[slot, rows_], send_sem=halo_send.at[sem],
            recv_sem=halo_recv.at[sem], device_id=device, device_id_type=MESH,
        )

    def halos(s, k):
        return halo(s, k, 2, CHUNKS * SLICES, xn), halo(s, k, 1, 0, sibling)

    def out_copies(s):
        return (
            pltpu.make_async_copy(qbuf.at[slice_rows(s)], q_out.at[slice_rows(s)], out_sem.at[s]),
            pltpu.make_async_copy(kvbuf.at[slice_rows(s)], kv_out.at[0, slice_rows(s)], out_sem.at[SLICES + s]),
        )

    def slice_of(dy, dz, flip_):
        return (y + dy) % 4 * 2 + (zl + dz + flip_) % 2

    q_gain = qg_ref[...] * QSCALE

    def put(mixed, spans):
        for h in range(heads):
            at = h * 3 * HD
            query = head_norm(mixed[:, at : at + HD], q_gain)
            key = head_norm(mixed[:, at + HD : at + 2 * HD], kg_ref[...])
            value = mixed[:, at + 2 * HD : at + 3 * HD].astype(jnp.bfloat16)
            for first, count, here in spans:
                taken = slice(first, first + count)
                qbuf[here, h * HD : (h + 1) * HD] = query[taken]
                kvbuf[here, h * HD : (h + 1) * HD] = key[taken]
                kvbuf[here, (heads + h) * HD : (heads + h + 1) * HD] = value[taken]

    def step(n, carry):
        dy, dz = jnp.int32(0), jnp.int32(0)
        for k, (one, two, handler) in enumerate(order):
            dy = jnp.where(n == k, one, dy)
            dz = jnp.where(n == k, two, dz)
            if handler is not None:
                pl.when(n == k)(handler)
        s = slice_of(dy, dz, flip)
        put(jnp.dot(xbuf[slot_of(dy, dz)], w[...], preferred_element_type=jnp.float32), ((0, rows, slice_rows(s)),))
        for copy in halos(s, None) + out_copies(s):
            copy.start()
        return carry

    for copy in w_copies:
        copy.wait()
    lax.fori_loop(0, len(order), step, 0)

    def last_step(n, carry):
        k = jnp.int32(0)
        for at, one in enumerate((0, 3, 1, 2)):
            k = jnp.where(n == at, one, k)
            pl.when(n == at)(last_chunk(one))
        taken, spans = [], []
        for dy, _ in last:
            s = slice_of(dy, 1, flip)
            spans.append((len(taken) * part, part, pl.ds(pl.multiple_of(s * rows + k * part, part), part)))
            taken.append(xbuf[slot_of(dy, 1), pl.ds(pl.multiple_of(k * part, part), part), :])
        put(jnp.dot(jnp.concatenate(taken, axis=0), w[...], preferred_element_type=jnp.float32), spans)
        for dy, _ in last:
            s = slice_of(dy, 1, flip)
            for copy in halos(s, k):
                copy.start()
        return carry

    lax.fori_loop(0, CHUNKS, last_step, 0)
    for dy, _ in last:
        for copy in out_copies(slice_of(dy, 1, flip)):
            copy.start()
    w_half(2)
    w_five(0)
    w_five(1)

    @pl.when(flip == 1)
    def _():
        for k in range(CHUNKS):
            swap(k, y * 2 + 1 - zl).wait_send()

    for number, ks in ((YP_OWN, range(4)), (YM_OWN, range(4)), (Z_OWN, range(4)), (YP_FWD, (0, 1)), (YM_FWD, (2, 3)),
                       (YP_PEER, range(4)), (YM_PEER, range(4)), (Z_OPP, range(4))):
        for k in ks:
            message(number, k, pos, zp).wait_send()

    for dy, dz in [one[:2] for one in order]:
        for copy in out_copies(slice_of(dy, dz, flip)):
            copy.wait()
        for copy in halos(slice_of(dy, dz, flip), None):
            copy.wait_send()
        for copy in halos(slice_of(dy, dz, 1 - flip), None):
            copy.wait_recv()
    for dy, _ in last:
        for copy in out_copies(slice_of(dy, 1, flip)):
            copy.wait()
        for k in range(CHUNKS):
            for copy in halos(slice_of(dy, 1, flip), k):
                copy.wait_send()
            for copy in halos(slice_of(dy, 1, 1 - flip), k):
                copy.wait_recv()
    w_first(W_YP, 3, yp).wait_send()
    w_first(W_YM, 1, ym).wait_send()
    w_forward(W_YP_FWD, 2, low, yp).wait_send()
    w_forward(W_YM_FWD, 2, high, ym).wait_send()
    w_diagonal_all(zl, 0).wait_send()
    w_diagonal_all(zl, 2).wait_send()
    w_sibling_all(1 - c, 0).wait()
    w_sibling_all(1 - c, 2).wait()
    for dy in (1, 2, 3):
        w_diagonal(dy, zl).wait_send()
        for z in (0, 1):
            w_along(W_XP, dy, z, x, xp).wait_send()
            w_along(W_XM, dy, z, x, xm).wait_send()
            for which in (0, 1, 3):
                w_sibling(which, dy, z, 1 - c).wait()


def gather_project(tokens, shift, mod_scale, w, q_gain, k_gain, w_out):
    rows, depth = tokens.shape
    heads = w.shape[0]
    width = heads * HD
    vmem = pl.BlockSpec(memory_space=pltpu.VMEM)
    hbm = pl.BlockSpec(memory_space=pl.ANY)
    dma = pltpu.SemaphoreType.DMA
    return pl.pallas_call(
        functools.partial(gather_kernel, heads),
        name="gather_project",
        out_shape=(
            jax.ShapeDtypeStruct((SLICES * rows, width), jnp.bfloat16),
            jax.ShapeDtypeStruct((3, SLICES * rows, 2 * width), jnp.bfloat16),
            jax.ShapeDtypeStruct((4, 2) + w_out.shape, jnp.bfloat16),
        ),
        in_specs=[vmem, vmem, vmem, hbm, vmem, vmem, hbm],
        out_specs=(hbm, hbm, hbm),
        scratch_shapes=[
            pltpu.VMEM((SLICES, rows, depth), jnp.bfloat16),
            pltpu.VMEM((rows, depth), jnp.bfloat16),
            pltpu.VMEM((depth, 3 * width), jnp.bfloat16),
            pltpu.VMEM((SLICES * rows, width), jnp.bfloat16),
            pltpu.VMEM((SLICES * rows, 2 * width), jnp.bfloat16),
            dma((MESSAGES,)), dma((MESSAGES,)), dma((2 * CHUNKS * SLICES,)), dma((2 * CHUNKS * SLICES,)), dma((2 * SLICES,)), dma((heads,)),
            dma((W_MESSAGES,)), dma((W_MESSAGES,)),
        ],
        compiler_params=pltpu.CompilerParams(
            vmem_limit_bytes=VMEM_LIMIT, collective_id=0, has_side_effects=True
        ),
    )(tokens, mod_scale[None], shift[None], w, q_gain[None], k_gain[None], w_out)


def attention_kernel(heads, pat_ref, cnt_ref, t_ref, q_ref, kv_ref, out_ref, kwin, vwin, ones, acc, todo, sem):
    t = t_ref[0]
    width = heads * HD
    slots = (2 - t % 2, 0, 1 + t % 2)
    copies = []
    for o in range(3):
        for part, into in ((0, kwin), (1, vwin)):
            copy = pltpu.make_async_copy(
                kv_ref.at[slots[o], :, :, part * width : (part + 1) * width],
                into.at[o * GS : (o + 1) * GS],
                sem.at[2 * o + part],
            )
            copy.start()
            copies.append(copy)

    def list_tile(i, carry):
        count = jnp.int32(0)
        for o in range(3):
            inside = (t + o - 1 >= 0) & (t + o - 1 < NT)
            for j in range(GS):
                todo[i * 14 + 1 + count] = o * GS + j
                live = inside & (pat_ref[o, i, j] > 0)
                count = count + live.astype(jnp.int32)
        todo[i * 14 + 1 + count] = NONE
        todo[i * 14] = (count + 1) // 2
        return carry

    lax.fori_loop(0, GS, list_tile, 0)
    kwin[NONE] = jnp.zeros_like(kwin[NONE])
    vwin[NONE] = jnp.zeros_like(vwin[NONE])
    ones[3] = jnp.zeros_like(ones[3])
    place = lax.broadcasted_iota(jnp.int32, (TILE, HD), 0)
    for o in range(3):
        ones[o] = jnp.where(place < cnt_ref[jnp.clip(t + o - 1, 0, NT - 1)], 1.0, 0.0).astype(jnp.bfloat16)
    for copy in copies:
        copy.wait()

    for o in range(3):
        @pl.when(cnt_ref[jnp.clip(t + o - 1, 0, NT - 1)] < TILE)
        def _():
            def clear(j, carry):
                for h in range(heads):
                    cols = slice(h * HD, (h + 1) * HD)
                    vwin[o * GS + j, :, cols] = vwin[o * GS + j, :, cols] * ones[o]
                return carry

            lax.fori_loop(0, GS, clear, 0)

    def tile(i, carry):
        mine = pl.ds(pl.multiple_of(i * TILE, TILE), TILE)
        acc[...] = jnp.zeros_like(acc)

        def attend(which):
            probs = []
            for h in range(heads):
                cols = slice(h * HD, (h + 1) * HD)
                score = lax.dot_general(
                    q_ref[mine, cols],
                    jnp.concatenate([kwin[one, :, cols] for one in which], axis=0),
                    (((1,), (1,)), ((), ())),
                    preferred_element_type=jnp.float32,
                )
                probs.append(jnp.exp2(score).astype(jnp.bfloat16))
            valid = jnp.concatenate([ones[one // GS] for one in which], axis=0)
            for h in range(heads):
                cols = slice(h * HD, (h + 1) * HD)
                values = jnp.concatenate([vwin[one, :, cols] for one in which], axis=0)
                acc[h] += jnp.dot(
                    probs[h], jnp.concatenate([values, valid], axis=1), preferred_element_type=jnp.float32
                )

        pairs = todo[i * 14]
        first = i * 14 + 1

        def four(n, carry):
            attend([todo[first + 4 * n + m] for m in range(4)])
            return carry

        lax.fori_loop(0, pairs // 2, four, 0)

        @pl.when(pairs % 2 == 1)
        def _():
            attend([todo[first + 2 * (pairs - 1) + m] for m in range(2)])

        for h in range(heads):
            out_ref[mine, h * HD : (h + 1) * HD] = (acc[h, :, :HD] / acc[h, :, HD:]).astype(jnp.bfloat16)
        return carry

    lax.fori_loop(0, GS, tile, 0)


def attention(q, kv, pattern, counts, t):
    rows, width = q.shape
    heads = width // HD
    smem = pl.BlockSpec(memory_space=pltpu.SMEM)
    hbm = pl.BlockSpec(memory_space=pl.ANY)
    vmem = pl.BlockSpec(memory_space=pltpu.VMEM)
    return pl.pallas_call(
        functools.partial(attention_kernel, heads),
        name="attention",
        out_shape=jax.ShapeDtypeStruct((rows, width), jnp.bfloat16),
        in_specs=[smem, smem, smem, vmem, hbm],
        out_specs=vmem,
        scratch_shapes=[
            pltpu.VMEM((NONE + 1, TILE, width), jnp.bfloat16),
            pltpu.VMEM((NONE + 1, TILE, width), jnp.bfloat16),
            pltpu.VMEM((GS, TILE, HD), jnp.bfloat16),
            pltpu.VMEM((heads, TILE, 2 * HD), jnp.float32),
            pltpu.SMEM((GS * 14,), jnp.int32),
            pltpu.SemaphoreType.DMA((6,)),
        ],
        compiler_params=pltpu.CompilerParams(vmem_limit_bytes=VMEM_LIMIT),
    )(pattern, counts, t.reshape(1), q, kv.reshape(3, GS, TILE, 2 * width))


def finish_kernel(attn, wo_ref, wall, out_ref, rows_in, wv, a_send, a_recv, x_send, x_recv, s_send, s_recv, w_sem, own_sem):
    x, zh, y, zl, c = place()
    nx = lax.axis_size("frame") // 2
    rows, depth = out_ref.shape
    width = attn.shape[1]
    pos = y * 2 + zl
    straight = zh == c
    sibling = {"rep": 1 - c}
    xp, xm = {"frame": (x + 1) % nx * 2 + zh}, {"frame": (x + nx - 1) % nx * 2 + zh}

    def owner(s):
        return {"frame": x * 2 + c, "head": s, "rep": zh}

    def others(s):
        return jnp.logical_or(s != pos, jnp.logical_not(straight))

    barrier = pltpu.get_barrier_semaphore()
    for device in (sibling, xp, xm):
        pl.semaphore_signal(barrier, inc=1, device_id=device, device_id_type=MESH)

    def greet(s, carry):
        @pl.when(others(s))
        def _():
            pl.semaphore_signal(barrier, inc=1, device_id=owner(s), device_id_type=MESH)

        return carry

    lax.fori_loop(0, SLICES, greet, 0)

    def load(dy, k):
        return pltpu.make_async_copy(wall.at[dy, :, :, k], wv.at[dy, :, :, k], w_sem.at[4 * dy + k])

    def loads(act):
        act(pltpu.make_async_copy(wo_ref, wv.at[0, zl], w_sem.at[0]))
        act(pltpu.make_async_copy(wall.at[0, 1 - zl], wv.at[0, 1 - zl], w_sem.at[1]))

    loads(lambda copy: copy.start())
    for dy in (1, 3, 2):
        for which in (0, 1, 3):
            load(dy, (x + which) % 4).start()
    pl.semaphore_wait(barrier, jnp.where(straight, SLICES + 2, SLICES + 3))

    def landing(source):
        cols = pl.ds(pl.multiple_of(source % 2 * width, width), width)
        return rows_in.at[source // 2, :, cols]

    def hand_out(s, source):
        return pltpu.make_async_remote_copy(
            src_ref=attn.at[pl.ds(pl.multiple_of(s * rows, rows), rows)], dst_ref=landing(source),
            send_sem=a_send.at[s], recv_sem=a_recv.at[source], device_id=owner(s), device_id_type=MESH,
        )

    def keep():
        return pltpu.make_async_copy(
            attn.at[pl.ds(pl.multiple_of(pos * rows, rows), rows)], landing(pos), own_sem
        )

    def far(number, dy, z, k, device):
        return pltpu.make_async_remote_copy(
            src_ref=wall.at[dy, z, c, k], dst_ref=wv.at[dy, z, c, k], send_sem=x_send.at[number + dy],
            recv_sem=x_recv.at[number + dy], device_id=device, device_id_type=MESH,
        )

    def scatter(n, carry):
        ahead = jnp.where(n < 4, n // 2, 5 - n // 2)
        s = (y + ahead) % 4 * 2 + (zl + n) % 2

        @pl.when(others(s))
        def _():
            hand_out(s, pos).start()

        return carry

    for dy in (1, 3, 2):
        far(0, dy, 0, (x + 3) % 4, xp).start()
        far(4, dy, 1, (x + 1) % 4, xm).start()
    lax.fori_loop(0, SLICES, scatter, 0)

    @pl.when(straight)
    def _():
        keep().start()

    def share(number, dy, z, core):
        there = wv.at[dy, z, core, (x + 2) % 4]
        return pltpu.make_async_remote_copy(
            src_ref=there, dst_ref=there, send_sem=s_send.at[number + dy], recv_sem=s_recv.at[number + dy],
            device_id=sibling, device_id_type=MESH,
        )

    cols = depth

    def arrived(dy, z):
        source = (y + dy) % 4 * 2 + (zl + z) % 2
        kept = jnp.logical_and(straight, source == pos)

        @pl.when(kept)
        def _():
            keep().wait()

        @pl.when(jnp.logical_not(kept))
        def _():
            hand_out(0, source).wait_recv()

    def add(dy, first):
        arrived(dy, 0)
        arrived(dy, 1)

        def column(n, carry):
            here = pl.ds(pl.multiple_of(n * cols, cols), cols)
            weight = wv[dy, :, :, :, :, here].reshape(2 * width, cols)
            term = jnp.dot(rows_in[(y + dy) % 4], weight, preferred_element_type=jnp.float32)
            out_ref[:, here] = term if first else out_ref[:, here] + term
            return carry

        lax.fori_loop(0, depth // cols, column, 0)

    loads(lambda copy: copy.wait())
    add(0, True)
    for dy in (1, 3, 2):
        far(0, dy, 0, (x + 2) % 4, xp).wait_recv()
        share(0, dy, 0, c).start()
        far(4, dy, 1, (x + 2) % 4, xm).wait_recv()
        share(4, dy, 1, c).start()
        for which in (0, 1, 3):
            load(dy, (x + which) % 4).wait()
        share(0, dy, 0, 1 - c).wait_recv()
        share(4, dy, 1, 1 - c).wait_recv()
        add(dy, False)

    def sent(s, carry):
        @pl.when(others(s))
        def _():
            hand_out(s, pos).wait_send()

        return carry

    lax.fori_loop(0, SLICES, sent, 0)
    for dy in (1, 3, 2):
        far(0, dy, 0, (x + 3) % 4, xp).wait_send()
        far(4, dy, 1, (x + 1) % 4, xm).wait_send()
        share(0, dy, 0, c).wait_send()
        share(4, dy, 1, c).wait_send()


def finish(attn, rows, w_out, wall):
    width = attn.shape[1]
    depth = wall.shape[-1]
    vmem = pl.BlockSpec(memory_space=pltpu.VMEM)
    hbm = pl.BlockSpec(memory_space=pl.ANY)
    dma = pltpu.SemaphoreType.DMA
    return pl.pallas_call(
        finish_kernel,
        name="finish",
        out_shape=jax.ShapeDtypeStruct((rows, depth), jnp.float32),
        in_specs=[hbm, hbm, hbm],
        out_specs=vmem,
        scratch_shapes=[
            pltpu.VMEM((SLICES // 2, rows, 2 * width), jnp.bfloat16),
            pltpu.VMEM(wall.shape, jnp.bfloat16),
            dma((SLICES,)), dma((SLICES,)), dma((8,)), dma((8,)), dma((8,)), dma((8,)), dma((16,)), dma(()),
        ],
        compiler_params=pltpu.CompilerParams(
            vmem_limit_bytes=VMEM_LIMIT, collective_id=1, has_side_effects=True
        ),
    )(attn, w_out, wall)


def per_device(tokens, shift, mod_scale, gate, w_qkv, q_gain, k_gain, w_out, pattern, counts):
    w_parts = w_out.reshape(2, 4, w_out.shape[0] // 8, w_out.shape[1])
    q, kv, wall = gather_project(tokens, shift, mod_scale, jnp.transpose(w_qkv, (1, 0, 2)), q_gain, k_gain, w_parts)
    block = lax.axis_index("frame") // 2 * 2 + lax.axis_index("rep")
    attn = attention(q, kv, pattern, counts, block)
    result = finish(attn, tokens.shape[0], w_parts, wall)
    return (tokens.astype(jnp.float32) + gate * result).astype(jnp.bfloat16)


def solution(mesh):
    placed = (
        P(("rep", "frame", "head"), None),
        P(),
        P(),
        P(),
        P(None, "head", None),
        P(),
        P(),
        P("head", None),
        P(),
        P(),
    )
    return jax.shard_map(
        per_device,
        mesh=mesh,
        in_specs=placed,
        out_specs=P(("rep", "frame", "head"), None),
        check_vma=False,
    )
```

```python
import functools

import jax
import jax.numpy as jnp
from jax import lax
from jax.experimental import pallas as pl
from jax.experimental.pallas import tpu as pltpu
from jax.sharding import PartitionSpec as P

TILE = 384
GS = 4
HD = 128
NT = 8
ROWS = GS * TILE
NONE = 3 * GS
MIB = 1024 * 1024
QSCALE = HD**-0.5 * 1.4426950408889634


def head_norm(values, gain):
    square = jnp.mean(values * values, axis=-1, keepdims=True)
    return (values * lax.rsqrt(square + 1e-06) * gain).astype(jnp.bfloat16)


MESH = pl.DeviceIdType.MESH
CHUNKS = 4
SWAP, YP_OWN, YM_OWN, Z_OWN, YP_FWD, YM_FWD, YP_PEER, YM_PEER, Z_OPP = range(0, 4 * 9, 4)
Z_BELOW, Z_ABOVE = YP_PEER, YM_PEER
MESSAGES = 36
W_YP, W_YM, W_YP_FWD, W_YM_FWD, W_ZF, W_ZF_ALL, W_XP, W_XM, W_SIB, W_SIB_ALL = 0, 1, 2, 3, 4, 7, 8, 14, 20, 38
W_MESSAGES = 42
SLICES = 8


def place():
    f, h, c = lax.axis_index("frame"), lax.axis_index("head"), lax.axis_index("rep")
    return f // 2, f % 2, h // 2, h % 2, c


def gather_kernel(heads, tok_hbm, scale_hbm, shift_hbm, w_hbm, qg_hbm, kg_hbm, wo_ref, q_out, kv_out, wall,
                  tok_ref, scale_ref, shift_ref, qg_ref, kg_ref, in_sem, xbuf, mine, w, qbuf, kvbuf, send, recv, halo_send, halo_recv, out_sem, w_sem, wo_send, wo_recv):
    x, zh, y, zl, c = place()
    nx = lax.axis_size("frame") // 2
    rows = mine.shape[0]
    part = rows // CHUNKS
    pos = y * 2 + zl
    flip = (zh + c) % 2
    yp, ym = {"head": (y + 1) % 4 * 2 + zl}, {"head": (y + 3) % 4 * 2 + zl}
    zp = {"head": y * 2 + 1 - zl}
    partner = {"frame": x * 2 + 1 - zh, "head": y * 2 + 1 - zl, "rep": 1 - c}
    sibling = {"rep": 1 - c}
    xn = {"frame": (x + nx + 2 * c - 1) % nx * 2 + zh, "rep": 1 - c}

    zf = {"frame": x * 2 + 1 - zh, "head": y * 2 + 1 - zl}
    xp, xm = {"frame": (x + 1) % nx * 2 + zh}, {"frame": (x + nx - 1) % nx * 2 + zh}

    barrier = pltpu.get_barrier_semaphore()
    neighbours = (yp, ym, zp, partner, sibling, xn, zf, xp, xm)
    for device in neighbours:
        pl.semaphore_signal(barrier, inc=1, device_id=device, device_id_type=MESH)

    in_copies = [
        pltpu.make_async_copy(source, into, in_sem.at[n])
        for n, (source, into) in enumerate((
            (tok_hbm, tok_ref), (scale_hbm, scale_ref), (shift_hbm, shift_ref), (qg_hbm, qg_ref), (kg_hbm, kg_ref),
        ))
    ]
    for copy in in_copies:
        copy.start()
    w_copies = [
        pltpu.make_async_copy(w_hbm.at[h], w.at[:, h * 3 * HD : (h + 1) * 3 * HD], w_sem.at[h]) for h in range(heads)
    ]
    for copy in w_copies:
        copy.start()

    def chunk(k):
        return pl.ds(k * part, part)

    for copy in in_copies:
        copy.wait()
    scale = 1.0 + scale_ref[...]

    def normalise(k):
        values = tok_ref[chunk(k), :].astype(jnp.float32)
        center = jnp.mean(values, axis=-1, keepdims=True)
        centred = values - center
        spread = jnp.mean(centred * centred, axis=-1, keepdims=True)
        normed = (centred * lax.rsqrt(spread + 1e-06) * scale + shift_ref[...]).astype(jnp.bfloat16)
        mine[chunk(k), :] = normed

        @pl.when(flip == 0)
        def _():
            xbuf[pos, chunk(k), :] = normed

    def slot_of(dy, dz):
        return (y + dy) % 4 * 2 + (zl + dz) % 2

    def message(number, k, slot, device):
        there = xbuf.at[slot, chunk(k)]
        return pltpu.make_async_remote_copy(
            src_ref=there, dst_ref=there, send_sem=send.at[number + k], recv_sem=recv.at[number + k],
            device_id=device, device_id_type=MESH,
        )

    def swap(k, slot):
        return pltpu.make_async_remote_copy(
            src_ref=mine.at[chunk(k)], dst_ref=xbuf.at[slot, chunk(k)], send_sem=send.at[SWAP + k],
            recv_sem=recv.at[SWAP + k], device_id=partner, device_id_type=MESH,
        )

    half = wo_ref.shape[-1] // 2

    def piece(number, src, dst, device):
        return pltpu.make_async_remote_copy(
            src_ref=src, dst_ref=dst, send_sem=wo_send.at[number], recv_sem=wo_recv.at[number],
            device_id=device, device_id_type=MESH,
        )

    def held(dy, zl_, k):
        return wall.at[dy, zl_, c, k]

    def w_first(number, dy, device):
        return piece(number, wo_ref.at[c, x], held(dy, zl, x), device)

    def w_forward(number, dy, cols, device):
        return piece(number, held(dy, zl, x).at[:, cols], held(2, zl, x).at[:, cols], device)

    def w_diagonal(dy, zl_):
        return piece(W_ZF + dy - 1, held(dy, zl_, x), held(dy, zl_, x), zf)

    def w_diagonal_all(zl_, k):
        both = pl.ds(k, 2)
        return piece(W_ZF_ALL + k // 2 * (W_MESSAGES - 1 - W_ZF_ALL), wo_ref.at[c, both], wall.at[0, zl_, c, both], zf)

    def w_along(number, dy, z, k, device):
        return piece(number + 2 * (dy - 1) + z, held(dy, (zl + z) % 2, k), held(dy, (zl + z) % 2, k), device)

    def w_sibling(which, dy, z, core):
        there = wall.at[dy, (zl + z) % 2, core, (x + which) % 4]
        return piece(W_SIB + 6 * {0: 0, 1: 1, 3: 2}[which] + 2 * (dy - 1) + z, there, there, sibling)

    def w_sibling_all(core, k):
        there = wall.at[0, 1 - zl, core, pl.ds(k, 2)]
        return piece(W_SIB_ALL + k, there, there, sibling)

    def w_half(k):
        w_diagonal_all(1 - zl, k).wait_recv()
        w_sibling_all(c, k).start()

    def w_spread(dy, z):
        w_along(W_XP, dy, z, x, xp).start()
        w_along(W_XM, dy, z, x, xm).start()
        w_sibling(0, dy, z, c).start()

    low, high = pl.ds(0, half), pl.ds(half, half)

    def w_one():
        w_first(W_YP, 3, yp).wait_recv()
        w_forward(W_YP_FWD, 3, low, yp).start()
        w_diagonal(3, zl).start()
        w_spread(3, 0)
        w_first(W_YM, 1, ym).wait_recv()
        w_forward(W_YM_FWD, 1, high, ym).start()
        w_diagonal(1, zl).start()
        w_spread(1, 0)

    def w_two():
        for dy in (3, 1):
            w_diagonal(dy, 1 - zl).wait_recv()
            w_spread(dy, 1)
        w_diagonal_all(zl, 0).start()

    def w_three():
        w_forward(W_YP_FWD, 2, low, yp).wait_recv()
        w_forward(W_YM_FWD, 2, high, ym).wait_recv()
        w_diagonal(2, zl).start()
        w_spread(2, 0)
        w_diagonal_all(zl, 2).start()

    def w_four():
        w_diagonal(2, 1 - zl).wait_recv()
        w_spread(2, 1)

    def w_five(z):
        for dy in (3, 1, 2):
            w_along(W_XP, dy, z, (x + 3) % 4, xp).wait_recv()
            w_sibling(3, dy, z, c).start()
            w_along(W_XM, dy, z, (x + 1) % 4, xm).wait_recv()
            w_sibling(1, dy, z, c).start()

    def arrive(number, k, slot):
        message(number, k, slot, zp).wait_recv()

    def own(number, ks, device):
        for k in ks:
            message(number, k, pos, device).start()

    def own_out(k, to_yp, to_ym):
        own(Z_OWN, (k,), zp)
        own(YP_OWN, to_yp, yp)
        own(YM_OWN, to_ym, ym)

    first_out = ((0, (0,), ()), (3, (), (3,)), (1, (1,), ()), (2, (), (2,)))
    for k, to_yp, to_ym in first_out:
        normalise(k)
        if k == 0:
            pl.semaphore_wait(barrier, len(neighbours))
            w_first(W_YP, 3, yp).start()
            w_first(W_YM, 1, ym).start()

        @pl.when(flip == 1)
        def _():
            swap(k, y * 2 + 1 - zl).start()

        @pl.when(flip == 0)
        def _():
            own_out(k, to_yp, to_ym)

    @pl.when(flip == 1)
    def _():
        for k, to_yp, to_ym in first_out:
            swap(k, pos).wait_recv()
            own_out(k, to_yp, to_ym)

    below, above, across, facing = slot_of(3, 0), slot_of(1, 0), slot_of(0, 1), slot_of(2, 0)

    def peer(k):
        arrive(Z_OWN, k, across)
        if k != 0:
            message(YP_PEER, k, across, yp).start()
        if k != 3:
            message(YM_PEER, k, across, ym).start()

    def forward_up(k):
        arrive(YP_OWN, k, below)
        message(YP_FWD, k, below, yp).start()

    def forward_down(k):
        arrive(YM_OWN, k, above)
        message(YM_FWD, k, above, ym).start()

    def opposite(number, k):
        arrive(number, k, facing)
        message(Z_OPP, k, facing, zp).start()

    def second():
        w_one()
        forward_up(0)
        message(Z_BELOW, 0, below, zp).start()
        forward_down(3)
        message(Z_ABOVE, 3, above, zp).start()
        forward_up(1)
        forward_down(2)
        own(YP_OWN, (2, 3), yp)
        own(YM_OWN, (1, 0), ym)
        peer(0)
        peer(3)
        w_two()
        peer(1)
        opposite(YP_FWD, 0)
        opposite(YM_FWD, 3)
        peer(2)
        w_three()
        opposite(YP_FWD, 1)
        opposite(YM_FWD, 2)
        w_four()

    def fourth():
        arrive(YP_OWN, 2, below)
        arrive(YP_OWN, 3, below)

    def fifth():
        arrive(YM_OWN, 1, above)
        arrive(YM_OWN, 0, above)

    last = ((3, YP_PEER), (1, YM_PEER), (2, Z_OPP))

    def last_chunk(k):
        def handler():
            if k == 0:
                w_half(0)
            for dy, number in last:
                arrive(number, k, slot_of(dy, 1))

        return handler

    order = ((0, 0, None), (0, 1, second), (2, 0, None), (3, 0, fourth), (1, 0, fifth))

    def slice_rows(s):
        return pl.ds(pl.multiple_of(s * rows, rows), rows)

    def halo(s, k, slot, number, device):
        rows_ = slice_rows(s) if k is None else pl.ds(pl.multiple_of(s * rows + k * part, part), part)
        sem = number + CHUNKS * s + (0 if k is None else k)
        return pltpu.make_async_remote_copy(
            src_ref=kvbuf.at[rows_], dst_ref=kv_out.at[slot, rows_], send_sem=halo_send.at[sem],
            recv_sem=halo_recv.at[sem], device_id=device, device_id_type=MESH,
        )

    def halos(s, k):
        return halo(s, k, 2, CHUNKS * SLICES, xn), halo(s, k, 1, 0, sibling)

    def out_copies(s):
        return (
            pltpu.make_async_copy(qbuf.at[slice_rows(s)], q_out.at[slice_rows(s)], out_sem.at[s]),
            pltpu.make_async_copy(kvbuf.at[slice_rows(s)], kv_out.at[0, slice_rows(s)], out_sem.at[SLICES + s]),
        )

    def slice_of(dy, dz, flip_):
        return (y + dy) % 4 * 2 + (zl + dz + flip_) % 2

    q_gain = qg_ref[...] * QSCALE

    def put(mixed, spans):
        for h in range(heads):
            at = h * 3 * HD
            query = head_norm(mixed[:, at : at + HD], q_gain)
            key = head_norm(mixed[:, at + HD : at + 2 * HD], kg_ref[...])
            value = mixed[:, at + 2 * HD : at + 3 * HD].astype(jnp.bfloat16)
            for first, count, here in spans:
                taken = slice(first, first + count)
                qbuf[here, h * HD : (h + 1) * HD] = query[taken]
                kvbuf[here, h * HD : (h + 1) * HD] = key[taken]
                kvbuf[here, (heads + h) * HD : (heads + h + 1) * HD] = value[taken]

    def step(n, carry):
        dy, dz = jnp.int32(0), jnp.int32(0)
        for k, (one, two, handler) in enumerate(order):
            dy = jnp.where(n == k, one, dy)
            dz = jnp.where(n == k, two, dz)
            if handler is not None:
                pl.when(n == k)(handler)
        s = slice_of(dy, dz, flip)
        put(jnp.dot(xbuf[slot_of(dy, dz)], w[...], preferred_element_type=jnp.float32), ((0, rows, slice_rows(s)),))
        for copy in halos(s, None) + out_copies(s):
            copy.start()
        return carry

    for copy in w_copies:
        copy.wait()
    lax.fori_loop(0, len(order), step, 0)

    def last_step(n, carry):
        k = jnp.int32(0)
        for at, one in enumerate((0, 3, 1, 2)):
            k = jnp.where(n == at, one, k)
            pl.when(n == at)(last_chunk(one))
        taken, spans = [], []
        for dy, _ in last:
            s = slice_of(dy, 1, flip)
            spans.append((len(taken) * part, part, pl.ds(pl.multiple_of(s * rows + k * part, part), part)))
            taken.append(xbuf[slot_of(dy, 1), pl.ds(pl.multiple_of(k * part, part), part), :])
        put(jnp.dot(jnp.concatenate(taken, axis=0), w[...], preferred_element_type=jnp.float32), spans)
        for dy, _ in last:
            s = slice_of(dy, 1, flip)
            for copy in halos(s, k):
                copy.start()
        return carry

    lax.fori_loop(0, CHUNKS, last_step, 0)
    for dy, _ in last:
        for copy in out_copies(slice_of(dy, 1, flip)):
            copy.start()
    w_half(2)
    w_five(0)
    w_five(1)

    @pl.when(flip == 1)
    def _():
        for k in range(CHUNKS):
            swap(k, y * 2 + 1 - zl).wait_send()

    for number, ks in ((YP_OWN, range(4)), (YM_OWN, range(4)), (Z_OWN, range(4)), (YP_FWD, (0, 1)), (YM_FWD, (2, 3)),
                       (YP_PEER, range(4)), (YM_PEER, range(4)), (Z_OPP, range(4))):
        for k in ks:
            message(number, k, pos, zp).wait_send()

    for dy, dz in [one[:2] for one in order]:
        for copy in out_copies(slice_of(dy, dz, flip)):
            copy.wait()
        for copy in halos(slice_of(dy, dz, flip), None):
            copy.wait_send()
        for copy in halos(slice_of(dy, dz, 1 - flip), None):
            copy.wait_recv()
    for dy, _ in last:
        for copy in out_copies(slice_of(dy, 1, flip)):
            copy.wait()
        for k in range(CHUNKS):
            for copy in halos(slice_of(dy, 1, flip), k):
                copy.wait_send()
            for copy in halos(slice_of(dy, 1, 1 - flip), k):
                copy.wait_recv()
    w_first(W_YP, 3, yp).wait_send()
    w_first(W_YM, 1, ym).wait_send()
    w_forward(W_YP_FWD, 2, low, yp).wait_send()
    w_forward(W_YM_FWD, 2, high, ym).wait_send()
    w_diagonal_all(zl, 0).wait_send()
    w_diagonal_all(zl, 2).wait_send()
    w_sibling_all(1 - c, 0).wait()
    w_sibling_all(1 - c, 2).wait()
    for dy in (1, 2, 3):
        w_diagonal(dy, zl).wait_send()
        for z in (0, 1):
            w_along(W_XP, dy, z, x, xp).wait_send()
            w_along(W_XM, dy, z, x, xm).wait_send()
            for which in (0, 1, 3):
                w_sibling(which, dy, z, 1 - c).wait()


def gather_project(tokens, shift, mod_scale, w, q_gain, k_gain, w_out):
    rows, depth = tokens.shape
    heads = w.shape[0]
    width = heads * HD
    hbm = pl.BlockSpec(memory_space=pl.ANY)
    dma = pltpu.SemaphoreType.DMA
    return pl.pallas_call(
        functools.partial(gather_kernel, heads),
        name="gather_project",
        out_shape=(
            jax.ShapeDtypeStruct((SLICES * rows, width), jnp.bfloat16),
            jax.ShapeDtypeStruct((3, SLICES * rows, 2 * width), jnp.bfloat16),
            jax.ShapeDtypeStruct((4, 2) + w_out.shape, jnp.bfloat16),
        ),
        in_specs=[pl.BlockSpec(memory_space=pltpu.HBM)] * 7,
        out_specs=(hbm, hbm, hbm),
        scratch_shapes=[
            pltpu.VMEM((rows, depth), jnp.bfloat16),
            pltpu.VMEM((1, depth), jnp.float32),
            pltpu.VMEM((1, depth), jnp.float32),
            pltpu.VMEM((1, HD), jnp.float32),
            pltpu.VMEM((1, HD), jnp.float32),
            dma((5,)),
            pltpu.VMEM((SLICES, rows, depth), jnp.bfloat16),
            pltpu.VMEM((rows, depth), jnp.bfloat16),
            pltpu.VMEM((depth, 3 * width), jnp.bfloat16),
            pltpu.VMEM((SLICES * rows, width), jnp.bfloat16),
            pltpu.VMEM((SLICES * rows, 2 * width), jnp.bfloat16),
            dma((MESSAGES,)), dma((MESSAGES,)), dma((2 * CHUNKS * SLICES,)), dma((2 * CHUNKS * SLICES,)), dma((2 * SLICES,)), dma((heads,)),
            dma((W_MESSAGES,)), dma((W_MESSAGES,)),
        ],
        compiler_params=pltpu.CompilerParams(
            vmem_limit_bytes=36 * MIB, collective_id=0, has_side_effects=True
        ),
    )(*(pltpu.with_memory_space_constraint(one, pltpu.HBM) for one in
        (tokens, mod_scale[None], shift[None], w, q_gain[None], k_gain[None], w_out)))


def attention_kernel(heads, pat_ref, cnt_ref, t_ref, q_ref, kv_ref, out_ref, kwin, vwin, ones, acc, todo, sem):
    t = t_ref[0]
    width = heads * HD
    slots = (2 - t % 2, 0, 1 + t % 2)
    copies = []
    for o in range(3):
        for part, into in ((0, kwin), (1, vwin)):
            copy = pltpu.make_async_copy(
                kv_ref.at[slots[o], :, :, part * width : (part + 1) * width],
                into.at[o * GS : (o + 1) * GS],
                sem.at[2 * o + part],
            )
            copy.start()
            copies.append(copy)

    def list_tile(i, carry):
        count = jnp.int32(0)
        for o in range(3):
            inside = (t + o - 1 >= 0) & (t + o - 1 < NT)
            for j in range(GS):
                todo[i * 14 + 1 + count] = o * GS + j
                live = inside & (pat_ref[o, i, j] > 0)
                count = count + live.astype(jnp.int32)
        todo[i * 14 + 1 + count] = NONE
        todo[i * 14] = (count + 1) // 2
        return carry

    lax.fori_loop(0, GS, list_tile, 0)
    kwin[NONE] = jnp.zeros_like(kwin[NONE])
    vwin[NONE] = jnp.zeros_like(vwin[NONE])
    ones[3] = jnp.zeros_like(ones[3])
    place = lax.broadcasted_iota(jnp.int32, (TILE, HD), 0)
    for o in range(3):
        ones[o] = jnp.where(place < cnt_ref[jnp.clip(t + o - 1, 0, NT - 1)], 1.0, 0.0).astype(jnp.bfloat16)
    for copy in copies:
        copy.wait()

    for o in range(3):
        @pl.when(cnt_ref[jnp.clip(t + o - 1, 0, NT - 1)] < TILE)
        def _():
            def clear(j, carry):
                for h in range(heads):
                    cols = slice(h * HD, (h + 1) * HD)
                    vwin[o * GS + j, :, cols] = vwin[o * GS + j, :, cols] * ones[o]
                return carry

            lax.fori_loop(0, GS, clear, 0)

    def tile(i, carry):
        mine = pl.ds(pl.multiple_of(i * TILE, TILE), TILE)
        acc[...] = jnp.zeros_like(acc)

        def attend(which):
            probs = []
            for h in range(heads):
                cols = slice(h * HD, (h + 1) * HD)
                score = lax.dot_general(
                    q_ref[mine, cols],
                    jnp.concatenate([kwin[one, :, cols] for one in which], axis=0),
                    (((1,), (1,)), ((), ())),
                    preferred_element_type=jnp.float32,
                )
                probs.append(jnp.exp2(score).astype(jnp.bfloat16))
            valid = jnp.concatenate([ones[one // GS] for one in which], axis=0)
            for h in range(heads):
                cols = slice(h * HD, (h + 1) * HD)
                values = jnp.concatenate([vwin[one, :, cols] for one in which], axis=0)
                acc[h] += jnp.dot(
                    probs[h], jnp.concatenate([values, valid], axis=1), preferred_element_type=jnp.float32
                )

        pairs = todo[i * 14]
        first = i * 14 + 1

        def four(n, carry):
            attend([todo[first + 4 * n + m] for m in range(4)])
            return carry

        lax.fori_loop(0, pairs // 2, four, 0)

        @pl.when(pairs % 2 == 1)
        def _():
            attend([todo[first + 2 * (pairs - 1) + m] for m in range(2)])

        for h in range(heads):
            out_ref[mine, h * HD : (h + 1) * HD] = (acc[h, :, :HD] / acc[h, :, HD:]).astype(jnp.bfloat16)
        return carry

    lax.fori_loop(0, GS, tile, 0)


def attention(q, kv, pattern, counts, t):
    rows, width = q.shape
    heads = width // HD
    smem = pl.BlockSpec(memory_space=pltpu.SMEM)
    hbm = pl.BlockSpec(memory_space=pl.ANY)
    vmem = pl.BlockSpec(memory_space=pltpu.VMEM)
    return pl.pallas_call(
        functools.partial(attention_kernel, heads),
        name="attention",
        out_shape=jax.ShapeDtypeStruct((rows, width), jnp.bfloat16),
        in_specs=[smem, smem, smem, vmem, hbm],
        out_specs=vmem,
        scratch_shapes=[
            pltpu.VMEM((NONE + 1, TILE, width), jnp.bfloat16),
            pltpu.VMEM((NONE + 1, TILE, width), jnp.bfloat16),
            pltpu.VMEM((GS, TILE, HD), jnp.bfloat16),
            pltpu.VMEM((heads, TILE, 2 * HD), jnp.float32),
            pltpu.SMEM((GS * 14,), jnp.int32),
            pltpu.SemaphoreType.DMA((6,)),
        ],
        compiler_params=pltpu.CompilerParams(vmem_limit_bytes=32 * MIB),
    )(pattern, counts, t.reshape(1), q, kv.reshape(3, GS, TILE, 2 * width))


def finish_kernel(attn, wo_ref, wall, out_ref, rows_in, wv, a_send, a_recv, x_send, x_recv, s_send, s_recv, w_sem, own_sem):
    x, zh, y, zl, c = place()
    nx = lax.axis_size("frame") // 2
    rows, depth = out_ref.shape
    width = attn.shape[1]
    pos = y * 2 + zl
    straight = zh == c
    sibling = {"rep": 1 - c}
    xp, xm = {"frame": (x + 1) % nx * 2 + zh}, {"frame": (x + nx - 1) % nx * 2 + zh}

    def owner(s):
        return {"frame": x * 2 + c, "head": s, "rep": zh}

    def others(s):
        return jnp.logical_or(s != pos, jnp.logical_not(straight))

    barrier = pltpu.get_barrier_semaphore()
    for device in (sibling, xp, xm):
        pl.semaphore_signal(barrier, inc=1, device_id=device, device_id_type=MESH)

    def greet(s, carry):
        @pl.when(others(s))
        def _():
            pl.semaphore_signal(barrier, inc=1, device_id=owner(s), device_id_type=MESH)

        return carry

    lax.fori_loop(0, SLICES, greet, 0)

    def load(dy, k):
        return pltpu.make_async_copy(wall.at[dy, :, :, k], wv.at[dy, :, :, k], w_sem.at[4 * dy + k])

    def loads(act):
        act(pltpu.make_async_copy(wo_ref, wv.at[0, zl], w_sem.at[0]))
        act(pltpu.make_async_copy(wall.at[0, 1 - zl], wv.at[0, 1 - zl], w_sem.at[1]))

    loads(lambda copy: copy.start())
    for dy in (1, 3, 2):
        for which in (0, 1, 3):
            load(dy, (x + which) % 4).start()
    pl.semaphore_wait(barrier, jnp.where(straight, SLICES + 2, SLICES + 3))

    def landing(source):
        cols = pl.ds(pl.multiple_of(source % 2 * width, width), width)
        return rows_in.at[source // 2, :, cols]

    def hand_out(s, source):
        return pltpu.make_async_remote_copy(
            src_ref=attn.at[pl.ds(pl.multiple_of(s * rows, rows), rows)], dst_ref=landing(source),
            send_sem=a_send.at[s], recv_sem=a_recv.at[source], device_id=owner(s), device_id_type=MESH,
        )

    def keep():
        return pltpu.make_async_copy(
            attn.at[pl.ds(pl.multiple_of(pos * rows, rows), rows)], landing(pos), own_sem
        )

    def far(number, dy, z, k, device):
        return pltpu.make_async_remote_copy(
            src_ref=wall.at[dy, z, c, k], dst_ref=wv.at[dy, z, c, k], send_sem=x_send.at[number + dy],
            recv_sem=x_recv.at[number + dy], device_id=device, device_id_type=MESH,
        )

    def scatter(n, carry):
        ahead = jnp.where(n < 4, n // 2, 5 - n // 2)
        s = (y + ahead) % 4 * 2 + (zl + n) % 2

        @pl.when(others(s))
        def _():
            hand_out(s, pos).start()

        return carry

    for dy in (1, 3, 2):
        far(0, dy, 0, (x + 3) % 4, xp).start()
        far(4, dy, 1, (x + 1) % 4, xm).start()
    lax.fori_loop(0, SLICES, scatter, 0)

    @pl.when(straight)
    def _():
        keep().start()

    def share(number, dy, z, core):
        there = wv.at[dy, z, core, (x + 2) % 4]
        return pltpu.make_async_remote_copy(
            src_ref=there, dst_ref=there, send_sem=s_send.at[number + dy], recv_sem=s_recv.at[number + dy],
            device_id=sibling, device_id_type=MESH,
        )

    cols = depth

    def arrived(dy, z):
        source = (y + dy) % 4 * 2 + (zl + z) % 2
        kept = jnp.logical_and(straight, source == pos)

        @pl.when(kept)
        def _():
            keep().wait()

        @pl.when(jnp.logical_not(kept))
        def _():
            hand_out(0, source).wait_recv()

    def add(dy, first):
        arrived(dy, 0)
        arrived(dy, 1)

        def column(n, carry):
            here = pl.ds(pl.multiple_of(n * cols, cols), cols)
            weight = wv[dy, :, :, :, :, here].reshape(2 * width, cols)
            term = jnp.dot(rows_in[(y + dy) % 4], weight, preferred_element_type=jnp.float32)
            out_ref[:, here] = term if first else out_ref[:, here] + term
            return carry

        lax.fori_loop(0, depth // cols, column, 0)

    loads(lambda copy: copy.wait())
    add(0, True)
    for dy in (1, 3, 2):
        far(0, dy, 0, (x + 2) % 4, xp).wait_recv()
        share(0, dy, 0, c).start()
        far(4, dy, 1, (x + 2) % 4, xm).wait_recv()
        share(4, dy, 1, c).start()
        for which in (0, 1, 3):
            load(dy, (x + which) % 4).wait()
        share(0, dy, 0, 1 - c).wait_recv()
        share(4, dy, 1, 1 - c).wait_recv()
        add(dy, False)

    def sent(s, carry):
        @pl.when(others(s))
        def _():
            hand_out(s, pos).wait_send()

        return carry

    lax.fori_loop(0, SLICES, sent, 0)
    for dy in (1, 3, 2):
        far(0, dy, 0, (x + 3) % 4, xp).wait_send()
        far(4, dy, 1, (x + 1) % 4, xm).wait_send()
        share(0, dy, 0, c).wait_send()
        share(4, dy, 1, c).wait_send()


def finish(attn, rows, w_out, wall):
    width = attn.shape[1]
    depth = wall.shape[-1]
    vmem = pl.BlockSpec(memory_space=pltpu.VMEM)
    hbm = pl.BlockSpec(memory_space=pl.ANY)
    dma = pltpu.SemaphoreType.DMA
    return pl.pallas_call(
        finish_kernel,
        name="finish",
        out_shape=jax.ShapeDtypeStruct((rows, depth), jnp.float32),
        in_specs=[hbm, pl.BlockSpec(memory_space=pltpu.HBM), hbm],
        out_specs=vmem,
        scratch_shapes=[
            pltpu.VMEM((SLICES // 2, rows, 2 * width), jnp.bfloat16),
            pltpu.VMEM(wall.shape, jnp.bfloat16),
            dma((SLICES,)), dma((SLICES,)), dma((8,)), dma((8,)), dma((8,)), dma((8,)), dma((16,)), dma(()),
        ],
        compiler_params=pltpu.CompilerParams(
            vmem_limit_bytes=32 * MIB, collective_id=1, has_side_effects=True
        ),
    )(attn, w_out, wall)


def per_device(tokens, shift, mod_scale, gate, w_qkv, q_gain, k_gain, w_out, pattern, counts):
    w_parts = w_out.reshape(2, 4, w_out.shape[0] // 8, w_out.shape[1])
    q, kv, wall = gather_project(tokens, shift, mod_scale, jnp.transpose(w_qkv, (1, 0, 2)), q_gain, k_gain, w_parts)
    block = lax.axis_index("frame") // 2 * 2 + lax.axis_index("rep")
    attn = attention(q, kv, pattern, counts, block)
    result = finish(attn, tokens.shape[0], w_parts, wall)
    return (tokens.astype(jnp.float32) + gate * result).astype(jnp.bfloat16)


def solution(mesh):
    placed = (
        P(("rep", "frame", "head"), None),
        P(),
        P(),
        P(),
        P(None, "head", None),
        P(),
        P(),
        P("head", None),
        P(),
        P(),
    )
    return jax.shard_map(
        per_device,
        mesh=mesh,
        in_specs=placed,
        out_specs=P(("rep", "frame", "head"), None),
        check_vma=False,
    )
```

```python
import functools

import jax
import jax.numpy as jnp
from jax import lax
from jax.experimental import pallas as pl
from jax.experimental.pallas import tpu as pltpu
from jax.sharding import PartitionSpec as P

TILE = 384
GS = 4
HD = 128
NT = 8
ROWS = GS * TILE
NONE = 9 * GS
MIB = 1024 * 1024
QSCALE = HD**-0.5 * 1.4426950408889634


def head_norm(values, gain):
    square = jnp.mean(values * values, axis=-1, keepdims=True)
    return (values * lax.rsqrt(square + 1e-06) * gain).astype(jnp.bfloat16)


MESH = pl.DeviceIdType.MESH
CHUNKS = 4
SWAP, YP_OWN, YM_OWN, Z_OWN, YP_FWD, YM_FWD, YP_PEER, YM_PEER, Z_OPP = range(0, 4 * 9, 4)
Z_BELOW, Z_ABOVE = YP_PEER, YM_PEER
MESSAGES = 36
W_YP, W_YM, W_YP_FWD, W_YM_FWD, W_ZF, W_ZF_ALL, W_XP, W_XM, W_SIB, W_SIB_ALL = 0, 1, 2, 3, 4, 7, 8, 14, 20, 38
W_MESSAGES = 42
SLICES = 8


def place():
    f, h, c = lax.axis_index("frame"), lax.axis_index("head"), lax.axis_index("rep")
    return f // 2, f % 2, h // 2, h % 2, c


def gather_kernel(heads, tok_hbm, scale_hbm, shift_hbm, w_hbm, qg_hbm, kg_hbm, wo_ref, q_out, kv_out, wall,
                  tok_ref, scale_ref, shift_ref, qg_ref, kg_ref, in_sem, xbuf, mine, w, qbuf, kvbuf, send, recv, halo_send, halo_recv, out_sem, w_sem, wo_send, wo_recv):
    x, zh, y, zl, c = place()
    nx = lax.axis_size("frame") // 2
    rows = mine.shape[0]
    part = rows // CHUNKS
    pos = y * 2 + zl
    flip = (zh + c) % 2
    yp, ym = {"head": (y + 1) % 4 * 2 + zl}, {"head": (y + 3) % 4 * 2 + zl}
    zp = {"head": y * 2 + 1 - zl}
    partner = {"frame": x * 2 + 1 - zh, "head": y * 2 + 1 - zl, "rep": 1 - c}
    sibling = {"rep": 1 - c}
    xn = {"frame": (x + nx + 2 * c - 1) % nx * 2 + zh, "rep": 1 - c}

    zf = {"frame": x * 2 + 1 - zh, "head": y * 2 + 1 - zl}
    xp, xm = {"frame": (x + 1) % nx * 2 + zh}, {"frame": (x + nx - 1) % nx * 2 + zh}

    barrier = pltpu.get_barrier_semaphore()
    neighbours = (yp, ym, zp, partner, sibling, xn, zf, xp, xm)
    for device in neighbours:
        pl.semaphore_signal(barrier, inc=1, device_id=device, device_id_type=MESH)

    in_copies = [
        pltpu.make_async_copy(source, into, in_sem.at[n])
        for n, (source, into) in enumerate((
            (tok_hbm, tok_ref), (scale_hbm, scale_ref), (shift_hbm, shift_ref), (qg_hbm, qg_ref), (kg_hbm, kg_ref),
        ))
    ]
    for copy in in_copies:
        copy.start()
    w_copies = [
        pltpu.make_async_copy(w_hbm.at[h], w.at[:, h * 3 * HD : (h + 1) * 3 * HD], w_sem.at[h]) for h in range(heads)
    ]
    for copy in w_copies:
        copy.start()

    def chunk(k):
        return pl.ds(k * part, part)

    for copy in in_copies:
        copy.wait()
    scale = 1.0 + scale_ref[...]

    def normalise(k):
        values = tok_ref[chunk(k), :].astype(jnp.float32)
        center = jnp.mean(values, axis=-1, keepdims=True)
        centred = values - center
        spread = jnp.mean(centred * centred, axis=-1, keepdims=True)
        normed = (centred * lax.rsqrt(spread + 1e-06) * scale + shift_ref[...]).astype(jnp.bfloat16)
        mine[chunk(k), :] = normed

        @pl.when(flip == 0)
        def _():
            xbuf[pos, chunk(k), :] = normed

    def slot_of(dy, dz):
        return (y + dy) % 4 * 2 + (zl + dz) % 2

    def message(number, k, slot, device):
        there = xbuf.at[slot, chunk(k)]
        return pltpu.make_async_remote_copy(
            src_ref=there, dst_ref=there, send_sem=send.at[number + k], recv_sem=recv.at[number + k],
            device_id=device, device_id_type=MESH,
        )

    def swap(k, slot):
        return pltpu.make_async_remote_copy(
            src_ref=mine.at[chunk(k)], dst_ref=xbuf.at[slot, chunk(k)], send_sem=send.at[SWAP + k],
            recv_sem=recv.at[SWAP + k], device_id=partner, device_id_type=MESH,
        )

    half = wo_ref.shape[-1] // 2

    def piece(number, src, dst, device):
        return pltpu.make_async_remote_copy(
            src_ref=src, dst_ref=dst, send_sem=wo_send.at[number], recv_sem=wo_recv.at[number],
            device_id=device, device_id_type=MESH,
        )

    def held(dy, zl_, k):
        return wall.at[dy, zl_, c, k]

    def w_first(number, dy, device):
        return piece(number, wo_ref.at[c, x], held(dy, zl, x), device)

    def w_forward(number, dy, cols, device):
        return piece(number, held(dy, zl, x).at[:, cols], held(2, zl, x).at[:, cols], device)

    def w_diagonal(dy, zl_):
        return piece(W_ZF + dy - 1, held(dy, zl_, x), held(dy, zl_, x), zf)

    def w_diagonal_all(zl_, k):
        both = pl.ds(k, 2)
        return piece(W_ZF_ALL + k // 2 * (W_MESSAGES - 1 - W_ZF_ALL), wo_ref.at[c, both], wall.at[0, zl_, c, both], zf)

    def w_along(number, dy, z, k, device):
        return piece(number + 2 * (dy - 1) + z, held(dy, (zl + z) % 2, k), held(dy, (zl + z) % 2, k), device)

    def w_sibling(which, dy, z, core):
        there = wall.at[dy, (zl + z) % 2, core, (x + which) % 4]
        return piece(W_SIB + 6 * {0: 0, 1: 1, 3: 2}[which] + 2 * (dy - 1) + z, there, there, sibling)

    def w_sibling_all(core, k):
        there = wall.at[0, 1 - zl, core, pl.ds(k, 2)]
        return piece(W_SIB_ALL + k, there, there, sibling)

    def w_half(k):
        w_diagonal_all(1 - zl, k).wait_recv()
        w_sibling_all(c, k).start()

    def w_spread(dy, z):
        w_along(W_XP, dy, z, x, xp).start()
        w_along(W_XM, dy, z, x, xm).start()
        w_sibling(0, dy, z, c).start()

    low, high = pl.ds(0, half), pl.ds(half, half)

    def w_one():
        w_first(W_YP, 3, yp).wait_recv()
        w_forward(W_YP_FWD, 3, low, yp).start()
        w_diagonal(3, zl).start()
        w_spread(3, 0)
        w_first(W_YM, 1, ym).wait_recv()
        w_forward(W_YM_FWD, 1, high, ym).start()
        w_diagonal(1, zl).start()
        w_spread(1, 0)

    def w_two():
        for dy in (3, 1):
            w_diagonal(dy, 1 - zl).wait_recv()
            w_spread(dy, 1)
        w_diagonal_all(zl, 0).start()

    def w_three():
        w_forward(W_YP_FWD, 2, low, yp).wait_recv()
        w_forward(W_YM_FWD, 2, high, ym).wait_recv()
        w_diagonal(2, zl).start()
        w_spread(2, 0)
        w_diagonal_all(zl, 2).start()

    def w_four():
        w_diagonal(2, 1 - zl).wait_recv()
        w_spread(2, 1)

    def w_five(z):
        for dy in (3, 1, 2):
            w_along(W_XP, dy, z, (x + 3) % 4, xp).wait_recv()
            w_sibling(3, dy, z, c).start()
            w_along(W_XM, dy, z, (x + 1) % 4, xm).wait_recv()
            w_sibling(1, dy, z, c).start()

    def arrive(number, k, slot):
        message(number, k, slot, zp).wait_recv()

    def own(number, ks, device):
        for k in ks:
            message(number, k, pos, device).start()

    def own_out(k, to_yp, to_ym):
        own(Z_OWN, (k,), zp)
        own(YP_OWN, to_yp, yp)
        own(YM_OWN, to_ym, ym)

    first_out = ((0, (0,), ()), (3, (), (3,)), (1, (1,), ()), (2, (), (2,)))
    for k, to_yp, to_ym in first_out:
        normalise(k)
        if k == 0:
            pl.semaphore_wait(barrier, len(neighbours))
            w_first(W_YP, 3, yp).start()
            w_first(W_YM, 1, ym).start()

        @pl.when(flip == 1)
        def _():
            swap(k, y * 2 + 1 - zl).start()

        @pl.when(flip == 0)
        def _():
            own_out(k, to_yp, to_ym)

    @pl.when(flip == 1)
    def _():
        for k, to_yp, to_ym in first_out:
            swap(k, pos).wait_recv()
            own_out(k, to_yp, to_ym)

    below, above, across, facing = slot_of(3, 0), slot_of(1, 0), slot_of(0, 1), slot_of(2, 0)

    def peer(k):
        arrive(Z_OWN, k, across)
        if k != 0:
            message(YP_PEER, k, across, yp).start()
        if k != 3:
            message(YM_PEER, k, across, ym).start()

    def forward_up(k):
        arrive(YP_OWN, k, below)
        message(YP_FWD, k, below, yp).start()

    def forward_down(k):
        arrive(YM_OWN, k, above)
        message(YM_FWD, k, above, ym).start()

    def opposite(number, k):
        arrive(number, k, facing)
        message(Z_OPP, k, facing, zp).start()

    def second():
        w_one()
        forward_up(0)
        message(Z_BELOW, 0, below, zp).start()
        forward_down(3)
        message(Z_ABOVE, 3, above, zp).start()
        forward_up(1)
        forward_down(2)
        own(YP_OWN, (2, 3), yp)
        own(YM_OWN, (1, 0), ym)
        peer(0)
        peer(3)
        w_two()
        peer(1)
        opposite(YP_FWD, 0)
        opposite(YM_FWD, 3)
        peer(2)
        w_three()
        opposite(YP_FWD, 1)
        opposite(YM_FWD, 2)
        w_four()

    def fourth():
        arrive(YP_OWN, 2, below)
        arrive(YP_OWN, 3, below)

    def fifth():
        arrive(YM_OWN, 1, above)
        arrive(YM_OWN, 0, above)

    last = ((3, YP_PEER), (1, YM_PEER), (2, Z_OPP))

    def last_chunk(k):
        def handler():
            if k == 0:
                w_half(0)
            for dy, number in last:
                arrive(number, k, slot_of(dy, 1))

        return handler

    order = ((0, 0, None), (0, 1, second), (2, 0, None), (3, 0, fourth), (1, 0, fifth))

    def slice_rows(s):
        return pl.ds(pl.multiple_of(s * rows, rows), rows)

    def halo(s, k, slot, number, device):
        rows_ = slice_rows(s) if k is None else pl.ds(pl.multiple_of(s * rows + k * part, part), part)
        sem = number + CHUNKS * s + (0 if k is None else k)
        return pltpu.make_async_remote_copy(
            src_ref=kvbuf.at[rows_], dst_ref=kv_out.at[slot, rows_], send_sem=halo_send.at[sem],
            recv_sem=halo_recv.at[sem], device_id=device, device_id_type=MESH,
        )

    def halos(s, k):
        return halo(s, k, 2, CHUNKS * SLICES, xn), halo(s, k, 1, 0, sibling)

    def out_copies(s):
        return (
            pltpu.make_async_copy(qbuf.at[slice_rows(s)], q_out.at[slice_rows(s)], out_sem.at[s]),
            pltpu.make_async_copy(kvbuf.at[slice_rows(s)], kv_out.at[0, slice_rows(s)], out_sem.at[SLICES + s]),
        )

    def slice_of(dy, dz, flip_):
        return (y + dy) % 4 * 2 + (zl + dz + flip_) % 2

    q_gain = qg_ref[...] * QSCALE

    def put(mixed, spans):
        for h in range(heads):
            at = h * 3 * HD
            query = head_norm(mixed[:, at : at + HD], q_gain)
            key = head_norm(mixed[:, at + HD : at + 2 * HD], kg_ref[...])
            value = mixed[:, at + 2 * HD : at + 3 * HD].astype(jnp.bfloat16)
            for first, count, here in spans:
                taken = slice(first, first + count)
                qbuf[here, h * HD : (h + 1) * HD] = query[taken]
                kvbuf[here, h * HD : (h + 1) * HD] = key[taken]
                kvbuf[here, (heads + h) * HD : (heads + h + 1) * HD] = value[taken]

    def step(n, carry):
        dy, dz = jnp.int32(0), jnp.int32(0)
        for k, (one, two, handler) in enumerate(order):
            dy = jnp.where(n == k, one, dy)
            dz = jnp.where(n == k, two, dz)
            if handler is not None:
                pl.when(n == k)(handler)
        s = slice_of(dy, dz, flip)
        put(jnp.dot(xbuf[slot_of(dy, dz)], w[...], preferred_element_type=jnp.float32), ((0, rows, slice_rows(s)),))
        for copy in halos(s, None) + out_copies(s):
            copy.start()
        return carry

    for copy in w_copies:
        copy.wait()
    lax.fori_loop(0, len(order), step, 0)

    def last_step(n, carry):
        k = jnp.int32(0)
        for at, one in enumerate((0, 3, 1, 2)):
            k = jnp.where(n == at, one, k)
            pl.when(n == at)(last_chunk(one))
        taken, spans = [], []
        for dy, _ in last:
            s = slice_of(dy, 1, flip)
            spans.append((len(taken) * part, part, pl.ds(pl.multiple_of(s * rows + k * part, part), part)))
            taken.append(xbuf[slot_of(dy, 1), pl.ds(pl.multiple_of(k * part, part), part), :])
        put(jnp.dot(jnp.concatenate(taken, axis=0), w[...], preferred_element_type=jnp.float32), spans)
        for dy, _ in last:
            s = slice_of(dy, 1, flip)
            for copy in halos(s, k):
                copy.start()
        return carry

    lax.fori_loop(0, CHUNKS, last_step, 0)
    for dy, _ in last:
        for copy in out_copies(slice_of(dy, 1, flip)):
            copy.start()
    w_half(2)
    w_five(0)
    w_five(1)

    @pl.when(flip == 1)
    def _():
        for k in range(CHUNKS):
            swap(k, y * 2 + 1 - zl).wait_send()

    for number, ks in ((YP_OWN, range(4)), (YM_OWN, range(4)), (Z_OWN, range(4)), (YP_FWD, (0, 1)), (YM_FWD, (2, 3)),
                       (YP_PEER, range(4)), (YM_PEER, range(4)), (Z_OPP, range(4))):
        for k in ks:
            message(number, k, pos, zp).wait_send()

    for dy, dz in [one[:2] for one in order]:
        for copy in out_copies(slice_of(dy, dz, flip)):
            copy.wait()
        for copy in halos(slice_of(dy, dz, flip), None):
            copy.wait_send()
        for copy in halos(slice_of(dy, dz, 1 - flip), None):
            copy.wait_recv()
    for dy, _ in last:
        for copy in out_copies(slice_of(dy, 1, flip)):
            copy.wait()
        for k in range(CHUNKS):
            for copy in halos(slice_of(dy, 1, flip), k):
                copy.wait_send()
            for copy in halos(slice_of(dy, 1, 1 - flip), k):
                copy.wait_recv()
    w_first(W_YP, 3, yp).wait_send()
    w_first(W_YM, 1, ym).wait_send()
    w_forward(W_YP_FWD, 2, low, yp).wait_send()
    w_forward(W_YM_FWD, 2, high, ym).wait_send()
    w_diagonal_all(zl, 0).wait_send()
    w_diagonal_all(zl, 2).wait_send()
    w_sibling_all(1 - c, 0).wait()
    w_sibling_all(1 - c, 2).wait()
    for dy in (1, 2, 3):
        w_diagonal(dy, zl).wait_send()
        for z in (0, 1):
            w_along(W_XP, dy, z, x, xp).wait_send()
            w_along(W_XM, dy, z, x, xm).wait_send()
            for which in (0, 1, 3):
                w_sibling(which, dy, z, 1 - c).wait()


def gather_project(tokens, shift, mod_scale, w, q_gain, k_gain, w_out):
    rows, depth = tokens.shape
    heads = w.shape[0]
    width = heads * HD
    hbm = pl.BlockSpec(memory_space=pl.ANY)
    dma = pltpu.SemaphoreType.DMA
    return pl.pallas_call(
        functools.partial(gather_kernel, heads),
        name="gather_project",
        out_shape=(
            jax.ShapeDtypeStruct((SLICES * rows, width), jnp.bfloat16),
            jax.ShapeDtypeStruct((3, SLICES * rows, 2 * width), jnp.bfloat16),
            jax.ShapeDtypeStruct((4, 2) + w_out.shape, jnp.bfloat16),
        ),
        in_specs=[pl.BlockSpec(memory_space=pltpu.HBM)] * 7,
        out_specs=(hbm, hbm, hbm),
        scratch_shapes=[
            pltpu.VMEM((rows, depth), jnp.bfloat16),
            pltpu.VMEM((1, depth), jnp.float32),
            pltpu.VMEM((1, depth), jnp.float32),
            pltpu.VMEM((1, HD), jnp.float32),
            pltpu.VMEM((1, HD), jnp.float32),
            dma((5,)),
            pltpu.VMEM((SLICES, rows, depth), jnp.bfloat16),
            pltpu.VMEM((rows, depth), jnp.bfloat16),
            pltpu.VMEM((depth, 3 * width), jnp.bfloat16),
            pltpu.VMEM((SLICES * rows, width), jnp.bfloat16),
            pltpu.VMEM((SLICES * rows, 2 * width), jnp.bfloat16),
            dma((MESSAGES,)), dma((MESSAGES,)), dma((2 * CHUNKS * SLICES,)), dma((2 * CHUNKS * SLICES,)), dma((2 * SLICES,)), dma((heads,)),
            dma((W_MESSAGES,)), dma((W_MESSAGES,)),
        ],
        compiler_params=pltpu.CompilerParams(
            vmem_limit_bytes=36 * MIB, collective_id=0, has_side_effects=True
        ),
    )(*(pltpu.with_memory_space_constraint(one, pltpu.HBM) for one in
        (tokens, mod_scale[None], shift[None], w, q_gain[None], k_gain[None], w_out)))


def attention_kernel(heads, pat_ref, cnt_ref, t_ref, q_ref, kv_ref, out_ref, ones, acc, todo):
    t = t_ref[0]
    width = heads * HD
    slots = (2 - t % 2, 0, 1 + t % 2)
    def list_tile(i, carry):
        count = jnp.int32(0)
        for o in range(3):
            inside = (t + o - 1 >= 0) & (t + o - 1 < NT)
            for j in range(GS):
                todo[i * 14 + 1 + count] = (o * 3 + slots[o]) * GS + j
                live = inside & (pat_ref[o, i, j] > 0)
                count = count + live.astype(jnp.int32)
        todo[i * 14 + 1 + count] = NONE
        todo[i * 14] = (count + 1) // 2
        return carry

    lax.fori_loop(0, GS, list_tile, 0)
    ones[3] = jnp.zeros_like(ones[3])
    place = lax.broadcasted_iota(jnp.int32, (TILE, HD), 0)
    for o in range(3):
        ones[o] = jnp.where(place < cnt_ref[jnp.clip(t + o - 1, 0, NT - 1)], 1.0, 0.0).astype(jnp.bfloat16)
    def keys_of(one, cols):
        return kv_ref[one // GS % 3, one % GS, :, cols]

    def values_of(one, h):
        return kv_ref[one // GS % 3, one % GS, :, width + h * HD : width + (h + 1) * HD] * ones[one // (3 * GS)]

    def tile(i, carry):
        mine = pl.ds(pl.multiple_of(i * TILE, TILE), TILE)
        acc[...] = jnp.zeros_like(acc)

        def attend(which):
            probs = []
            for h in range(heads):
                cols = slice(h * HD, (h + 1) * HD)
                score = lax.dot_general(
                    q_ref[mine, cols],
                    jnp.concatenate([keys_of(one, cols) for one in which], axis=0),
                    (((1,), (1,)), ((), ())),
                    preferred_element_type=jnp.float32,
                )
                probs.append(jnp.exp2(score).astype(jnp.bfloat16))
            valid = jnp.concatenate([ones[one // (3 * GS)] for one in which], axis=0)
            for h in range(heads):
                values = jnp.concatenate([values_of(one, h) for one in which], axis=0)
                acc[h] += jnp.dot(
                    probs[h], jnp.concatenate([values, valid], axis=1), preferred_element_type=jnp.float32
                )

        pairs = todo[i * 14]
        first = i * 14 + 1

        def four(n, carry):
            attend([todo[first + 4 * n + m] for m in range(4)])
            return carry

        lax.fori_loop(0, pairs // 2, four, 0)

        @pl.when(pairs % 2 == 1)
        def _():
            attend([todo[first + 2 * (pairs - 1) + m] for m in range(2)])

        for h in range(heads):
            out_ref[mine, h * HD : (h + 1) * HD] = (acc[h, :, :HD] / acc[h, :, HD:]).astype(jnp.bfloat16)
        return carry

    lax.fori_loop(0, GS, tile, 0)


def attention(q, kv, pattern, counts, t):
    rows, width = q.shape
    heads = width // HD
    smem = pl.BlockSpec(memory_space=pltpu.SMEM)
    vmem = pl.BlockSpec(memory_space=pltpu.VMEM)
    return pl.pallas_call(
        functools.partial(attention_kernel, heads),
        name="attention",
        out_shape=jax.ShapeDtypeStruct((rows, width), jnp.bfloat16),
        in_specs=[smem, smem, smem, vmem, vmem],
        out_specs=vmem,
        scratch_shapes=[
            pltpu.VMEM((GS, TILE, HD), jnp.bfloat16),
            pltpu.VMEM((heads, TILE, 2 * HD), jnp.float32),
            pltpu.SMEM((GS * 14,), jnp.int32),
        ],
        compiler_params=pltpu.CompilerParams(vmem_limit_bytes=32 * MIB),
    )(pattern, counts, t.reshape(1), q, kv.reshape(3, GS, TILE, 2 * width))


def finish_kernel(attn, wo_ref, wall, out_ref, rows_in, wv, a_send, a_recv, x_send, x_recv, s_send, s_recv, w_sem, own_sem):
    x, zh, y, zl, c = place()
    nx = lax.axis_size("frame") // 2
    rows, depth = out_ref.shape
    width = attn.shape[1]
    pos = y * 2 + zl
    straight = zh == c
    sibling = {"rep": 1 - c}
    xp, xm = {"frame": (x + 1) % nx * 2 + zh}, {"frame": (x + nx - 1) % nx * 2 + zh}

    def owner(s):
        return {"frame": x * 2 + c, "head": s, "rep": zh}

    def others(s):
        return jnp.logical_or(s != pos, jnp.logical_not(straight))

    barrier = pltpu.get_barrier_semaphore()
    for device in (sibling, xp, xm):
        pl.semaphore_signal(barrier, inc=1, device_id=device, device_id_type=MESH)

    def greet(s, carry):
        @pl.when(others(s))
        def _():
            pl.semaphore_signal(barrier, inc=1, device_id=owner(s), device_id_type=MESH)

        return carry

    lax.fori_loop(0, SLICES, greet, 0)

    def load(dy, k):
        return pltpu.make_async_copy(wall.at[dy, :, :, k], wv.at[dy, :, :, k], w_sem.at[4 * dy + k])

    def loads(act):
        act(pltpu.make_async_copy(wo_ref, wv.at[0, zl], w_sem.at[0]))
        act(pltpu.make_async_copy(wall.at[0, 1 - zl], wv.at[0, 1 - zl], w_sem.at[1]))

    loads(lambda copy: copy.start())
    for dy in (1, 3, 2):
        for which in (0, 1, 3):
            load(dy, (x + which) % 4).start()
    pl.semaphore_wait(barrier, jnp.where(straight, SLICES + 2, SLICES + 3))

    def landing(source):
        cols = pl.ds(pl.multiple_of(source % 2 * width, width), width)
        return rows_in.at[source // 2, :, cols]

    def hand_out(s, source):
        return pltpu.make_async_remote_copy(
            src_ref=attn.at[pl.ds(pl.multiple_of(s * rows, rows), rows)], dst_ref=landing(source),
            send_sem=a_send.at[s], recv_sem=a_recv.at[source], device_id=owner(s), device_id_type=MESH,
        )

    def keep():
        return pltpu.make_async_copy(
            attn.at[pl.ds(pl.multiple_of(pos * rows, rows), rows)], landing(pos), own_sem
        )

    def far(number, dy, z, k, device):
        return pltpu.make_async_remote_copy(
            src_ref=wall.at[dy, z, c, k], dst_ref=wv.at[dy, z, c, k], send_sem=x_send.at[number + dy],
            recv_sem=x_recv.at[number + dy], device_id=device, device_id_type=MESH,
        )

    def scatter(n, carry):
        ahead = jnp.where(n < 4, n // 2, 5 - n // 2)
        s = (y + ahead) % 4 * 2 + (zl + n) % 2

        @pl.when(others(s))
        def _():
            hand_out(s, pos).start()

        return carry

    for dy in (1, 3, 2):
        far(0, dy, 0, (x + 3) % 4, xp).start()
        far(4, dy, 1, (x + 1) % 4, xm).start()
    lax.fori_loop(0, SLICES, scatter, 0)

    @pl.when(straight)
    def _():
        keep().start()

    def share(number, dy, z, core):
        there = wv.at[dy, z, core, (x + 2) % 4]
        return pltpu.make_async_remote_copy(
            src_ref=there, dst_ref=there, send_sem=s_send.at[number + dy], recv_sem=s_recv.at[number + dy],
            device_id=sibling, device_id_type=MESH,
        )

    cols = depth

    def arrived(dy, z):
        source = (y + dy) % 4 * 2 + (zl + z) % 2
        kept = jnp.logical_and(straight, source == pos)

        @pl.when(kept)
        def _():
            keep().wait()

        @pl.when(jnp.logical_not(kept))
        def _():
            hand_out(0, source).wait_recv()

    def add(dy, first):
        arrived(dy, 0)
        arrived(dy, 1)

        def column(n, carry):
            here = pl.ds(pl.multiple_of(n * cols, cols), cols)
            weight = wv[dy, :, :, :, :, here].reshape(2 * width, cols)
            term = jnp.dot(rows_in[(y + dy) % 4], weight, preferred_element_type=jnp.float32)
            out_ref[:, here] = term if first else out_ref[:, here] + term
            return carry

        lax.fori_loop(0, depth // cols, column, 0)

    loads(lambda copy: copy.wait())
    add(0, True)
    for dy in (1, 3, 2):
        far(0, dy, 0, (x + 2) % 4, xp).wait_recv()
        share(0, dy, 0, c).start()
        far(4, dy, 1, (x + 2) % 4, xm).wait_recv()
        share(4, dy, 1, c).start()
        for which in (0, 1, 3):
            load(dy, (x + which) % 4).wait()
        share(0, dy, 0, 1 - c).wait_recv()
        share(4, dy, 1, 1 - c).wait_recv()
        add(dy, False)

    def sent(s, carry):
        @pl.when(others(s))
        def _():
            hand_out(s, pos).wait_send()

        return carry

    lax.fori_loop(0, SLICES, sent, 0)
    for dy in (1, 3, 2):
        far(0, dy, 0, (x + 3) % 4, xp).wait_send()
        far(4, dy, 1, (x + 1) % 4, xm).wait_send()
        share(0, dy, 0, c).wait_send()
        share(4, dy, 1, c).wait_send()


def finish(attn, rows, w_out, wall):
    width = attn.shape[1]
    depth = wall.shape[-1]
    vmem = pl.BlockSpec(memory_space=pltpu.VMEM)
    hbm = pl.BlockSpec(memory_space=pl.ANY)
    dma = pltpu.SemaphoreType.DMA
    return pl.pallas_call(
        finish_kernel,
        name="finish",
        out_shape=jax.ShapeDtypeStruct((rows, depth), jnp.float32),
        in_specs=[hbm, pl.BlockSpec(memory_space=pltpu.HBM), hbm],
        out_specs=vmem,
        scratch_shapes=[
            pltpu.VMEM((SLICES // 2, rows, 2 * width), jnp.bfloat16),
            pltpu.VMEM(wall.shape, jnp.bfloat16),
            dma((SLICES,)), dma((SLICES,)), dma((8,)), dma((8,)), dma((8,)), dma((8,)), dma((16,)), dma(()),
        ],
        compiler_params=pltpu.CompilerParams(
            vmem_limit_bytes=32 * MIB, collective_id=1, has_side_effects=True
        ),
    )(attn, w_out, wall)


def per_device(tokens, shift, mod_scale, gate, w_qkv, q_gain, k_gain, w_out, pattern, counts):
    w_parts = w_out.reshape(2, 4, w_out.shape[0] // 8, w_out.shape[1])
    q, kv, wall = gather_project(tokens, shift, mod_scale, jnp.transpose(w_qkv, (1, 0, 2)), q_gain, k_gain, w_parts)
    block = lax.axis_index("frame") // 2 * 2 + lax.axis_index("rep")
    attn = attention(q, kv, pattern, counts, block)
    result = finish(attn, tokens.shape[0], w_parts, wall)
    return (tokens.astype(jnp.float32) + gate * result).astype(jnp.bfloat16)


def solution(mesh):
    placed = (
        P(("rep", "frame", "head"), None),
        P(),
        P(),
        P(),
        P(None, "head", None),
        P(),
        P(),
        P("head", None),
        P(),
        P(),
    )
    return jax.shard_map(
        per_device,
        mesh=mesh,
        in_specs=placed,
        out_specs=P(("rep", "frame", "head"), None),
        check_vma=False,
    )
```

```python
import functools

import jax
import jax.numpy as jnp
from jax import lax
from jax.experimental import pallas as pl
from jax.experimental.pallas import tpu as pltpu
from jax.sharding import PartitionSpec as P

TILE = 384
GS = 4
HD = 128
NT = 8
ROWS = GS * TILE
NONE = 9 * GS
MIB = 1024 * 1024
QSCALE = HD**-0.5 * 1.4426950408889634


def head_norm(values, gain):
    square = jnp.mean(values * values, axis=-1, keepdims=True)
    return (values * lax.rsqrt(square + 1e-06) * gain).astype(jnp.bfloat16)


MESH = pl.DeviceIdType.MESH
CHUNKS = 4
SWAP, YP_OWN, YM_OWN, Z_OWN, YP_FWD, YM_FWD, YP_PEER, YM_PEER, Z_OPP = range(0, 4 * 9, 4)
Z_BELOW, Z_ABOVE = YP_PEER, YM_PEER
MESSAGES = 36
W_YP, W_YM, W_YP_FWD, W_YM_FWD, W_ZF, W_ZF_ALL, W_XP, W_XM, W_SIB, W_SIB_ALL = 0, 1, 2, 3, 4, 7, 8, 14, 20, 38
W_MESSAGES = 42
SLICES = 8


def place():
    f, h, c = lax.axis_index("frame"), lax.axis_index("head"), lax.axis_index("rep")
    return f // 2, f % 2, h // 2, h % 2, c


def gather_kernel(heads, tok_hbm, scale_hbm, shift_hbm, w_hbm, qg_hbm, kg_hbm, wo_ref, q_out, kv_out, wall,
                  tok_ref, scale_ref, shift_ref, qg_ref, kg_ref, in_sem, xbuf, mine, w, qbuf, kvbuf, send, recv, halo_send, halo_recv, out_sem, w_sem, wo_send, wo_recv):
    x, zh, y, zl, c = place()
    nx = lax.axis_size("frame") // 2
    rows = mine.shape[0]
    part = rows // CHUNKS
    pos = y * 2 + zl
    flip = (zh + c) % 2
    yp, ym = {"head": (y + 1) % 4 * 2 + zl}, {"head": (y + 3) % 4 * 2 + zl}
    zp = {"head": y * 2 + 1 - zl}
    partner = {"frame": x * 2 + 1 - zh, "head": y * 2 + 1 - zl, "rep": 1 - c}
    sibling = {"rep": 1 - c}
    xn = {"frame": (x + nx + 2 * c - 1) % nx * 2 + zh, "rep": 1 - c}

    zf = {"frame": x * 2 + 1 - zh, "head": y * 2 + 1 - zl}
    xp, xm = {"frame": (x + 1) % nx * 2 + zh}, {"frame": (x + nx - 1) % nx * 2 + zh}

    barrier = pltpu.get_barrier_semaphore()
    neighbours = (yp, ym, zp, partner, sibling, xn, zf, xp, xm)
    for device in neighbours:
        pl.semaphore_signal(barrier, inc=1, device_id=device, device_id_type=MESH)

    in_copies = [
        pltpu.make_async_copy(source, into, in_sem.at[n])
        for n, (source, into) in enumerate((
            (tok_hbm, tok_ref), (scale_hbm, scale_ref), (shift_hbm, shift_ref), (qg_hbm, qg_ref), (kg_hbm, kg_ref),
        ))
    ]
    for copy in in_copies:
        copy.start()
    w_copies = [
        pltpu.make_async_copy(w_hbm.at[h], w.at[:, h * 3 * HD : (h + 1) * 3 * HD], w_sem.at[h]) for h in range(heads)
    ]
    for copy in w_copies:
        copy.start()

    def chunk(k):
        return pl.ds(k * part, part)

    for copy in in_copies:
        copy.wait()
    scale = 1.0 + scale_ref[...]

    def normalise(k):
        values = tok_ref[chunk(k), :].astype(jnp.float32)
        center = jnp.mean(values, axis=-1, keepdims=True)
        centred = values - center
        spread = jnp.mean(centred * centred, axis=-1, keepdims=True)
        normed = (centred * lax.rsqrt(spread + 1e-06) * scale + shift_ref[...]).astype(jnp.bfloat16)
        mine[chunk(k), :] = normed

        @pl.when(flip == 0)
        def _():
            xbuf[pos, chunk(k), :] = normed

    def slot_of(dy, dz):
        return (y + dy) % 4 * 2 + (zl + dz) % 2

    def message(number, k, slot, device):
        there = xbuf.at[slot, chunk(k)]
        return pltpu.make_async_remote_copy(
            src_ref=there, dst_ref=there, send_sem=send.at[number + k], recv_sem=recv.at[number + k],
            device_id=device, device_id_type=MESH,
        )

    def swap(k, slot):
        return pltpu.make_async_remote_copy(
            src_ref=mine.at[chunk(k)], dst_ref=xbuf.at[slot, chunk(k)], send_sem=send.at[SWAP + k],
            recv_sem=recv.at[SWAP + k], device_id=partner, device_id_type=MESH,
        )

    half = wo_ref.shape[-1] // 2

    def piece(number, src, dst, device):
        return pltpu.make_async_remote_copy(
            src_ref=src, dst_ref=dst, send_sem=wo_send.at[number], recv_sem=wo_recv.at[number],
            device_id=device, device_id_type=MESH,
        )

    def held(dy, zl_, k):
        return wall.at[dy, zl_, c, k]

    def w_first(number, dy, device):
        return piece(number, wo_ref.at[c, x], held(dy, zl, x), device)

    def w_forward(number, dy, cols, device):
        return piece(number, held(dy, zl, x).at[:, cols], held(2, zl, x).at[:, cols], device)

    def w_diagonal(dy, zl_):
        return piece(W_ZF + dy - 1, held(dy, zl_, x), held(dy, zl_, x), zf)

    def w_diagonal_all(zl_, k):
        both = pl.ds(k, 2)
        return piece(W_ZF_ALL + k // 2 * (W_MESSAGES - 1 - W_ZF_ALL), wo_ref.at[c, both], wall.at[0, zl_, c, both], zf)

    def w_along(number, dy, z, k, device):
        return piece(number + 2 * (dy - 1) + z, held(dy, (zl + z) % 2, k), held(dy, (zl + z) % 2, k), device)

    def w_sibling(which, dy, z, core):
        there = wall.at[dy, (zl + z) % 2, core, (x + which) % 4]
        return piece(W_SIB + 6 * {0: 0, 1: 1, 3: 2}[which] + 2 * (dy - 1) + z, there, there, sibling)

    def w_sibling_all(core, k):
        there = wall.at[0, 1 - zl, core, pl.ds(k, 2)]
        return piece(W_SIB_ALL + k, there, there, sibling)

    def w_half(k):
        w_diagonal_all(1 - zl, k).wait_recv()
        w_sibling_all(c, k).start()

    def w_spread(dy, z):
        w_along(W_XP, dy, z, x, xp).start()
        w_along(W_XM, dy, z, x, xm).start()
        w_sibling(0, dy, z, c).start()

    low, high = pl.ds(0, half), pl.ds(half, half)

    def w_one():
        w_first(W_YP, 3, yp).wait_recv()
        w_forward(W_YP_FWD, 3, low, yp).start()
        w_diagonal(3, zl).start()
        w_spread(3, 0)
        w_first(W_YM, 1, ym).wait_recv()
        w_forward(W_YM_FWD, 1, high, ym).start()
        w_diagonal(1, zl).start()
        w_spread(1, 0)

    def w_two():
        for dy in (3, 1):
            w_diagonal(dy, 1 - zl).wait_recv()
            w_spread(dy, 1)
        w_diagonal_all(zl, 0).start()

    def w_three():
        w_forward(W_YP_FWD, 2, low, yp).wait_recv()
        w_forward(W_YM_FWD, 2, high, ym).wait_recv()
        w_diagonal(2, zl).start()
        w_spread(2, 0)
        w_diagonal_all(zl, 2).start()

    def w_four():
        w_diagonal(2, 1 - zl).wait_recv()
        w_spread(2, 1)

    def w_five(z):
        for dy in (3, 1, 2):
            w_along(W_XP, dy, z, (x + 3) % 4, xp).wait_recv()
            w_sibling(3, dy, z, c).start()
            w_along(W_XM, dy, z, (x + 1) % 4, xm).wait_recv()
            w_sibling(1, dy, z, c).start()

    def arrive(number, k, slot):
        message(number, k, slot, zp).wait_recv()

    def own(number, ks, device):
        for k in ks:
            message(number, k, pos, device).start()

    def own_out(k, to_yp, to_ym):
        own(Z_OWN, (k,), zp)
        own(YP_OWN, to_yp, yp)
        own(YM_OWN, to_ym, ym)

    first_out = ((0, (0,), ()), (3, (), (3,)), (1, (1,), ()), (2, (), (2,)))
    for k, to_yp, to_ym in first_out:
        normalise(k)
        if k == 0:
            pl.semaphore_wait(barrier, len(neighbours))
            w_first(W_YP, 3, yp).start()
            w_first(W_YM, 1, ym).start()

        @pl.when(flip == 1)
        def _():
            swap(k, y * 2 + 1 - zl).start()

        @pl.when(flip == 0)
        def _():
            own_out(k, to_yp, to_ym)

    @pl.when(flip == 1)
    def _():
        for k, to_yp, to_ym in first_out:
            swap(k, pos).wait_recv()
            own_out(k, to_yp, to_ym)

    below, above, across, facing = slot_of(3, 0), slot_of(1, 0), slot_of(0, 1), slot_of(2, 0)

    def peer(k):
        arrive(Z_OWN, k, across)
        if k != 0:
            message(YP_PEER, k, across, yp).start()
        if k != 3:
            message(YM_PEER, k, across, ym).start()

    def forward_up(k):
        arrive(YP_OWN, k, below)
        message(YP_FWD, k, below, yp).start()

    def forward_down(k):
        arrive(YM_OWN, k, above)
        message(YM_FWD, k, above, ym).start()

    def opposite(number, k):
        arrive(number, k, facing)
        message(Z_OPP, k, facing, zp).start()

    def second():
        w_one()
        forward_up(0)
        message(Z_BELOW, 0, below, zp).start()
        forward_down(3)
        message(Z_ABOVE, 3, above, zp).start()
        forward_up(1)
        forward_down(2)
        own(YP_OWN, (2, 3), yp)
        own(YM_OWN, (1, 0), ym)
        peer(0)
        peer(3)
        w_two()
        peer(1)
        opposite(YP_FWD, 0)
        opposite(YM_FWD, 3)
        peer(2)
        w_three()
        opposite(YP_FWD, 1)
        opposite(YM_FWD, 2)
        w_four()

    def fourth():
        arrive(YP_OWN, 2, below)
        arrive(YP_OWN, 3, below)

    def fifth():
        arrive(YM_OWN, 1, above)
        arrive(YM_OWN, 0, above)

    last = ((3, YP_PEER), (1, YM_PEER), (2, Z_OPP))

    def last_chunk(k):
        def handler():
            if k == 1:
                w_half(0)
            for dy, number in last:
                arrive(number, k, slot_of(dy, 1))

        return handler

    order = ((0, 0, None), (0, 1, second), (2, 0, None), (3, 0, fourth), (1, 0, fifth))

    def slice_rows(s):
        return pl.ds(pl.multiple_of(s * rows, rows), rows)

    def halo(s, k, slot, number, device):
        rows_ = slice_rows(s) if k is None else pl.ds(pl.multiple_of(s * rows + k * part, part), part)
        sem = number + CHUNKS * s + (0 if k is None else k)
        return pltpu.make_async_remote_copy(
            src_ref=kvbuf.at[rows_], dst_ref=kv_out.at[slot, rows_], send_sem=halo_send.at[sem],
            recv_sem=halo_recv.at[sem], device_id=device, device_id_type=MESH,
        )

    def halos(s, k):
        return halo(s, k, 2, CHUNKS * SLICES, xn), halo(s, k, 1, 0, sibling)

    def out_copies(s):
        return (
            pltpu.make_async_copy(qbuf.at[slice_rows(s)], q_out.at[slice_rows(s)], out_sem.at[s]),
            pltpu.make_async_copy(kvbuf.at[slice_rows(s)], kv_out.at[0, slice_rows(s)], out_sem.at[SLICES + s]),
        )

    def slice_of(dy, dz, flip_):
        return (y + dy) % 4 * 2 + (zl + dz + flip_) % 2

    q_gain = qg_ref[...] * QSCALE

    def put(mixed, spans):
        for h in range(heads):
            at = h * 3 * HD
            query = head_norm(mixed[:, at : at + HD], q_gain)
            key = head_norm(mixed[:, at + HD : at + 2 * HD], kg_ref[...])
            value = mixed[:, at + 2 * HD : at + 3 * HD].astype(jnp.bfloat16)
            for first, count, here in spans:
                taken = slice(first, first + count)
                qbuf[here, h * HD : (h + 1) * HD] = query[taken]
                kvbuf[here, h * HD : (h + 1) * HD] = key[taken]
                kvbuf[here, (heads + h) * HD : (heads + h + 1) * HD] = value[taken]

    def step(n, carry):
        dy, dz = jnp.int32(0), jnp.int32(0)
        for k, (one, two, handler) in enumerate(order):
            dy = jnp.where(n == k, one, dy)
            dz = jnp.where(n == k, two, dz)
            if handler is not None:
                pl.when(n == k)(handler)
        s = slice_of(dy, dz, flip)
        put(jnp.dot(xbuf[slot_of(dy, dz)], w[...], preferred_element_type=jnp.float32), ((0, rows, slice_rows(s)),))
        for copy in halos(s, None) + out_copies(s):
            copy.start()
        return carry

    for copy in w_copies:
        copy.wait()
    lax.fori_loop(0, len(order), step, 0)

    def last_step(n, carry):
        k = jnp.int32(0)
        for at, one in enumerate((0, 3, 1, 2)):
            k = jnp.where(n == at, one, k)
            pl.when(n == at)(last_chunk(one))
        taken, spans = [], []
        for dy, _ in last:
            s = slice_of(dy, 1, flip)
            spans.append((len(taken) * part, part, pl.ds(pl.multiple_of(s * rows + k * part, part), part)))
            taken.append(xbuf[slot_of(dy, 1), pl.ds(pl.multiple_of(k * part, part), part), :])
        put(jnp.dot(jnp.concatenate(taken, axis=0), w[...], preferred_element_type=jnp.float32), spans)
        for dy, _ in last:
            s = slice_of(dy, 1, flip)
            for copy in halos(s, k):
                copy.start()
        return carry

    lax.fori_loop(0, CHUNKS, last_step, 0)
    for dy, _ in last:
        for copy in out_copies(slice_of(dy, 1, flip)):
            copy.start()
    w_half(2)
    w_five(0)
    w_five(1)

    @pl.when(flip == 1)
    def _():
        for k in range(CHUNKS):
            swap(k, y * 2 + 1 - zl).wait_send()

    for number, ks in ((YP_OWN, range(4)), (YM_OWN, range(4)), (Z_OWN, range(4)), (YP_FWD, (0, 1)), (YM_FWD, (2, 3)),
                       (YP_PEER, range(4)), (YM_PEER, range(4)), (Z_OPP, range(4))):
        for k in ks:
            message(number, k, pos, zp).wait_send()

    for dy, dz in [one[:2] for one in order]:
        for copy in out_copies(slice_of(dy, dz, flip)):
            copy.wait()
        for copy in halos(slice_of(dy, dz, flip), None):
            copy.wait_send()
        for copy in halos(slice_of(dy, dz, 1 - flip), None):
            copy.wait_recv()
    for dy, _ in last:
        for copy in out_copies(slice_of(dy, 1, flip)):
            copy.wait()
        for k in range(CHUNKS):
            for copy in halos(slice_of(dy, 1, flip), k):
                copy.wait_send()
            for copy in halos(slice_of(dy, 1, 1 - flip), k):
                copy.wait_recv()
    w_first(W_YP, 3, yp).wait_send()
    w_first(W_YM, 1, ym).wait_send()
    w_forward(W_YP_FWD, 2, low, yp).wait_send()
    w_forward(W_YM_FWD, 2, high, ym).wait_send()
    w_diagonal_all(zl, 0).wait_send()
    w_diagonal_all(zl, 2).wait_send()
    w_sibling_all(1 - c, 0).wait()
    w_sibling_all(1 - c, 2).wait()
    for dy in (1, 2, 3):
        w_diagonal(dy, zl).wait_send()
        for z in (0, 1):
            w_along(W_XP, dy, z, x, xp).wait_send()
            w_along(W_XM, dy, z, x, xm).wait_send()
            for which in (0, 1, 3):
                w_sibling(which, dy, z, 1 - c).wait()


def gather_project(tokens, shift, mod_scale, w, q_gain, k_gain, w_out):
    rows, depth = tokens.shape
    heads = w.shape[0]
    width = heads * HD
    hbm = pl.BlockSpec(memory_space=pl.ANY)
    dma = pltpu.SemaphoreType.DMA
    return pl.pallas_call(
        functools.partial(gather_kernel, heads),
        name="gather_project",
        out_shape=(
            jax.ShapeDtypeStruct((SLICES * rows, width), jnp.bfloat16),
            jax.ShapeDtypeStruct((3, SLICES * rows, 2 * width), jnp.bfloat16),
            jax.ShapeDtypeStruct((4, 2) + w_out.shape, jnp.bfloat16),
        ),
        in_specs=[pl.BlockSpec(memory_space=pltpu.HBM)] * 7,
        out_specs=(hbm, hbm, hbm),
        scratch_shapes=[
            pltpu.VMEM((rows, depth), jnp.bfloat16),
            pltpu.VMEM((1, depth), jnp.float32),
            pltpu.VMEM((1, depth), jnp.float32),
            pltpu.VMEM((1, HD), jnp.float32),
            pltpu.VMEM((1, HD), jnp.float32),
            dma((5,)),
            pltpu.VMEM((SLICES, rows, depth), jnp.bfloat16),
            pltpu.VMEM((rows, depth), jnp.bfloat16),
            pltpu.VMEM((depth, 3 * width), jnp.bfloat16),
            pltpu.VMEM((SLICES * rows, width), jnp.bfloat16),
            pltpu.VMEM((SLICES * rows, 2 * width), jnp.bfloat16),
            dma((MESSAGES,)), dma((MESSAGES,)), dma((2 * CHUNKS * SLICES,)), dma((2 * CHUNKS * SLICES,)), dma((2 * SLICES,)), dma((heads,)),
            dma((W_MESSAGES,)), dma((W_MESSAGES,)),
        ],
        compiler_params=pltpu.CompilerParams(
            vmem_limit_bytes=36 * MIB, collective_id=0, has_side_effects=True
        ),
    )(*(pltpu.with_memory_space_constraint(one, pltpu.HBM) for one in
        (tokens, mod_scale[None], shift[None], w, q_gain[None], k_gain[None], w_out)))


def attention_kernel(heads, pat_ref, cnt_ref, t_ref, q_ref, kv_ref, out_ref, ones, acc, todo):
    t = t_ref[0]
    width = heads * HD
    slots = (2 - t % 2, 0, 1 + t % 2)
    def list_tile(i, carry):
        count = jnp.int32(0)
        for o in range(3):
            inside = (t + o - 1 >= 0) & (t + o - 1 < NT)
            for j in range(GS):
                todo[i * 14 + 1 + count] = (o * 3 + slots[o]) * GS + j
                live = inside & (pat_ref[o, i, j] > 0)
                count = count + live.astype(jnp.int32)
        todo[i * 14 + 1 + count] = NONE
        todo[i * 14] = (count + 1) // 2
        return carry

    lax.fori_loop(0, GS, list_tile, 0)
    ones[3] = jnp.zeros_like(ones[3])
    place = lax.broadcasted_iota(jnp.int32, (TILE, HD), 0)
    for o in range(3):
        ones[o] = jnp.where(place < cnt_ref[jnp.clip(t + o - 1, 0, NT - 1)], 1.0, 0.0).astype(jnp.bfloat16)
    def keys_of(one, cols):
        return kv_ref[one // GS % 3, one % GS, :, cols]

    def values_of(one, h):
        return kv_ref[one // GS % 3, one % GS, :, width + h * HD : width + (h + 1) * HD] * ones[one // (3 * GS)]

    def tile(i, carry):
        mine = pl.ds(pl.multiple_of(i * TILE, TILE), TILE)
        acc[...] = jnp.zeros_like(acc)

        def attend(which):
            probs = []
            for h in range(heads):
                cols = slice(h * HD, (h + 1) * HD)
                score = lax.dot_general(
                    q_ref[mine, cols],
                    jnp.concatenate([keys_of(one, cols) for one in which], axis=0),
                    (((1,), (1,)), ((), ())),
                    preferred_element_type=jnp.float32,
                )
                probs.append(jnp.exp2(score).astype(jnp.bfloat16))
            valid = jnp.concatenate([ones[one // (3 * GS)] for one in which], axis=0)
            for h in range(heads):
                values = jnp.concatenate([values_of(one, h) for one in which], axis=0)
                acc[h] += jnp.dot(
                    probs[h], jnp.concatenate([values, valid], axis=1), preferred_element_type=jnp.float32
                )

        pairs = todo[i * 14]
        first = i * 14 + 1

        def four(n, carry):
            attend([todo[first + 4 * n + m] for m in range(4)])
            return carry

        lax.fori_loop(0, pairs // 2, four, 0)

        @pl.when(pairs % 2 == 1)
        def _():
            attend([todo[first + 2 * (pairs - 1) + m] for m in range(2)])

        for h in range(heads):
            out_ref[mine, h * HD : (h + 1) * HD] = (acc[h, :, :HD] / acc[h, :, HD:]).astype(jnp.bfloat16)
        return carry

    lax.fori_loop(0, GS, tile, 0)


def attention(q, kv, pattern, counts, t):
    rows, width = q.shape
    heads = width // HD
    smem = pl.BlockSpec(memory_space=pltpu.SMEM)
    vmem = pl.BlockSpec(memory_space=pltpu.VMEM)
    return pl.pallas_call(
        functools.partial(attention_kernel, heads),
        name="attention",
        out_shape=jax.ShapeDtypeStruct((rows, width), jnp.bfloat16),
        in_specs=[smem, smem, smem, vmem, vmem],
        out_specs=vmem,
        scratch_shapes=[
            pltpu.VMEM((GS, TILE, HD), jnp.bfloat16),
            pltpu.VMEM((heads, TILE, 2 * HD), jnp.float32),
            pltpu.SMEM((GS * 14,), jnp.int32),
        ],
        compiler_params=pltpu.CompilerParams(vmem_limit_bytes=32 * MIB),
    )(pattern, counts, t.reshape(1), q, kv.reshape(3, GS, TILE, 2 * width))


def finish_kernel(attn, wo_ref, wall, out_ref, rows_in, wv, a_send, a_recv, x_send, x_recv, s_send, s_recv, w_sem, own_sem):
    x, zh, y, zl, c = place()
    nx = lax.axis_size("frame") // 2
    rows, depth = out_ref.shape
    width = attn.shape[1]
    pos = y * 2 + zl
    straight = zh == c
    sibling = {"rep": 1 - c}
    xp, xm = {"frame": (x + 1) % nx * 2 + zh}, {"frame": (x + nx - 1) % nx * 2 + zh}

    def owner(s):
        return {"frame": x * 2 + c, "head": s, "rep": zh}

    def others(s):
        return jnp.logical_or(s != pos, jnp.logical_not(straight))

    barrier = pltpu.get_barrier_semaphore()
    for device in (sibling, xp, xm):
        pl.semaphore_signal(barrier, inc=1, device_id=device, device_id_type=MESH)

    def greet(s, carry):
        @pl.when(others(s))
        def _():
            pl.semaphore_signal(barrier, inc=1, device_id=owner(s), device_id_type=MESH)

        return carry

    lax.fori_loop(0, SLICES, greet, 0)

    def load(dy, k):
        return pltpu.make_async_copy(wall.at[dy, :, :, k], wv.at[dy, :, :, k], w_sem.at[4 * dy + k])

    def loads(act):
        act(pltpu.make_async_copy(wo_ref, wv.at[0, zl], w_sem.at[0]))
        act(pltpu.make_async_copy(wall.at[0, 1 - zl], wv.at[0, 1 - zl], w_sem.at[1]))

    loads(lambda copy: copy.start())
    for dy in (1, 3, 2):
        for which in (0, 1, 3):
            load(dy, (x + which) % 4).start()
    pl.semaphore_wait(barrier, jnp.where(straight, SLICES + 2, SLICES + 3))

    def landing(source):
        cols = pl.ds(pl.multiple_of(source % 2 * width, width), width)
        return rows_in.at[source // 2, :, cols]

    def hand_out(s, source):
        return pltpu.make_async_remote_copy(
            src_ref=attn.at[pl.ds(pl.multiple_of(s * rows, rows), rows)], dst_ref=landing(source),
            send_sem=a_send.at[s], recv_sem=a_recv.at[source], device_id=owner(s), device_id_type=MESH,
        )

    def keep():
        return pltpu.make_async_copy(
            attn.at[pl.ds(pl.multiple_of(pos * rows, rows), rows)], landing(pos), own_sem
        )

    def far(number, dy, z, k, device):
        return pltpu.make_async_remote_copy(
            src_ref=wall.at[dy, z, c, k], dst_ref=wv.at[dy, z, c, k], send_sem=x_send.at[number + dy],
            recv_sem=x_recv.at[number + dy], device_id=device, device_id_type=MESH,
        )

    def scatter(n, carry):
        ahead = jnp.where(n < 4, n // 2, 5 - n // 2)
        s = (y + ahead) % 4 * 2 + (zl + n) % 2

        @pl.when(others(s))
        def _():
            hand_out(s, pos).start()

        return carry

    for dy in (1, 3, 2):
        far(0, dy, 0, (x + 3) % 4, xp).start()
        far(4, dy, 1, (x + 1) % 4, xm).start()
    lax.fori_loop(0, SLICES, scatter, 0)

    @pl.when(straight)
    def _():
        keep().start()

    def share(number, dy, z, core):
        there = wv.at[dy, z, core, (x + 2) % 4]
        return pltpu.make_async_remote_copy(
            src_ref=there, dst_ref=there, send_sem=s_send.at[number + dy], recv_sem=s_recv.at[number + dy],
            device_id=sibling, device_id_type=MESH,
        )

    cols = depth

    def arrived(dy, z):
        source = (y + dy) % 4 * 2 + (zl + z) % 2
        kept = jnp.logical_and(straight, source == pos)

        @pl.when(kept)
        def _():
            keep().wait()

        @pl.when(jnp.logical_not(kept))
        def _():
            hand_out(0, source).wait_recv()

    def add(dy, first):
        arrived(dy, 0)
        arrived(dy, 1)

        def column(n, carry):
            here = pl.ds(pl.multiple_of(n * cols, cols), cols)
            weight = wv[dy, :, :, :, :, here].reshape(2 * width, cols)
            term = jnp.dot(rows_in[(y + dy) % 4], weight, preferred_element_type=jnp.float32)
            out_ref[:, here] = term if first else out_ref[:, here] + term
            return carry

        lax.fori_loop(0, depth // cols, column, 0)

    loads(lambda copy: copy.wait())
    add(0, True)
    for dy in (1, 3, 2):
        far(0, dy, 0, (x + 2) % 4, xp).wait_recv()
        share(0, dy, 0, c).start()
        far(4, dy, 1, (x + 2) % 4, xm).wait_recv()
        share(4, dy, 1, c).start()
        for which in (0, 1, 3):
            load(dy, (x + which) % 4).wait()
        share(0, dy, 0, 1 - c).wait_recv()
        share(4, dy, 1, 1 - c).wait_recv()
        add(dy, False)

    def sent(s, carry):
        @pl.when(others(s))
        def _():
            hand_out(s, pos).wait_send()

        return carry

    lax.fori_loop(0, SLICES, sent, 0)
    for dy in (1, 3, 2):
        far(0, dy, 0, (x + 3) % 4, xp).wait_send()
        far(4, dy, 1, (x + 1) % 4, xm).wait_send()
        share(0, dy, 0, c).wait_send()
        share(4, dy, 1, c).wait_send()


def finish(attn, rows, w_out, wall):
    width = attn.shape[1]
    depth = wall.shape[-1]
    vmem = pl.BlockSpec(memory_space=pltpu.VMEM)
    hbm = pl.BlockSpec(memory_space=pl.ANY)
    dma = pltpu.SemaphoreType.DMA
    return pl.pallas_call(
        finish_kernel,
        name="finish",
        out_shape=jax.ShapeDtypeStruct((rows, depth), jnp.float32),
        in_specs=[hbm, pl.BlockSpec(memory_space=pltpu.HBM), hbm],
        out_specs=vmem,
        scratch_shapes=[
            pltpu.VMEM((SLICES // 2, rows, 2 * width), jnp.bfloat16),
            pltpu.VMEM(wall.shape, jnp.bfloat16),
            dma((SLICES,)), dma((SLICES,)), dma((8,)), dma((8,)), dma((8,)), dma((8,)), dma((16,)), dma(()),
        ],
        compiler_params=pltpu.CompilerParams(
            vmem_limit_bytes=32 * MIB, collective_id=1, has_side_effects=True
        ),
    )(attn, w_out, wall)


def per_device(tokens, shift, mod_scale, gate, w_qkv, q_gain, k_gain, w_out, pattern, counts):
    w_parts = w_out.reshape(2, 4, w_out.shape[0] // 8, w_out.shape[1])
    q, kv, wall = gather_project(tokens, shift, mod_scale, jnp.transpose(w_qkv, (1, 0, 2)), q_gain, k_gain, w_parts)
    block = lax.axis_index("frame") // 2 * 2 + lax.axis_index("rep")
    attn = attention(q, kv, pattern, counts, block)
    result = finish(attn, tokens.shape[0], w_parts, wall)
    return (tokens.astype(jnp.float32) + gate * result).astype(jnp.bfloat16)


def solution(mesh):
    placed = (
        P(("rep", "frame", "head"), None),
        P(),
        P(),
        P(),
        P(None, "head", None),
        P(),
        P(),
        P("head", None),
        P(),
        P(),
    )
    return jax.shard_map(
        per_device,
        mesh=mesh,
        in_specs=placed,
        out_specs=P(("rep", "frame", "head"), None),
        check_vma=False,
    )
```
